32 devices in a mesh: dp: 4 (over z), row: 4 (over y, core), col: 2 (over x).
Axes of the slice: x: 2, y: 2, z: 4, core: 2. Of those that a mesh axis runs over, the one named last changes fastest.
Arguments:
- tokens: bfloat16 [20480, 1024], P(('dp', 'row'), 'col'), may hold values from -6 to 6
- segments: int32 [20480], P('dp'), may hold values from 0 to 159, never falling along the last dimension, each value on 1 to 512 neighbouring positions
- qkv_weight: bfloat16 [1024, 3072], P('col', 'row'), may hold values from -0.1875 to 0.1875
- qv_bias: float32 [16, 128], P(('row', 'col')), may hold values from -6 to 6
- out_weight: bfloat16 [1024, 1024], P('row', 'col'), may hold values from -1.5 to 1.5
- out_bias: float32 [1024], P('col'), may hold values from -6 to 6
- ln1_gain: float32 [1024], P('col'), may hold values from 0.25 to 1.75
- ln1_bias: float32 [1024], P('col'), may hold values from -6 to 6
- ff_in_weight: bfloat16 [1024, 4096], P('col', 'row'), may hold values from -0.1875 to 0.1875
- ff_in_bias: float32 [4096], P(('row', 'col')), may hold values from -6 to 6
- ff_out_weight: bfloat16 [4096, 1024], P('row', 'col'), may hold values from -0.09375 to 0.09375
- ff_out_bias: float32 [1024], P('col'), may hold values from -6 to 6
- ln2_gain: float32 [1024], P('col'), may hold values from 0.25 to 1.75
- ln2_bias: float32 [1024], P('col'), may hold values from -6 to 6
- out_grad: bfloat16 [20480, 1024], P(('dp', 'row'), 'col'), may hold values from -6 to 6
Outputs:
- layer_out: float32 [20480, 1024], P(('dp', 'row'), 'col')
- input_grad: float32 [20480, 1024], P(('dp', 'row'), 'col')
- qkv_weight_grad: float32 [1024, 3072], P('col', 'row')
- qv_bias_grad: float32 [16, 128], P(('row', 'col'))
- out_weight_grad: float32 [1024, 1024], P('row', 'col')
- out_bias_grad: float32 [1024], P('col')
- ln1_gain_grad: float32 [1024], P('col')
- ln1_bias_grad: float32 [1024], P('col')
- ff_in_weight_grad: float32 [1024, 4096], P('col', 'row')
- ff_in_bias_grad: float32 [4096], P(('row', 'col'))
- ff_out_weight_grad: float32 [4096, 1024], P('row', 'col')
- ff_out_bias_grad: float32 [1024], P('col')
- ln2_gain_grad: float32 [1024], P('col')
- ln2_bias_grad: float32 [1024], P('col')
The draws below stay inside these ranges and needn't reach their ends.
Inputs may be any that keep to these rules, and one draw needn't show every extreme that they name: `segments`: segment numbers never fall along the tokens; one segment holds at most 512 tokens.
All inputs are finite; a program needn't handle non-finite values.
Results may differ from the reference program's by a relative error of at most 0.02.
Values may be sent and summed in bfloat16 or wider, within the bound.
No kernel may reach another device: no remote copies, remote signals or barrier semaphores. Data moves between devices by JAX's collectives and lax.ppermute only.
A program may use at most 192 MiB of HBM per device.

```python
import math
import jax
import jax.numpy as jnp
import numpy as np
from jax import lax

D = 1024
H = 16
FF = 4096
HD = 64
SEQ = 512
TOK_GRP = 5120
TOKENS = 20480
N_DP = 4


def steps_of(own_key, extent, shards, low, top_value):
    loudness, own = 1.0, jax.random.fold_in(own_key, 6)
    for dim, shards_of in shards:
        heights = jnp.exp(jax.random.uniform(jax.random.fold_in(own, dim), (shards_of,), jnp.float32, low / len(shards), top_value / len(shards)))
        loudness = loudness * jnp.repeat(heights, extent[dim] // shards_of).reshape([-1 if axis == dim else 1 for axis in range(len(extent))])
    return loudness


def split_up(amount, total, most, lean):
    portions = [(1 << 20) // math.isqrt(rank ** lean) + 1 for rank in range(2, amount + 1)]
    spare, holding = total - most - (amount - 1), [1] * (amount - 1)
    while spare > 0:
        candidates = [i for i in range(amount - 1) if holding[i] < most]
        mass, remaining = sum([portions[i] for i in candidates]), spare
        for i in candidates:
            addition = min(most - holding[i], max(1, remaining * portions[i] // mass), spare)
            holding[i] = holding[i] + addition
            spare = spare - addition
    return np.array([most] + holding)


def uneven(stream_key, number_of, total, bound, slope):
    if number_of == 2:
        one = jax.random.randint(stream_key, (), max(1, total - bound), min(bound, total - 1) + 1)
        return jnp.stack([one, total - one])
    sizes = jnp.asarray(split_up(number_of, total, bound, slope), jnp.int32)
    couples = (number_of - 1) // 2
    donor, receiver = sizes[1:1 + 2 * couples:2], sizes[2:2 + 2 * couples:2]
    slack = jnp.minimum(donor - 1, bound - receiver)
    shifted = jax.random.randint(jax.random.fold_in(stream_key, 1), (couples,), 0, 1 << 20) % (slack + 1)
    sizes = sizes.at[1:1 + 2 * couples:2].set(donor - shifted).at[2:2 + 2 * couples:2].set(receiver + shifted)
    return sizes[jax.random.permutation(jax.random.fold_in(stream_key, 2), number_of)]


def scatter_about(rng, dims, scale, most, shards=(), kind=jnp.bfloat16):
    values = scale * jax.random.normal(rng, dims, jnp.float32)
    if shards:
        values = values * steps_of(rng, dims, shards, -0.22, 0.18)
    return jnp.clip(values, -most, most).astype(kind)


def setup_inputs(seed: int = 0) -> dict:
    streams_of = jax.random.split(jax.random.key(seed), 16)
    return {
        "tokens": scatter_about(streams_of[0], (TOKENS, D), 1.0, 6.0, ((0, 16), (1, 2))),
        "segments": jnp.searchsorted(jnp.cumsum(uneven(streams_of[1], TOKENS * 4 // SEQ, TOKENS, SEQ, 1)), jnp.arange(TOKENS), side="right").astype(jnp.int32),
        "qkv_weight": scatter_about(streams_of[2], (D, 3 * D), D ** -0.5, 0.1875, ((0, 2), (1, 4))),
        "qv_bias": scatter_about(streams_of[3], (H, 2 * HD), 0.5, 6.0, ((0, 8),), jnp.float32),
        "out_weight": scatter_about(streams_of[4], (D, D), (D // 64) ** -0.5, 1.5, ((0, 4), (1, 2))),
        "out_bias": scatter_about(streams_of[5], (D,), 0.5, 6.0, ((0, 2),), jnp.float32),
        "ln1_gain": jnp.clip(1.0 + 0.15 * jax.random.normal(streams_of[6], (D,), jnp.float32), 0.25, 1.75),
        "ln1_bias": scatter_about(streams_of[7], (D,), 0.5, 6.0, ((0, 2),), jnp.float32),
        "ff_in_weight": scatter_about(streams_of[8], (D, FF), D ** -0.5, 0.1875, ((0, 2), (1, 4))),
        "ff_in_bias": scatter_about(streams_of[9], (FF,), 0.5, 6.0, ((0, 8),), jnp.float32),
        "ff_out_weight": scatter_about(streams_of[10], (FF, D), FF ** -0.5, 0.09375, ((0, 4), (1, 2))),
        "ff_out_bias": scatter_about(streams_of[11], (D,), 0.5, 6.0, ((0, 2),), jnp.float32),
        "ln2_gain": jnp.clip(1.0 + 0.15 * jax.random.normal(streams_of[12], (D,), jnp.float32), 0.25, 1.75),
        "ln2_bias": scatter_about(streams_of[13], (D,), 0.5, 6.0, ((0, 2),), jnp.float32),
        "out_grad": scatter_about(streams_of[14], (TOKENS, D), 1.0, 6.0, ((0, 16), (1, 2))),
    }


EPSILON = 1e-06
NEGATIVE = -1e+30
PRECISE = lax.Precision.HIGHEST

@jax.custom_vjp
def low(v):
    return lax.optimization_barrier(v.astype(jnp.bfloat16)).astype(jnp.float32)

@jax.custom_vjp
def low_back(v):
    return v

def low_keep(v):
    return (low(v), None)

def low_pass(kept, grad):
    return (grad,)

def back_keep(v):
    return (v, None)

def back_low(kept, grad):
    return (low(grad),)
low.defvjp(low_keep, low_pass)
low_back.defvjp(back_keep, back_low)

def product(left, right):
    return jnp.dot(left, right, precision=PRECISE, preferred_element_type=jnp.float32)

def layer_norm(value, gain, bias):
    center = lax.optimization_barrier(jnp.mean(value, axis=-1, keepdims=True))
    spread = lax.optimization_barrier(jnp.mean(value * value, axis=-1, keepdims=True)) - center * center
    return (value - center) * lax.rsqrt(spread + EPSILON) * gain + bias

def attend(block):
    queries, keys, values, labels = block
    scores = jnp.einsum('qhd,khd->hqk', queries, keys, precision=PRECISE) / math.sqrt(HD)
    scores = low_back(scores)
    same_doc = labels[:, None] == labels[None, :]
    scores = jnp.where(same_doc[None], scores, NEGATIVE)
    highest = lax.optimization_barrier(jnp.max(scores, axis=-1, keepdims=True))
    weights = jnp.exp(scores - highest)
    weights = low(weights / lax.optimization_barrier(jnp.sum(weights, axis=-1, keepdims=True)))
    return jnp.einsum('hqk,khd->qhd', weights, values, precision=PRECISE)

def forward(tokens, labels, qkv_weight, qv_bias, out_weight, out_bias, ln1_gain, ln1_bias, ff_in_weight, ff_in_bias, ff_out_weight, ff_out_bias, ln2_gain, ln2_bias):
    count = tokens.shape[0]
    hollow = jnp.zeros((H, 1, HD), jnp.float32)
    full_bias = jnp.concatenate([qv_bias[:, None, :HD], hollow, qv_bias[:, None, HD:]], axis=1).reshape(3 * D)
    mixed = low_back(low(product(tokens, qkv_weight) + full_bias))
    mixed = mixed.reshape(count // SEQ, SEQ, H, 3, HD)
    attended = lax.map(jax.checkpoint(attend), (mixed[:, :, :, 0], mixed[:, :, :, 1], mixed[:, :, :, 2], labels.reshape(count // SEQ, SEQ)))
    attended = low_back(low(attended.reshape(count, D)))
    branch_one = low_back(product(attended, out_weight) + out_bias)
    middle = layer_norm(tokens + branch_one, ln1_gain, ln1_bias)
    hidden = low_back(product(low(middle), ff_in_weight) + ff_in_bias)
    active = low(jax.nn.gelu(hidden, approximate=False))
    branch_two = low_back(product(active, ff_out_weight) + ff_out_bias)
    return layer_norm(middle + branch_two, ln2_gain, ln2_bias)

def reference(tokens, segments, qkv_weight, qv_bias, out_weight, out_bias, ln1_gain, ln1_bias, ff_in_weight, ff_in_bias, ff_out_weight, ff_out_bias, ln2_gain, ln2_bias, out_grad):
    params = (qkv_weight.astype(jnp.float32), qv_bias, out_weight.astype(jnp.float32), out_bias, ln1_gain, ln1_bias, ff_in_weight.astype(jnp.float32), ff_in_bias, ff_out_weight.astype(jnp.float32), ff_out_bias, ln2_gain, ln2_bias)
    inputs = tokens.astype(jnp.float32).reshape(N_DP, TOK_GRP, D)
    labels = segments.reshape(N_DP, TOK_GRP)
    cotangent = out_grad.astype(jnp.float32).reshape(N_DP, TOK_GRP, D)

    def visit(totals, block):
        rows, marks, incoming = block
        result, pullback = jax.vjp(lambda first, rest: forward(first, marks, *rest), rows, params)
        row_grad, param_grads = pullback(incoming)
        return (jax.tree.map(jnp.add, totals, param_grads), (result, row_grad))
    start = jax.tree.map(jnp.zeros_like, params)
    totals, (outputs, row_grads) = lax.scan(visit, start, (inputs, labels, cotangent))
    return (outputs.reshape(TOKENS, D), row_grads.reshape(TOKENS, D), totals[0], totals[1], totals[2], totals[3], totals[4], totals[5], totals[6], totals[7], totals[8], totals[9], totals[10], totals[11])
```

```python
import math

import jax
import jax.numpy as jnp
from jax import lax
from jax.experimental import pallas as pl
from jax.experimental.pallas import tpu as pltpu
from jax.sharding import PartitionSpec as P

D = 1024
HD = 64
SEQ = 512
QUARTER = SEQ // 4
GRID = ("row", "col")

EPSILON = 1e-06
NEGATIVE = -1e30
F32 = jnp.float32
BF16 = jnp.bfloat16
NN = (((1,), (0,)), ((), ()))
NT = (((1,), (1,)), ((), ()))
TN = (((0,), (0,)), ((), ()))
MIB = 1 << 20


def mm(left, right, contract):
    return lax.dot_general(left, right, contract, preferred_element_type=F32)


def attend_kernel(qkv_ref, column_ref, line_ref, heads_ref, probs_ref, mask):
    @pl.when(pl.program_id(0) == 0)
    def _():
        mask[...] = jnp.where(column_ref[...] == line_ref[...], 0.0, NEGATIVE)

    mixed = []
    for head in range(2):
        base = head * 3 * HD
        query = qkv_ref[:, base : base + HD] * jnp.asarray(1 / math.sqrt(HD), BF16)
        key = qkv_ref[:, base + HD : base + 2 * HD]
        value = qkv_ref[:, base + 2 * HD : base + 3 * HD]
        scores = mm(key, query, NT) + mask[...]
        powers = jnp.exp(scores - jnp.max(scores, 0, keepdims=True))
        total = jnp.sum(powers, 0, keepdims=True)
        probs = (powers * (1.0 / total)).astype(BF16)
        probs_ref[head] = probs
        mixed.append(mm(value, probs, TN))
    heads_ref[...] = jnp.concatenate(mixed, 0).T.astype(BF16)


def attend(qkv, labels):
    pairs = qkv.shape[1] // (6 * HD)
    return pl.pallas_call(
        attend_kernel,
        grid=(pairs,),
        in_specs=[
            pl.BlockSpec((SEQ, 6 * HD), lambda i: (0, i)),
            pl.BlockSpec((SEQ, 1), lambda i: (0, 0)),
            pl.BlockSpec((1, SEQ), lambda i: (0, 0)),
        ],
        out_specs=[
            pl.BlockSpec((SEQ, 2 * HD), lambda i: (0, i)),
            pl.BlockSpec((2, SEQ, SEQ), lambda i: (i, 0, 0)),
        ],
        out_shape=[
            jax.ShapeDtypeStruct((SEQ, pairs * 2 * HD), BF16),
            jax.ShapeDtypeStruct((pairs * 2, SEQ, SEQ), BF16),
        ],
        scratch_shapes=[pltpu.VMEM((SEQ, SEQ), F32)],
        compiler_params=pltpu.CompilerParams(vmem_limit_bytes=32 * MIB),
        cost_estimate=pl.CostEstimate(
            flops=pairs * 2 * 4 * SEQ * SEQ * 256, bytes_accessed=pairs * 2 * SEQ * SEQ * 2, transcendentals=pairs * 2 * SEQ * SEQ
        ),
        name="attend",
    )(qkv, labels[:, None], labels[None, :])


def attend_back_kernel(qkv_ref, probs_ref, grad_ref, out_ref):
    for head in range(2):
        base = head * 3 * HD
        scale = jnp.asarray(1 / math.sqrt(HD), BF16)
        query = qkv_ref[:, base : base + HD] * scale
        key = qkv_ref[:, base + HD : base + 2 * HD] * scale
        value = qkv_ref[:, base + 2 * HD : base + 3 * HD]
        grad = grad_ref[:, head * HD : (head + 1) * HD]
        probs = probs_ref[head]
        d_value = mm(probs, grad, NN)
        d_probs = mm(value, grad, NT)
        wide = probs.astype(F32)
        delta = jnp.sum(wide * d_probs, 0, keepdims=True)
        d_scores = (wide * (d_probs - delta)).astype(BF16)
        d_key = mm(d_scores, query, NN)
        d_query = mm(key, d_scores, TN).T
        out_ref[:, base : base + HD] = d_query.astype(BF16)
        out_ref[:, base + HD : base + 2 * HD] = d_key.astype(BF16)
        out_ref[:, base + 2 * HD : base + 3 * HD] = d_value.astype(BF16)


def attend_back(qkv, probs, grad):
    pairs = qkv.shape[1] // (6 * HD)
    return pl.pallas_call(
        attend_back_kernel,
        grid=(pairs,),
        in_specs=[
            pl.BlockSpec((SEQ, 6 * HD), lambda i: (0, i)),
            pl.BlockSpec((2, SEQ, SEQ), lambda i: (i, 0, 0)),
            pl.BlockSpec((SEQ, 2 * HD), lambda i: (0, i)),
        ],
        out_specs=pl.BlockSpec((SEQ, 6 * HD), lambda i: (0, i)),
        out_shape=jax.ShapeDtypeStruct(qkv.shape, BF16),
        compiler_params=pltpu.CompilerParams(vmem_limit_bytes=32 * MIB),
        cost_estimate=pl.CostEstimate(
            flops=pairs * 2 * 10 * SEQ * SEQ * 256, bytes_accessed=pairs * 2 * SEQ * SEQ * 2, transcendentals=0
        ),
        name="attend_back",
    )(qkv, probs, grad)


def own_rows(value, odd, col):
    rolled = jnp.where(odd, jnp.roll(value, -2 * QUARTER, 0), value)
    first = jnp.concatenate([rolled[:SEQ], rolled[2 * SEQ : 2 * SEQ + QUARTER]], 0)
    second = jnp.concatenate([rolled[SEQ : 2 * SEQ], rolled[2 * SEQ + QUARTER :]], 0)
    mine = jnp.where(col == 0, first, second)
    other = lax.ppermute(jnp.where(col == 0, second, first), "col", [(0, 1), (1, 0)])
    return jnp.concatenate([jnp.where(col == 0, mine, other), jnp.where(col == 0, other, mine)], 1)


def give_back(value, odd, col):
    half = D // 2
    mine = jnp.where(col == 0, value[:, :half], value[:, half:])
    leaving = jnp.where(col == 0, value[:, half:], value[:, :half])
    other = lax.ppermute(leaving.astype(BF16), "col", [(0, 1), (1, 0)]).astype(F32)
    first = jnp.where(col == 0, mine, other)
    second = jnp.where(col == 0, other, mine)
    rolled = jnp.concatenate([first[:SEQ], second[:SEQ], first[SEQ:], second[SEQ:]], 0)
    return jnp.where(odd, jnp.roll(rolled, 2 * QUARTER, 0), rolled)


def swap(offset):
    return [(i, i ^ offset) for i in range(8)]


def spread_heads(value, member):
    width = value.shape[1] // 4
    pieces = []
    for offset in range(4):
        piece = lax.dynamic_slice_in_dim(value, (member ^ offset) * width, width, 1)
        pieces.append(piece if offset == 0 else lax.ppermute(piece, GRID, swap(offset)))
    return jnp.concatenate(pieces, 0)


def collect_heads(value, member):
    width = value.shape[1]
    whole = jnp.zeros((QUARTER, 4 * width), value.dtype)
    for offset in range(4):
        piece = value[offset * QUARTER : (offset + 1) * QUARTER]
        if offset:
            piece = lax.ppermute(piece, GRID, swap(offset))
        whole = lax.dynamic_update_slice_in_dim(whole, piece, (member ^ offset) * width, 1)
    return whole


def gather_weight(shard):
    return lax.all_gather(shard, GRID, axis=0, tiled=False)


def whole_up(stack):
    _, depth, width = stack.shape
    return stack.reshape(4, 2, depth, width).transpose(1, 2, 0, 3).reshape(2 * depth, 4 * width)


def whole_down(stack):
    _, depth, width = stack.shape
    return stack.reshape(4, 2, depth, width).transpose(0, 2, 1, 3).reshape(4 * depth, 2 * width)


def reduce_up(grad):
    depth, width = grad.shape
    stack = grad.astype(BF16).reshape(2, depth // 2, 4, width // 4).transpose(2, 0, 1, 3)
    return reduce_stack(stack.reshape(8, depth // 2, width // 4))


def reduce_down(grad):
    depth, width = grad.shape
    stack = grad.astype(BF16).reshape(4, depth // 4, 2, width // 2).transpose(0, 2, 1, 3)
    return reduce_stack(stack.reshape(8, depth // 4, width // 2))


def reduce_stack(stack):
    share = lax.psum_scatter(stack, GRID, scatter_dimension=0, tiled=False)
    return lax.psum(share, "dp").astype(F32)


def norm_forward(value, gain, bias):
    center = jnp.sum(value, 1, keepdims=True) / D
    squares = jnp.sum(value * value, 1, keepdims=True) / D
    inverse = lax.rsqrt(squares - center * center + EPSILON)
    unit = (value - center) * inverse
    return (unit * gain + bias, unit, inverse)


def norm_backward(grad, unit, inverse, gain):
    scaled = grad * gain
    total = jnp.sum(scaled, 1, keepdims=True)
    paired = jnp.sum(scaled * unit, 1, keepdims=True)
    back = inverse * (scaled - total / D - unit * (paired / D))
    return (back, jnp.sum(grad * unit, 0), jnp.sum(grad, 0))


def gelu_exact(value):
    return jax.nn.gelu(value, approximate=False)


def local(
    tokens,
    segments,
    qkv_weight,
    qv_bias,
    out_weight,
    out_bias,
    ln1_gain,
    ln1_bias,
    ff_in_weight,
    ff_in_bias,
    ff_out_weight,
    ff_out_bias,
    ln2_gain,
    ln2_bias,
    out_grad,
):
    row, col = lax.axis_index("row"), lax.axis_index("col")
    odd = row % 2 == 1
    member = (row % 2) * 2 + col

    qkv_w = whole_up(gather_weight(qkv_weight))
    out_w = whole_down(gather_weight(out_weight))
    ff_in_w = whole_up(gather_weight(ff_in_weight))
    ff_out_w = whole_down(gather_weight(ff_out_weight))

    packed = jnp.concatenate(
        [out_bias, ln1_gain, ln1_bias, ff_out_bias, ln2_gain, ln2_bias, ff_in_bias, qv_bias.reshape(-1)]
    )
    packed = lax.all_gather(packed, GRID, axis=0, tiled=False)
    vectors = packed[:2, : 6 * 512].reshape(2, 6, 512).transpose(1, 0, 2).reshape(6, D)
    out_b, gain_one, bias_one, ff_out_b, gain_two, bias_two = [vectors[i] for i in range(6)]
    ff_in_b = packed[:, 6 * 512 : 7 * 512].reshape(-1)
    qv_b = packed[:, 7 * 512 :].reshape(-1, 2 * HD)
    hollow = jnp.zeros((qv_b.shape[0], HD), F32)
    qkv_b = jnp.concatenate([qv_b[:, :HD], hollow, qv_b[:, HD:]], 1).reshape(-1)

    x = own_rows(tokens, odd, col)
    incoming = own_rows(out_grad, odd, col)

    group = (row // 2) * 5
    labels = lax.dynamic_slice_in_dim(segments, (group + (row % 2) * 3 + col) * SEQ, SEQ)
    shared = lax.dynamic_slice_in_dim(segments, (group + 2) * SEQ, SEQ)
    shared = jnp.concatenate(
        [lax.dynamic_slice_in_dim(shared, (member ^ offset) * QUARTER, QUARTER) for offset in range(4)]
    )

    qkv = (mm(x, qkv_w, NN) + qkv_b).astype(BF16)
    qkv_shared = spread_heads(qkv[SEQ:], member)
    heads_own, probs_own = attend(qkv[:SEQ], labels)
    heads_shared, probs_shared = attend(qkv_shared, shared)
    heads = jnp.concatenate([heads_own, collect_heads(heads_shared, member)], 0)
    branch_one = mm(heads, out_w, NN) + out_b
    middle, unit_one, inverse_one = norm_forward(x.astype(F32) + branch_one, gain_one, bias_one)
    middle_low = middle.astype(BF16)
    hidden = mm(middle_low, ff_in_w, NN) + ff_in_b
    gelu_value, pullback = jax.vjp(gelu_exact, hidden)
    active = gelu_value.astype(BF16)
    branch_two = mm(active, ff_out_w, NN) + ff_out_b
    layer_out, unit_two, inverse_two = norm_forward(middle + branch_two, gain_two, bias_two)
    layer_out = give_back(layer_out, odd, col)

    back_two, ln2_gain_part, ln2_bias_part = norm_backward(incoming.astype(F32), unit_two, inverse_two, gain_two)
    d_two = back_two.astype(BF16)
    ff_out_bias_part = jnp.sum(d_two, 0, dtype=F32)
    ff_out_grad = reduce_down(mm(active, d_two, TN))
    d_hidden = pullback(mm(d_two, ff_out_w, NT))[0].astype(BF16)
    ff_in_bias_part = jnp.sum(d_hidden, 0, dtype=F32)
    ff_in_grad = reduce_up(mm(middle_low, d_hidden, TN))
    back_middle = back_two + mm(d_hidden, ff_in_w, NT)
    back_one, ln1_gain_part, ln1_bias_part = norm_backward(back_middle, unit_one, inverse_one, gain_one)
    d_one = back_one.astype(BF16)
    out_bias_part = jnp.sum(d_one, 0, dtype=F32)
    out_grad_w = reduce_down(mm(heads, d_one, TN))
    d_heads = mm(d_one, out_w, NT).astype(BF16)
    d_shared = spread_heads(d_heads[SEQ:], member)
    d_qkv_own = attend_back(qkv[:SEQ], probs_own, d_heads[:SEQ])
    d_qkv_shared = attend_back(qkv_shared, probs_shared, d_shared)
    d_qkv = jnp.concatenate([d_qkv_own, collect_heads(d_qkv_shared, member)], 0)
    qkv_grad = reduce_up(mm(x, d_qkv, TN))
    column_sums = jnp.sum(d_qkv, 0, dtype=F32).reshape(-1, 3, HD)
    qv_part = jnp.concatenate([column_sums[:, 0], column_sums[:, 2]], 1).reshape(-1)
    input_grad = give_back(back_one + mm(d_qkv, qkv_w, NT), odd, col)

    sums = lax.psum(
        jnp.concatenate(
            [
                out_bias_part,
                ln1_gain_part,
                ln1_bias_part,
                ff_out_bias_part,
                ln2_gain_part,
                ln2_bias_part,
                ff_in_bias_part,
                qv_part,
            ]
        ),
        ("dp", "row", "col"),
    )
    halves = lax.dynamic_slice_in_dim(sums[: 6 * D].reshape(6, 2, D // 2), col, 1, 1)[:, 0]
    place = row * 2 + col
    ff_in_part = lax.dynamic_slice_in_dim(sums, 6 * D + place * 512, 512)
    qv_mine = lax.dynamic_slice_in_dim(sums, 6 * D + 4 * D + place * 256, 256).reshape(2, 2 * HD)
    return (
        layer_out,
        input_grad,
        qkv_grad,
        qv_mine,
        out_grad_w,
        halves[0],
        halves[1],
        halves[2],
        ff_in_grad,
        ff_in_part,
        ff_out_grad,
        halves[3],
        halves[4],
        halves[5],
    )


def solution(mesh):
    in_specs = (
        P(("dp", "row"), "col"),
        P("dp"),
        P("col", "row"),
        P(("row", "col"), None),
        P("row", "col"),
        P("col"),
        P("col"),
        P("col"),
        P("col", "row"),
        P(("row", "col")),
        P("row", "col"),
        P("col"),
        P("col"),
        P("col"),
        P(("dp", "row"), "col"),
    )
    out_specs = (
        P(("dp", "row"), "col"),
        P(("dp", "row"), "col"),
        P("col", "row"),
        P(("row", "col"), None),
        P("row", "col"),
        P("col"),
        P("col"),
        P("col"),
        P("col", "row"),
        P(("row", "col")),
        P("row", "col"),
        P("col"),
        P("col"),
        P("col"),
    )
    return jax.shard_map(local, mesh=mesh, in_specs=in_specs, out_specs=out_specs, check_vma=False)
```

```python
import math

import jax
import jax.numpy as jnp
from jax import lax
from jax.experimental import pallas as pl
from jax.experimental.pallas import tpu as pltpu
from jax.sharding import PartitionSpec as P

D = 1024
HD = 64
SEQ = 512
QUARTER = SEQ // 4
GRID = ("row", "col")

EPSILON = 1e-06
NEGATIVE = -1e30
F32 = jnp.float32
BF16 = jnp.bfloat16
NN = (((1,), (0,)), ((), ()))
NT = (((1,), (1,)), ((), ()))
TN = (((0,), (0,)), ((), ()))
MIB = 1 << 20


def mm(left, right, contract):
    return lax.dot_general(left, right, contract, preferred_element_type=F32)


def attend_kernel(qkv_ref, column_ref, line_ref, heads_ref, probs_ref, mask):
    @pl.when(pl.program_id(0) == 0)
    def _():
        mask[...] = jnp.where(column_ref[...] == line_ref[...], 0.0, NEGATIVE)

    mixed = []
    for head in range(2):
        base = head * 3 * HD
        query = qkv_ref[:, base : base + HD] * jnp.asarray(1 / math.sqrt(HD), BF16)
        key = qkv_ref[:, base + HD : base + 2 * HD]
        value = qkv_ref[:, base + 2 * HD : base + 3 * HD]
        scores = mm(key, query, NT) + mask[...]
        powers = jnp.exp(scores - jnp.max(scores, 0, keepdims=True))
        total = jnp.sum(powers, 0, keepdims=True)
        probs = (powers * (1.0 / total)).astype(BF16)
        probs_ref[head] = probs
        mixed.append(mm(value, probs, TN))
    heads_ref[...] = jnp.concatenate(mixed, 0).T.astype(BF16)


def attend(qkv, labels):
    pairs = qkv.shape[1] // (6 * HD)
    return pl.pallas_call(
        attend_kernel,
        grid=(pairs,),
        in_specs=[
            pl.BlockSpec((SEQ, 6 * HD), lambda i: (0, i)),
            pl.BlockSpec((SEQ, 1), lambda i: (0, 0)),
            pl.BlockSpec((1, SEQ), lambda i: (0, 0)),
        ],
        out_specs=[
            pl.BlockSpec((SEQ, 2 * HD), lambda i: (0, i)),
            pl.BlockSpec((2, SEQ, SEQ), lambda i: (i, 0, 0)),
        ],
        out_shape=[
            jax.ShapeDtypeStruct((SEQ, pairs * 2 * HD), BF16),
            jax.ShapeDtypeStruct((pairs * 2, SEQ, SEQ), BF16),
        ],
        scratch_shapes=[pltpu.VMEM((SEQ, SEQ), F32)],
        compiler_params=pltpu.CompilerParams(vmem_limit_bytes=32 * MIB),
        cost_estimate=pl.CostEstimate(
            flops=pairs * 2 * 4 * SEQ * SEQ * 256, bytes_accessed=pairs * 2 * SEQ * SEQ * 2, transcendentals=pairs * 2 * SEQ * SEQ
        ),
        name="attend",
    )(qkv, labels[:, None], labels[None, :])


def attend_back_kernel(qkv_ref, probs_ref, grad_ref, out_ref):
    for head in range(2):
        base = head * 3 * HD
        scale = jnp.asarray(1 / math.sqrt(HD), BF16)
        query = qkv_ref[:, base : base + HD] * scale
        key = qkv_ref[:, base + HD : base + 2 * HD] * scale
        value = qkv_ref[:, base + 2 * HD : base + 3 * HD]
        grad = grad_ref[:, head * HD : (head + 1) * HD]
        probs = probs_ref[head]
        d_value = mm(probs, grad, NN)
        d_probs = mm(value, grad, NT)
        wide = probs.astype(F32)
        delta = jnp.sum(wide * d_probs, 0, keepdims=True)
        d_scores = (wide * (d_probs - delta)).astype(BF16)
        d_key = mm(d_scores, query, NN)
        d_query = mm(key, d_scores, TN).T
        out_ref[:, base : base + HD] = d_query.astype(BF16)
        out_ref[:, base + HD : base + 2 * HD] = d_key.astype(BF16)
        out_ref[:, base + 2 * HD : base + 3 * HD] = d_value.astype(BF16)


def attend_back(qkv, probs, grad):
    pairs = qkv.shape[1] // (6 * HD)
    return pl.pallas_call(
        attend_back_kernel,
        grid=(pairs,),
        in_specs=[
            pl.BlockSpec((SEQ, 6 * HD), lambda i: (0, i)),
            pl.BlockSpec((2, SEQ, SEQ), lambda i: (i, 0, 0)),
            pl.BlockSpec((SEQ, 2 * HD), lambda i: (0, i)),
        ],
        out_specs=pl.BlockSpec((SEQ, 6 * HD), lambda i: (0, i)),
        out_shape=jax.ShapeDtypeStruct((SEQ, qkv.shape[1]), BF16),
        compiler_params=pltpu.CompilerParams(vmem_limit_bytes=32 * MIB),
        cost_estimate=pl.CostEstimate(
            flops=pairs * 2 * 10 * SEQ * SEQ * 256, bytes_accessed=pairs * 2 * SEQ * SEQ * 2, transcendentals=0
        ),
        name="attend_back",
    )(qkv, probs, grad)


def own_rows(value, odd, col):
    rolled = jnp.where(odd, jnp.roll(value, -2 * QUARTER, 0), value)
    first = jnp.concatenate([rolled[:SEQ], rolled[2 * SEQ : 2 * SEQ + QUARTER]], 0)
    second = jnp.concatenate([rolled[SEQ : 2 * SEQ], rolled[2 * SEQ + QUARTER :]], 0)
    mine = jnp.where(col == 0, first, second)
    other = lax.ppermute(jnp.where(col == 0, second, first), "col", [(0, 1), (1, 0)])
    return jnp.concatenate([jnp.where(col == 0, mine, other), jnp.where(col == 0, other, mine)], 1)


def give_back(value, odd, col):
    half = D // 2
    mine = jnp.where(col == 0, value[:, :half], value[:, half:])
    leaving = jnp.where(col == 0, value[:, half:], value[:, :half])
    other = lax.ppermute(leaving.astype(BF16), "col", [(0, 1), (1, 0)]).astype(F32)
    first = jnp.where(col == 0, mine, other)
    second = jnp.where(col == 0, other, mine)
    rolled = jnp.concatenate([first[:SEQ], second[:SEQ], first[SEQ:], second[SEQ:]], 0)
    return jnp.where(odd, jnp.roll(rolled, 2 * QUARTER, 0), rolled)


def swap(offset):
    return [(i, i ^ offset) for i in range(8)]


def spread_heads(value, member):
    width = value.shape[1] // 4
    pieces = []
    for offset in range(4):
        piece = lax.dynamic_slice_in_dim(value, (member ^ offset) * width, width, 1)
        pieces.append(piece if offset == 0 else lax.ppermute(piece, GRID, swap(offset)))
    return jnp.concatenate(pieces, 0)


def collect_heads(value, member):
    width = value.shape[1]
    whole = jnp.zeros((QUARTER, 4 * width), value.dtype)
    for offset in range(4):
        piece = value[offset * QUARTER : (offset + 1) * QUARTER]
        if offset:
            piece = lax.ppermute(piece, GRID, swap(offset))
        whole = lax.dynamic_update_slice_in_dim(whole, piece, (member ^ offset) * width, 1)
    return whole


def dense(kernel, grid, in_specs, out_specs, out_shape, scratch, flops, name):
    return pl.pallas_call(
        kernel,
        grid=(grid,),
        in_specs=in_specs,
        out_specs=out_specs,
        out_shape=out_shape,
        scratch_shapes=scratch,
        compiler_params=pltpu.CompilerParams(vmem_limit_bytes=48 * MIB),
        cost_estimate=pl.CostEstimate(flops=flops, bytes_accessed=flops // 640, transcendentals=0),
        name=name,
    )


def whole(value):
    return pl.BlockSpec(value.shape, lambda i: (0,) * value.ndim)


def columns_of(value, parts=4):
    return pl.BlockSpec((value.shape[0], value.shape[1] // parts), lambda i: (0, i))


def pair_of(stack):
    depth = stack.shape[1] // 256 * 256
    return pl.BlockSpec((2, depth, stack.shape[2]), lambda i: (i, 0, 0))


def shaped(shape, kind):
    return jax.ShapeDtypeStruct(shape, kind)


def halves_times(left_ref, weight_ref, start, width):
    half = left_ref.shape[1] // 2
    stop = start + width
    return mm(left_ref[:, :half], weight_ref[0, :, start:stop], NN) + mm(
        left_ref[:, half:], weight_ref[1, :, start:stop], NN
    )


def qkv_kernel(x_ref, weight_ref, bias_ref, out_ref):
    for start in range(0, out_ref.shape[1], 256):
        part = halves_times(x_ref, weight_ref, start, 256)
        out_ref[:, start : start + 256] = (part + bias_ref[:, start : start + 256]).astype(BF16)


def project_qkv(x, stack, bias):
    width = 4 * stack.shape[2]
    return dense(
        qkv_kernel,
        4,
        [whole(x), pair_of(stack), columns_of(bias)],
        pl.BlockSpec((x.shape[0], width // 4), lambda i: (0, i)),
        shaped((x.shape[0], width), BF16),
        [],
        2 * x.shape[0] * D * width,
        "project_qkv",
    )(x, stack, bias)


def hidden_kernel(x_ref, weight_ref, bias_ref, active_ref, slope_ref):
    for start in range(0, active_ref.shape[1], 256):
        stop = start + 256
        hidden = halves_times(x_ref, weight_ref, start, 256) + bias_ref[:, start:stop]
        share = 0.5 * (1.0 + lax.erf(hidden * math.sqrt(0.5)))
        bell = jnp.exp(hidden * hidden * -0.5) * (1 / math.sqrt(2 * math.pi))
        active_ref[:, start:stop] = (hidden * share).astype(BF16)
        slope_ref[:, start:stop] = (share + hidden * bell).astype(BF16)


def project_hidden(x, stack, bias):
    width = 4 * stack.shape[2]
    block = pl.BlockSpec((x.shape[0], width // 4), lambda i: (0, i))
    return dense(
        hidden_kernel,
        4,
        [whole(x), pair_of(stack), columns_of(bias)],
        [block, block],
        [shaped((x.shape[0], width), BF16)] * 2,
        [],
        4 * x.shape[0] * D * width,
        "project_hidden",
    )(x, stack, bias)


def add_product(left_ref, weight_ref, total, contract):
    step = pl.program_id(0)
    half = D // 2
    for col in range(2):
        part = mm(left_ref[...], weight_ref[col], contract)
        span = slice(col * half, (col + 1) * half)

        @pl.when(step == 0)
        def _():
            total[:, span] = part

        @pl.when(step > 0)
        def _():
            total[:, span] += part


ROWS = 128


def row_blocks(ref):
    return [pl.ds(start, ROWS) for start in range(0, ref.shape[0], ROWS)]


def norm_parts(value):
    center = jnp.sum(value, 1, keepdims=True) * (1 / D)
    squares = jnp.sum(value * value, 1, keepdims=True) * (1 / D)
    inverse = lax.rsqrt(squares - center * center + EPSILON)
    return ((value - center) * inverse, inverse)


def norm_back(grad, unit, inverse, gain):
    scaled = grad * gain
    mean = jnp.sum(scaled, 1, keepdims=True) * (1 / D)
    paired = jnp.sum(scaled * unit, 1, keepdims=True) * (1 / D)
    return inverse * (scaled - mean - unit * paired)


def total_of(value):
    return jnp.sum(value, 0, keepdims=True)


def first_norm_kernel(heads_ref, weight_ref, x_ref, vec_ref, unit_ref, inverse_ref, low_ref, total):
    add_product(heads_ref, weight_ref, total, NN)

    @pl.when(pl.program_id(0) == 3)
    def _():
        for rows in row_blocks(x_ref):
            value = x_ref[rows, :].astype(F32) + (total[rows, :] + vec_ref[0:1, :])
            unit, inverse = norm_parts(value)
            unit_ref[rows, :] = unit
            inverse_ref[rows, :] = inverse
            low_ref[rows, :] = (unit * vec_ref[1:2, :] + vec_ref[2:3, :]).astype(BF16)


def first_norm(heads, stack, x, vec):
    rows = x.shape[0]
    outs = [shaped((rows, D), F32), shaped((rows, 1), F32), shaped((rows, D), BF16)]
    return dense(
        first_norm_kernel,
        4,
        [columns_of(heads), pair_of(stack), whole(x), whole(vec)],
        [whole(out) for out in outs],
        outs,
        [pltpu.VMEM((rows, D), F32)],
        2 * rows * D * D,
        "first_norm",
    )(heads, stack, x, vec)


def second_norm_kernel(
    active_ref, weight_ref, unit_ref, incoming_ref, vec_ref, out_ref, back_ref, low_ref, sums_ref, total
):
    add_product(active_ref, weight_ref, total, NN)

    @pl.when(pl.program_id(0) == 3)
    def _():
        sums = [jnp.zeros((1, D), F32)] * 3
        for rows in row_blocks(out_ref):
            middle = unit_ref[rows, :] * vec_ref[1:2, :] + vec_ref[2:3, :]
            unit, inverse = norm_parts(middle + (total[rows, :] + vec_ref[3:4, :]))
            out_ref[rows, :] = unit * vec_ref[4:5, :] + vec_ref[5:6, :]
            grad = incoming_ref[rows, :].astype(F32)
            back = norm_back(grad, unit, inverse, vec_ref[4:5, :])
            low = back.astype(BF16)
            back_ref[rows, :] = back
            low_ref[rows, :] = low
            news = [total_of(low.astype(F32)), total_of(grad * unit), total_of(grad)]
            sums = [old + new for old, new in zip(sums, news)]
        for place in range(3):
            sums_ref[place : place + 1, :] = sums[place]


def second_norm(active, stack, unit, incoming, vec):
    rows = unit.shape[0]
    outs = [shaped((rows, D), F32), shaped((rows, D), F32), shaped((rows, D), BF16), shaped((3, D), F32)]
    return dense(
        second_norm_kernel,
        4,
        [columns_of(active), pair_of(stack), whole(unit), whole(incoming), whole(vec)],
        [whole(out) for out in outs],
        outs,
        [pltpu.VMEM((rows, D), F32)],
        2 * rows * D * active.shape[1],
        "second_norm",
    )(active, stack, unit, incoming, vec)


def first_back_kernel(
    d_hidden_ref, weight_ref, back_ref, unit_ref, inverse_ref, vec_ref, out_ref, low_ref, sums_ref, total
):
    add_product(d_hidden_ref, weight_ref, total, NT)

    @pl.when(pl.program_id(0) == 3)
    def _():
        sums = [jnp.zeros((1, D), F32)] * 3
        for rows in row_blocks(out_ref):
            grad = back_ref[rows, :] + total[rows, :]
            unit = unit_ref[rows, :]
            back = norm_back(grad, unit, inverse_ref[rows, :], vec_ref[1:2, :])
            low = back.astype(BF16)
            out_ref[rows, :] = back
            low_ref[rows, :] = low
            news = [total_of(low.astype(F32)), total_of(grad * unit), total_of(grad)]
            sums = [old + new for old, new in zip(sums, news)]
        for place in range(3):
            sums_ref[place : place + 1, :] = sums[place]


def first_back(d_hidden, stack, back, unit, inverse, vec):
    rows = unit.shape[0]
    outs = [shaped((rows, D), F32), shaped((rows, D), BF16), shaped((3, D), F32)]
    return dense(
        first_back_kernel,
        4,
        [columns_of(d_hidden), pair_of(stack), whole(back), whole(unit), whole(inverse), whole(vec)],
        [whole(out) for out in outs],
        outs,
        [pltpu.VMEM((rows, D), F32)],
        2 * rows * D * d_hidden.shape[1],
        "first_back",
    )(d_hidden, stack, back, unit, inverse, vec)


def input_back_kernel(d_qkv_ref, weight_ref, back_ref, out_ref, sums_ref):
    step = pl.program_id(0)
    half = D // 2
    sums_ref[...] = total_of(d_qkv_ref[...].astype(F32))
    for col in range(2):
        part = mm(d_qkv_ref[...], weight_ref[col], NT)
        span = slice(col * half, (col + 1) * half)

        @pl.when(step == 0)
        def _():
            out_ref[:, span] = back_ref[:, span] + part

        @pl.when(step > 0)
        def _():
            out_ref[:, span] += part


def input_back(d_qkv, stack, back):
    rows, width = d_qkv.shape
    outs = [shaped((rows, D), F32), shaped((1, width), F32)]
    return dense(
        input_back_kernel,
        4,
        [columns_of(d_qkv), pair_of(stack), whole(back)],
        [whole(outs[0]), columns_of(outs[1])],
        outs,
        [],
        2 * rows * D * width,
        "input_back",
    )(d_qkv, stack, back)


def columns_back(grad_ref, weight_ref, start, stop):
    half = D // 2
    return mm(grad_ref[:, :half], weight_ref[0, start:stop, :], NT) + mm(
        grad_ref[:, half:], weight_ref[1, start:stop, :], NT
    )


def hidden_back_kernel(grad_ref, weight_ref, slope_ref, out_ref, sums_ref):
    for start in range(0, out_ref.shape[1], 256):
        span = slice(start, start + 256)
        part = columns_back(grad_ref, weight_ref, start, start + 256)
        low = (part * slope_ref[:, span].astype(F32)).astype(BF16)
        out_ref[:, span] = low
        sums_ref[:, span] = total_of(low.astype(F32))


def hidden_back(grad, stack, slope):
    outs = [shaped(slope.shape, BF16), shaped((1, slope.shape[1]), F32)]
    return dense(
        hidden_back_kernel,
        4,
        [whole(grad), pair_of(stack), columns_of(slope)],
        [columns_of(out) for out in outs],
        outs,
        [],
        2 * grad.shape[0] * D * slope.shape[1],
        "hidden_back",
    )(grad, stack, slope)


def heads_back_kernel(grad_ref, weight_ref, out_ref):
    out_ref[...] = columns_back(grad_ref, weight_ref, 0, weight_ref.shape[1]).astype(BF16)


def heads_back(grad, stack):
    return dense(
        heads_back_kernel,
        4,
        [whole(grad), pair_of(stack)],
        columns_of(grad),
        shaped(grad.shape, BF16),
        [],
        2 * grad.shape[0] * D * D,
        "heads_back",
    )(grad, stack)


def grad_up_kernel(left_ref, right_ref, out_ref, turned):
    @pl.when(pl.program_id(0) == 0)
    def _():
        turned[...] = left_ref[...].T

    half = D // 2
    for col in range(2):
        out_ref[col] = mm(turned[col * half : (col + 1) * half, :], right_ref[...], NN).astype(BF16)


def grad_up(left, right):
    width = right.shape[1] // 4
    out = shaped((8, D // 2, width), BF16)
    return dense(
        grad_up_kernel,
        4,
        [whole(left), columns_of(right)],
        pair_of(out),
        out,
        [pltpu.VMEM((D, left.shape[0]), BF16)],
        2 * left.shape[0] * D * right.shape[1],
        "grad_up",
    )(left, right)


def grad_down_kernel(left_ref, right_ref, out_ref):
    half = D // 2
    turned = left_ref[...].T
    for col in range(2):
        out_ref[col] = mm(turned, right_ref[:, col * half : (col + 1) * half], NN).astype(BF16)


def grad_down(left, right):
    width = left.shape[1] // 4
    out = shaped((8, width, D // 2), BF16)
    return dense(
        grad_down_kernel,
        4,
        [columns_of(left), whole(right)],
        pair_of(out),
        out,
        [],
        2 * left.shape[0] * D * left.shape[1],
        "grad_down",
    )(left, right)


def gather_weight(shard):
    return lax.all_gather(shard, GRID, axis=0, tiled=False)


def reduce_stack(stack):
    return lax.psum_scatter(stack, GRID, scatter_dimension=0, tiled=False)


def in_three(value):
    high = lax.reduce_precision(value, 8, 7)
    rest = value - high
    mid = lax.reduce_precision(rest, 8, 7)
    return jnp.stack([high, mid, rest - mid]).astype(BF16)


def local(
    tokens,
    segments,
    qkv_weight,
    qv_bias,
    out_weight,
    out_bias,
    ln1_gain,
    ln1_bias,
    ff_in_weight,
    ff_in_bias,
    ff_out_weight,
    ff_out_bias,
    ln2_gain,
    ln2_bias,
    out_grad,
):
    row, col = lax.axis_index("row"), lax.axis_index("col")
    odd = row % 2 == 1
    member = (row % 2) * 2 + col

    packed = jnp.concatenate(
        [out_bias, ln1_gain, ln1_bias, ff_out_bias, ln2_gain, ln2_bias, ff_in_bias, qv_bias.reshape(-1)]
    )
    riders = in_three(packed).reshape(15, 768)
    riders = jnp.concatenate([qkv_weight, riders, jnp.zeros((1, 768), BF16)], 0)
    qkv_w = gather_weight(riders)
    out_w = gather_weight(out_weight)
    ff_in_w = gather_weight(ff_in_weight)
    ff_out_w = gather_weight(ff_out_weight)

    packed = qkv_w[:, D // 2 : D // 2 + 15].astype(F32).reshape(8, 3, packed.shape[0])
    packed = (packed[:, 0] + packed[:, 1]) + packed[:, 2]
    vec = packed[:2, : 6 * 512].reshape(2, 6, 512).transpose(1, 0, 2).reshape(6, D)
    ff_in_b = packed[:, 6 * 512 : 7 * 512].reshape(1, -1)
    qv_b = packed[:, 7 * 512 :].reshape(-1, 2 * HD)
    hollow = jnp.zeros((qv_b.shape[0], HD), F32)
    qkv_b = jnp.concatenate([qv_b[:, :HD], hollow, qv_b[:, HD:]], 1).reshape(1, -1)

    x = own_rows(tokens, odd, col)
    incoming = own_rows(out_grad, odd, col)

    group = (row // 2) * 5
    labels = lax.dynamic_slice_in_dim(segments, (group + (row % 2) * 3 + col) * SEQ, SEQ)
    shared = lax.dynamic_slice_in_dim(segments, (group + 2) * SEQ, SEQ)
    shared = jnp.concatenate(
        [lax.dynamic_slice_in_dim(shared, (member ^ offset) * QUARTER, QUARTER) for offset in range(4)]
    )

    qkv = project_qkv(x, qkv_w, qkv_b)
    qkv_shared = spread_heads(qkv[SEQ:], member)
    heads_own, probs_own = attend(qkv, labels)
    heads_shared, probs_shared = attend(qkv_shared, shared)
    heads = jnp.concatenate([heads_own, collect_heads(heads_shared, member)], 0)
    unit_one, inverse_one, middle_low = first_norm(heads, out_w, x, vec)
    active, slope = project_hidden(middle_low, ff_in_w, ff_in_b)
    layer_out, back_two, d_two, sums_two = second_norm(active, ff_out_w, unit_one, incoming, vec)

    ff_out_grad = grad_down(active, d_two)
    d_two, ff_out_grad = lax.optimization_barrier((d_two, ff_out_grad))
    ff_out_grad = reduce_stack(ff_out_grad)
    layer_out = give_back(layer_out, odd, col)
    d_hidden, ff_in_bias_part = hidden_back(d_two, ff_out_w, slope)
    ff_in_grad = grad_up(middle_low, d_hidden)
    d_hidden, ff_in_grad = lax.optimization_barrier((d_hidden, ff_in_grad))
    ff_in_grad = reduce_stack(ff_in_grad)
    back_one, d_one, sums_one = first_back(d_hidden, ff_in_w, back_two, unit_one, inverse_one, vec)
    out_w_grad = grad_down(heads, d_one)
    d_one, out_w_grad = lax.optimization_barrier((d_one, out_w_grad))
    out_w_grad = reduce_stack(out_w_grad)
    d_heads = heads_back(d_one, out_w)
    d_shared = spread_heads(d_heads[SEQ:], member)
    d_qkv_own = attend_back(qkv, probs_own, d_heads)
    d_qkv_shared = attend_back(qkv_shared, probs_shared, d_shared)
    d_qkv = jnp.concatenate([d_qkv_own, collect_heads(d_qkv_shared, member)], 0)
    qkv_grad = grad_up(x, d_qkv)
    d_qkv, qkv_grad = lax.optimization_barrier((d_qkv, qkv_grad))
    qkv_grad = reduce_stack(qkv_grad)
    input_grad, column_sums = input_back(d_qkv, qkv_w, back_one)
    input_grad = give_back(input_grad, odd, col)
    column_sums = column_sums.reshape(-1, 3, HD)
    qv_part = jnp.concatenate([column_sums[:, 0], column_sums[:, 2]], 1)

    ff_out_grad = lax.psum(ff_out_grad, "dp")
    ff_in_grad, ff_out_grad = lax.optimization_barrier((ff_in_grad, ff_out_grad))
    ff_in_grad = lax.psum(ff_in_grad, "dp")
    out_w_grad, ff_in_grad = lax.optimization_barrier((out_w_grad, ff_in_grad))
    out_w_grad = lax.psum(out_w_grad, "dp")
    qkv_grad, out_w_grad = lax.optimization_barrier((qkv_grad, out_w_grad))
    qkv_grad = lax.psum(qkv_grad, "dp")

    sums = jnp.concatenate(
        [sums_one.reshape(-1), sums_two.reshape(-1), ff_in_bias_part.reshape(-1), qv_part.reshape(-1)]
    )
    sums = lax.psum(sums, ("dp", "row", "col"))
    halves = lax.dynamic_slice_in_dim(sums[: 6 * D].reshape(6, 2, D // 2), col, 1, 1)[:, 0]
    place = row * 2 + col
    ff_in_part = lax.dynamic_slice_in_dim(sums, 6 * D + place * 512, 512)
    qv_mine = lax.dynamic_slice_in_dim(sums, 6 * D + 4 * D + place * 256, 256).reshape(2, 2 * HD)
    return (
        layer_out,
        input_grad,
        qkv_grad.astype(F32),
        qv_mine,
        out_w_grad.astype(F32),
        halves[0],
        halves[1],
        halves[2],
        ff_in_grad.astype(F32),
        ff_in_part,
        ff_out_grad.astype(F32),
        halves[3],
        halves[4],
        halves[5],
    )


def solution(mesh):
    in_specs = (
        P(("dp", "row"), "col"),
        P("dp"),
        P("col", "row"),
        P(("row", "col"), None),
        P("row", "col"),
        P("col"),
        P("col"),
        P("col"),
        P("col", "row"),
        P(("row", "col")),
        P("row", "col"),
        P("col"),
        P("col"),
        P("col"),
        P(("dp", "row"), "col"),
    )
    out_specs = (
        P(("dp", "row"), "col"),
        P(("dp", "row"), "col"),
        P("col", "row"),
        P(("row", "col"), None),
        P("row", "col"),
        P("col"),
        P("col"),
        P("col"),
        P("col", "row"),
        P(("row", "col")),
        P("row", "col"),
        P("col"),
        P("col"),
        P("col"),
    )
    return jax.shard_map(local, mesh=mesh, in_specs=in_specs, out_specs=out_specs, check_vma=False)
```

```python
import functools
import math

import jax
import jax.numpy as jnp
from jax import lax
from jax.experimental import pallas as pl
from jax.experimental.pallas import tpu as pltpu
from jax.sharding import PartitionSpec as P

D = 1024
HD = 64
SEQ = 512
QUARTER = SEQ // 4
GRID = ("row", "col")

EPSILON = 1e-06
NEGATIVE = -1e30
F32 = jnp.float32
BF16 = jnp.bfloat16
NN = (((1,), (0,)), ((), ()))
NT = (((1,), (1,)), ((), ()))
TN = (((0,), (0,)), ((), ()))
MIB = 1 << 20


def mm(left, right, contract):
    return lax.dot_general(left, right, contract, preferred_element_type=F32)


def attend_kernel(qkv_ref, column_ref, line_ref, heads_ref, probs_ref, mask):
    @pl.when(pl.program_id(0) == 0)
    def _():
        mask[...] = jnp.where(column_ref[...] == line_ref[...], 0.0, NEGATIVE)

    mixed = []
    for head in range(2):
        base = head * 3 * HD
        query = qkv_ref[:, base : base + HD] * jnp.asarray(1 / math.sqrt(HD), BF16)
        key = qkv_ref[:, base + HD : base + 2 * HD]
        value = qkv_ref[:, base + 2 * HD : base + 3 * HD]
        scores = mm(key, query, NT) + mask[...]
        powers = jnp.exp(scores - jnp.max(scores, 0, keepdims=True))
        total = jnp.sum(powers, 0, keepdims=True)
        probs = (powers * (1.0 / total)).astype(BF16)
        probs_ref[head] = probs
        mixed.append(mm(value, probs, TN))
    heads_ref[...] = jnp.concatenate(mixed, 0).T.astype(BF16)


def attend(qkv, labels):
    pairs = qkv.shape[1] // (6 * HD)
    return pl.pallas_call(
        attend_kernel,
        grid=(pairs,),
        in_specs=[
            pl.BlockSpec((SEQ, 6 * HD), lambda i: (0, i)),
            pl.BlockSpec((SEQ, 1), lambda i: (0, 0)),
            pl.BlockSpec((1, SEQ), lambda i: (0, 0)),
        ],
        out_specs=[
            pl.BlockSpec((SEQ, 2 * HD), lambda i: (0, i)),
            pl.BlockSpec((2, SEQ, SEQ), lambda i: (i, 0, 0)),
        ],
        out_shape=[
            jax.ShapeDtypeStruct((SEQ, pairs * 2 * HD), BF16),
            jax.ShapeDtypeStruct((pairs * 2, SEQ, SEQ), BF16),
        ],
        scratch_shapes=[pltpu.VMEM((SEQ, SEQ), F32)],
        compiler_params=pltpu.CompilerParams(vmem_limit_bytes=32 * MIB),
        cost_estimate=pl.CostEstimate(
            flops=pairs * 2 * 4 * SEQ * SEQ * 256, bytes_accessed=pairs * 2 * SEQ * SEQ * 2, transcendentals=pairs * 2 * SEQ * SEQ
        ),
        name="attend",
    )(qkv, labels[:, None], labels[None, :])


def attend_back_kernel(qkv_ref, probs_ref, grad_ref, out_ref):
    for head in range(2):
        base = head * 3 * HD
        scale = jnp.asarray(1 / math.sqrt(HD), BF16)
        query = qkv_ref[:, base : base + HD] * scale
        key = qkv_ref[:, base + HD : base + 2 * HD] * scale
        value = qkv_ref[:, base + 2 * HD : base + 3 * HD]
        grad = grad_ref[:, head * HD : (head + 1) * HD]
        probs = probs_ref[head]
        d_value = mm(probs, grad, NN)
        d_probs = mm(value, grad, NT)
        wide = probs.astype(F32)
        delta = jnp.sum(wide * d_probs, 0, keepdims=True)
        d_scores = (wide * (d_probs - delta)).astype(BF16)
        d_key = mm(d_scores, query, NN)
        d_query = mm(key, d_scores, TN).T
        out_ref[:, base : base + HD] = d_query.astype(BF16)
        out_ref[:, base + HD : base + 2 * HD] = d_key.astype(BF16)
        out_ref[:, base + 2 * HD : base + 3 * HD] = d_value.astype(BF16)


def attend_back(qkv, probs, grad):
    pairs = qkv.shape[1] // (6 * HD)
    return pl.pallas_call(
        attend_back_kernel,
        grid=(pairs,),
        in_specs=[
            pl.BlockSpec((SEQ, 6 * HD), lambda i: (0, i)),
            pl.BlockSpec((2, SEQ, SEQ), lambda i: (i, 0, 0)),
            pl.BlockSpec((SEQ, 2 * HD), lambda i: (0, i)),
        ],
        out_specs=pl.BlockSpec((SEQ, 6 * HD), lambda i: (0, i)),
        out_shape=jax.ShapeDtypeStruct((SEQ, qkv.shape[1]), BF16),
        compiler_params=pltpu.CompilerParams(vmem_limit_bytes=32 * MIB),
        cost_estimate=pl.CostEstimate(
            flops=pairs * 2 * 10 * SEQ * SEQ * 256, bytes_accessed=pairs * 2 * SEQ * SEQ * 2, transcendentals=0
        ),
        name="attend_back",
    )(qkv, probs, grad)


def swap_core(value):
    return lax.ppermute(value, "row", [(i, i ^ 1) for i in range(4)])


def swap_row(value):
    return lax.ppermute(value, "row", [(i, i ^ 2) for i in range(4)])


def swap_col(value):
    return lax.ppermute(value, "col", [(0, 1), (1, 0)])


def after(value, *others):
    return lax.optimization_barrier((value, *others))[0]


def add(*values):
    total = values[0].astype(F32)
    for value in values[1:]:
        total = total + value.astype(F32)
    return total.astype(BF16)


def own_rows(value, odd, col):
    rolled = jnp.where(odd, jnp.roll(value, -2 * QUARTER, 0), value)
    first = jnp.concatenate([rolled[:SEQ], rolled[2 * SEQ : 2 * SEQ + QUARTER]], 0)
    second = jnp.concatenate([rolled[SEQ : 2 * SEQ], rolled[2 * SEQ + QUARTER :]], 0)
    mine = jnp.where(col == 0, first, second)
    return jnp.concatenate([mine, swap_col(jnp.where(col == 0, second, first))], 1)


def give_back(mine, leaving, odd, col):
    other = swap_col(leaving).astype(F32)
    first = jnp.where(col == 0, mine, other)
    second = jnp.where(col == 0, other, mine)
    rolled = jnp.concatenate([first[:SEQ], second[:SEQ], first[SEQ:], second[SEQ:]], 0)
    return jnp.where(odd, jnp.roll(rolled, 2 * QUARTER, 0), rolled)


def swap(offset):
    return [(i, i ^ offset) for i in range(8)]


def spread_heads(value, member, row):
    width = value.shape[1] // 4
    pieces = []
    for offset in range(4):
        piece = lax.dynamic_slice_in_dim(value, ((member ^ offset) ^ row) * width, width, 1)
        pieces.append(piece if offset == 0 else lax.ppermute(piece, GRID, swap(offset)))
    return jnp.concatenate(pieces, 0)


def collect_heads(value, member, row):
    width = value.shape[1]
    whole = jnp.zeros((QUARTER, 4 * width), value.dtype)
    for offset in range(4):
        piece = value[offset * QUARTER : (offset + 1) * QUARTER]
        if offset:
            piece = lax.ppermute(piece, GRID, swap(offset))
        whole = lax.dynamic_update_slice_in_dim(whole, piece, ((member ^ offset) ^ row) * width, 1)
    return whole


class Shards:
    def __init__(self, shard, depth):
        half = depth // 2
        self.depth, self.width = depth, shard.shape[1]
        beside = swap_col(shard)
        across = swap_row(shard)
        top, bottom = swap_col(across[:half]), swap_row(beside[half:])
        self.first = (beside, across)
        near = [(0, 0, shard), (1, 0, beside), (4, 0, across), (5, 0, top), (5, half, bottom)]
        far = [(place + 2, start, swap_core(part)) for place, start, part in near]
        self.parts = near + far

    def riders(self):
        found = {}
        for place, start, part in self.parts:
            if start + part.shape[0] > self.depth:
                found[place] = part[self.depth - start :]
        return jnp.stack([found[place] for place in range(8)])


def dense(kernel, in_specs, out_specs, out_shape, scratch, flops, name, shards=None):
    if shards is None:
        body, extra_specs, extra_scratch = kernel, [], []
    else:
        places = [(place, start, min(part.shape[0], shards.depth - start)) for place, start, part in shards.parts]
        count = len(places)
        extra_specs = [pl.BlockSpec(memory_space=pl.ANY)] * count
        extra_scratch = [
            pltpu.VMEM((8, shards.depth, shards.width), BF16),
            pltpu.SemaphoreType.DMA((count,)),
        ]

        def body(*refs):
            step = pl.program_id(0)
            held, done = refs[-2:]
            copies = [
                pltpu.make_async_copy(
                    refs[k].at[pl.ds(0, rows)], held.at[place, pl.ds(start, rows)], done.at[k]
                )
                for k, (place, start, rows) in enumerate(places)
            ]
            for block in range(4):

                @pl.when(step == 0)
                def _():
                    for copy, (place, _, _) in zip(copies, places):
                        if place // 2 == block:
                            copy.start()

            for block in range(4):

                @pl.when(step == block)
                def _():
                    for copy, (place, _, _) in zip(copies, places):
                        if place // 2 == block:
                            copy.wait()

            kernel(held.at[pl.ds(2 * step, 2)], *refs[count:-2])

    return pl.pallas_call(
        body,
        grid=(4,),
        in_specs=extra_specs + in_specs,
        out_specs=out_specs,
        out_shape=out_shape,
        scratch_shapes=scratch + extra_scratch,
        compiler_params=pltpu.CompilerParams(vmem_limit_bytes=48 * MIB),
        cost_estimate=pl.CostEstimate(flops=flops, bytes_accessed=flops // 640, transcendentals=0),
        name=name,
    )


def whole(value):
    return pl.BlockSpec(value.shape, lambda i: (0,) * value.ndim)


def columns_of(value, parts=4):
    return pl.BlockSpec((value.shape[0], value.shape[1] // parts), lambda i: (0, i))


def shaped(shape, kind):
    return jax.ShapeDtypeStruct(shape, kind)


def halves_times(left_ref, weight_ref, start, width):
    half = left_ref.shape[1] // 2
    stop = start + width
    return mm(left_ref[:, :half], weight_ref[0, :, start:stop], NN) + mm(
        left_ref[:, half:], weight_ref[1, :, start:stop], NN
    )


def qkv_kernel(weight_ref, x_ref, bias_ref, out_ref):
    for start in range(0, out_ref.shape[1], 256):
        part = halves_times(x_ref, weight_ref, start, 256)
        out_ref[:, start : start + 256] = (part + bias_ref[:, start : start + 256]).astype(BF16)


def project_qkv(x, shards, bias):
    width = 4 * shards.width
    return dense(
        qkv_kernel,
        [whole(x), columns_of(bias)],
        pl.BlockSpec((x.shape[0], width // 4), lambda i: (0, i)),
        shaped((x.shape[0], width), BF16),
        [],
        2 * x.shape[0] * D * width,
        "project_qkv",
        shards,
    )(*[part for _, _, part in shards.parts], x, bias)


def hidden_kernel(weight_ref, x_ref, bias_ref, active_ref, slope_ref):
    for start in range(0, active_ref.shape[1], 256):
        stop = start + 256
        hidden = halves_times(x_ref, weight_ref, start, 256) + bias_ref[:, start:stop]
        share = 0.5 * (1.0 + lax.erf(hidden * math.sqrt(0.5)))
        bell = jnp.exp(hidden * hidden * -0.5) * (1 / math.sqrt(2 * math.pi))
        active_ref[:, start:stop] = (hidden * share).astype(BF16)
        slope_ref[:, start:stop] = (share + hidden * bell).astype(BF16)


def project_hidden(x, shards, bias):
    width = 4 * shards.width
    block = pl.BlockSpec((x.shape[0], width // 4), lambda i: (0, i))
    return dense(
        hidden_kernel,
        [whole(x), columns_of(bias)],
        [block, block],
        [shaped((x.shape[0], width), BF16)] * 2,
        [],
        4 * x.shape[0] * D * width,
        "project_hidden",
        shards,
    )(*[part for _, _, part in shards.parts], x, bias)


def add_product(left_ref, weight_ref, total, contract):
    step = pl.program_id(0)
    half = D // 2
    for col in range(2):
        part = mm(left_ref[...], weight_ref[col], contract)
        span = slice(col * half, (col + 1) * half)

        @pl.when(step == 0)
        def _():
            total[:, span] = part

        @pl.when(step > 0)
        def _():
            total[:, span] += part


ROWS = 16


def each_rows(count, body):
    @pl.loop(0, count // (2 * ROWS))
    def _(step):
        for part in range(2):
            body(pl.ds(pl.multiple_of((2 * step + part) * ROWS, ROWS), ROWS))


def add_rows(partial, place, value):
    partial[place] += value[:8] + value[8:]


def norm_parts(value):
    center = jnp.sum(value, 1, keepdims=True) * (1 / D)
    squares = jnp.sum(value * value, 1, keepdims=True) * (1 / D)
    inverse = lax.rsqrt(squares - center * center + EPSILON)
    return ((value - center) * inverse, inverse)


def norm_back(grad, unit, inverse, gain):
    scaled = grad * gain
    mean = jnp.sum(scaled, 1, keepdims=True) * (1 / D)
    paired = jnp.sum(scaled * unit, 1, keepdims=True) * (1 / D)
    return inverse * (scaled - mean - unit * paired)


def total_of(value):
    return jnp.sum(value, 0, keepdims=True)


def first_norm_kernel(weight_ref, heads_ref, x_ref, vec_ref, unit_ref, inverse_ref, low_ref, total):
    add_product(heads_ref, weight_ref, total, NN)

    @pl.when(pl.program_id(0) == 3)
    def _():
        def body(rows):
            value = x_ref[rows, :].astype(F32) + (total[rows, :] + vec_ref[0:1, :])
            unit, inverse = norm_parts(value)
            unit_ref[rows, :] = unit
            inverse_ref[rows, :] = inverse
            low_ref[rows, :] = (unit * vec_ref[1:2, :] + vec_ref[2:3, :]).astype(BF16)

        each_rows(x_ref.shape[0], body)


def first_norm(heads, shards, x, vec):
    rows = x.shape[0]
    outs = [shaped((rows, D), F32), shaped((rows, 1), F32), shaped((rows, D), BF16)]
    return dense(
        first_norm_kernel,
        [columns_of(heads), whole(x), whole(vec)],
        [whole(out) for out in outs],
        outs,
        [pltpu.VMEM((rows, D), F32)],
        2 * rows * D * D,
        "first_norm",
        shards,
    )(*[part for _, _, part in shards.parts], heads, x, vec)


def second_norm_kernel(
    weight_ref, active_ref, unit_ref, incoming_ref, vec_ref, out_ref, leave_ref, back_ref, low_ref, sums_ref, total, partial
):
    add_product(active_ref, weight_ref, total, NN)

    @pl.when(pl.program_id(0) == 3)
    def _():
        partial[...] = jnp.zeros_like(partial)
        half = D // 2

        def body(rows):
            middle = unit_ref[rows, :] * vec_ref[1:2, :] + vec_ref[2:3, :]
            unit, inverse = norm_parts(middle + (total[rows, :] + vec_ref[3:4, :]))
            out = unit * vec_ref[4:5, :] + vec_ref[5:6, :]
            out_ref[rows, :] = out[:, :half]
            leave_ref[rows, :] = out[:, half:].astype(BF16)
            grad = incoming_ref[rows, :].astype(F32)
            add_rows(partial, 1, grad * unit)
            add_rows(partial, 2, grad)
            back = norm_back(grad, unit, inverse, vec_ref[4:5, :])
            low = back.astype(BF16)
            back_ref[rows, :] = back
            low_ref[rows, :] = low
            add_rows(partial, 0, low.astype(F32))

        each_rows(unit_ref.shape[0], body)
        for place in range(3):
            sums_ref[place : place + 1, :] = total_of(partial[place])


def second_norm(active, shards, unit, incoming, vec):
    rows = unit.shape[0]
    outs = [
        shaped((rows, D // 2), F32),
        shaped((rows, D // 2), BF16),
        shaped((rows, D), F32),
        shaped((rows, D), BF16),
        shaped((3, D), F32),
    ]
    return dense(
        second_norm_kernel,
        [columns_of(active), whole(unit), whole(incoming), whole(vec)],
        [whole(out) for out in outs],
        outs,
        [pltpu.VMEM((rows, D), F32), pltpu.VMEM((3, 8, D), F32)],
        2 * rows * D * active.shape[1],
        "second_norm",
        shards,
    )(*[part for _, _, part in shards.parts], active, unit, incoming, vec)


def first_back_kernel(
    weight_ref, d_hidden_ref, back_ref, unit_ref, inverse_ref, vec_ref, out_ref, low_ref, sums_ref, total, partial
):
    add_product(d_hidden_ref, weight_ref, total, NT)

    @pl.when(pl.program_id(0) == 3)
    def _():
        partial[...] = jnp.zeros_like(partial)

        def body(rows):
            grad = back_ref[rows, :] + total[rows, :]
            unit = unit_ref[rows, :]
            add_rows(partial, 1, grad * unit)
            add_rows(partial, 2, grad)
            back = norm_back(grad, unit, inverse_ref[rows, :], vec_ref[1:2, :])
            low = back.astype(BF16)
            out_ref[rows, :] = back
            low_ref[rows, :] = low
            add_rows(partial, 0, low.astype(F32))

        each_rows(unit_ref.shape[0], body)
        for place in range(3):
            sums_ref[place : place + 1, :] = total_of(partial[place])


def first_back(d_hidden, shards, back, unit, inverse, vec):
    rows = unit.shape[0]
    outs = [shaped((rows, D), F32), shaped((rows, D), BF16), shaped((3, D), F32)]
    return dense(
        first_back_kernel,
        [columns_of(d_hidden), whole(back), whole(unit), whole(inverse), whole(vec)],
        [whole(out) for out in outs],
        outs,
        [pltpu.VMEM((rows, D), F32), pltpu.VMEM((3, 8, D), F32)],
        2 * rows * D * d_hidden.shape[1],
        "first_back",
        shards,
    )(*[part for _, _, part in shards.parts], d_hidden, back, unit, inverse, vec)


def input_back_kernel(weight_ref, d_qkv_ref, back_ref, out_ref, leave_ref, sums_ref, total):
    add_product(d_qkv_ref, weight_ref, total, NT)
    sums_ref[...] = total_of(d_qkv_ref[...].astype(F32))

    @pl.when(pl.program_id(0) == 3)
    def _():
        half = D // 2
        out_ref[...] = back_ref[:, :half] + total[:, :half]
        leave_ref[...] = (back_ref[:, half:] + total[:, half:]).astype(BF16)


def input_back(d_qkv, shards, back):
    rows, width = d_qkv.shape
    outs = [shaped((rows, D // 2), F32), shaped((rows, D // 2), BF16), shaped((1, width), F32)]
    return dense(
        input_back_kernel,
        [columns_of(d_qkv), whole(back)],
        [whole(outs[0]), whole(outs[1]), columns_of(outs[2])],
        outs,
        [pltpu.VMEM((rows, D), F32)],
        2 * rows * D * width,
        "input_back",
        shards,
    )(*[part for _, _, part in shards.parts], d_qkv, back)


def columns_back(grad_ref, weight_ref, start, stop):
    half = D // 2
    return mm(grad_ref[:, :half], weight_ref[0, start:stop, :], NT) + mm(
        grad_ref[:, half:], weight_ref[1, start:stop, :], NT
    )


def hidden_back_kernel(weight_ref, grad_ref, slope_ref, out_ref, sums_ref):
    for start in range(0, out_ref.shape[1], 256):
        span = slice(start, start + 256)
        part = columns_back(grad_ref, weight_ref, start, start + 256)
        low = (part * slope_ref[:, span].astype(F32)).astype(BF16)
        out_ref[:, span] = low
        sums_ref[:, span] = total_of(low.astype(F32))


def hidden_back(grad, shards, slope):
    outs = [shaped(slope.shape, BF16), shaped((1, slope.shape[1]), F32)]
    return dense(
        hidden_back_kernel,
        [whole(grad), columns_of(slope)],
        [columns_of(out) for out in outs],
        outs,
        [],
        2 * grad.shape[0] * D * slope.shape[1],
        "hidden_back",
        shards,
    )(*[part for _, _, part in shards.parts], grad, slope)


def heads_back_kernel(weight_ref, grad_ref, out_ref):
    out_ref[...] = columns_back(grad_ref, weight_ref, 0, weight_ref.shape[1]).astype(BF16)


def heads_back(grad, shards):
    return dense(
        heads_back_kernel,
        [whole(grad)],
        columns_of(grad),
        shaped(grad.shape, BF16),
        [],
        2 * grad.shape[0] * D * D,
        "heads_back",
        shards,
    )(*[part for _, _, part in shards.parts], grad)


def grad_up_kernel(left_ref, right_ref, keep_ref, leave_ref, turned):
    step = pl.program_id(0)
    half = D // 2

    @pl.when(step == 0)
    def _():
        turned[...] = left_ref[...].T

    for parity, out_ref in enumerate((keep_ref, leave_ref)):

        @pl.when(step % 2 == parity)
        def _():
            for col in range(2):
                out_ref[col] = mm(turned[col * half : (col + 1) * half, :], right_ref[...], NN).astype(BF16)


def two_blocks(out):
    return pl.BlockSpec((2, *out.shape[1:]), lambda i: (i // 2, 0, 0))


def grad_up(left, right):
    out = shaped((4, D // 2, right.shape[1] // 4), BF16)
    return dense(
        grad_up_kernel,
        [whole(left), columns_of(right)],
        [two_blocks(out)] * 2,
        [out] * 2,
        [pltpu.VMEM((D, left.shape[0]), BF16)],
        2 * left.shape[0] * D * right.shape[1],
        "grad_up",
    )(left, right)


def grad_down_kernel(left_ref, right_ref, keep_ref, leave_ref):
    step = pl.program_id(0)
    half = D // 2
    for parity, out_ref in enumerate((keep_ref, leave_ref)):

        @pl.when(step % 2 == parity)
        def _():
            turned = left_ref[...].T
            for col in range(2):
                out_ref[col] = mm(turned, right_ref[:, col * half : (col + 1) * half], NN).astype(BF16)


def grad_down(left, right):
    out = shaped((4, left.shape[1] // 4, D // 2), BF16)
    return dense(
        grad_down_kernel,
        [columns_of(left), whole(right)],
        [two_blocks(out)] * 2,
        [out] * 2,
        [],
        2 * left.shape[0] * D * left.shape[1],
        "grad_down",
    )(left, right)


def sum_devices(value, axis, size):
    if size & (size - 1):
        return lax.psum(value, axis)
    step = 1
    while step < size:
        value = value + lax.ppermute(value, axis, [(i, i ^ step) for i in range(size)])
        step *= 2
    return value


def sum_dp(value, size):
    return lax.psum(value, "dp")


def reduce_grid(keep, leaving):
    other = swap_core(leaving)
    half = keep.shape[1] // 2
    own, beside, across, corner = [(keep[k], other[k]) for k in range(4)]

    def upper(pair):
        return add(pair[0][:half], pair[1][:half])

    def lower(pair):
        return add(pair[0][half:], pair[1][half:])

    from_col = swap_col(jnp.concatenate([upper(corner), upper(beside)], 0))
    from_row = swap_row(jnp.concatenate([lower(corner), lower(across)], 0))
    last_col = swap_col(add(beside[0][half:], beside[1][half:], from_row[:half]))
    last_row = swap_row(add(across[0][:half], across[1][:half], from_col[:half]))
    return jnp.concatenate(
        [
            add(own[0][:half], own[1][:half], from_col[half:], last_row),
            add(own[0][half:], own[1][half:], from_row[half:], last_col),
        ],
        0,
    )


def in_three(value):
    high = lax.reduce_precision(value, 8, 7)
    rest = value - high
    mid = lax.reduce_precision(rest, 8, 7)
    return jnp.stack([high, mid, rest - mid]).astype(BF16)


def local(
    n_dp,
    tokens,
    segments,
    qkv_weight,
    qv_bias,
    out_weight,
    out_bias,
    ln1_gain,
    ln1_bias,
    ff_in_weight,
    ff_in_bias,
    ff_out_weight,
    ff_out_bias,
    ln2_gain,
    ln2_bias,
    out_grad,
):
    row, col = lax.axis_index("row"), lax.axis_index("col")
    odd = row % 2 == 1
    member = (row % 2) * 2 + col

    def in_order(mine, other):
        return jnp.where(col == 0, mine, other), jnp.where(col == 0, other, mine)

    packed = jnp.concatenate(
        [out_bias, ln1_gain, ln1_bias, ff_out_bias, ln2_gain, ln2_bias, ff_in_bias, qv_bias.reshape(-1)]
    )
    riders = in_three(packed).reshape(15, 768)
    riders = jnp.concatenate([qkv_weight, riders, jnp.zeros((1, 768), BF16)], 0)
    x = own_rows(tokens, odd, col)
    qkv_w = Shards(riders, D // 2)
    out_w = Shards(out_weight, D // 4)
    ff_in_w = Shards(after(ff_in_weight, *qkv_w.first), D // 2)
    incoming = own_rows(after(out_grad, *qkv_w.first), odd, col)
    ff_out_w = Shards(after(ff_out_weight, *ff_in_w.first), D)

    packed = qkv_w.riders()[:, :15].astype(F32).reshape(8, 3, packed.shape[0])
    packed = (packed[:, 0] + packed[:, 1]) + packed[:, 2]
    vec = packed[:2, : 6 * 512].reshape(2, 6, 512).transpose(1, 0, 2).reshape(6, D)
    pairs = packed[:, 6 * 512 :].reshape(4, 2, 768)
    first, second = in_order(pairs[:, 0], pairs[:, 1])
    ff_in_b = jnp.concatenate([first[:, :512], second[:, :512]], 1).reshape(1, -1)
    qv_b = jnp.concatenate([first[:, 512:], second[:, 512:]], 1).reshape(-1, 2 * HD)
    hollow = jnp.zeros((qv_b.shape[0], HD), F32)
    qkv_b = jnp.concatenate([qv_b[:, :HD], hollow, qv_b[:, HD:]], 1).reshape(1, -1)

    group = (row // 2) * 5
    labels = lax.dynamic_slice_in_dim(segments, (group + (row % 2) * 3 + col) * SEQ, SEQ)
    shared = lax.dynamic_slice_in_dim(segments, (group + 2) * SEQ, SEQ)
    shared = jnp.concatenate(
        [lax.dynamic_slice_in_dim(shared, (member ^ offset) * QUARTER, QUARTER) for offset in range(4)]
    )

    qkv = project_qkv(x, qkv_w, qkv_b)
    qkv_shared = spread_heads(qkv[SEQ:], member, row)
    heads_own, probs_own = attend(qkv, labels)
    heads_shared, probs_shared = attend(qkv_shared, shared)
    heads = jnp.concatenate([heads_own, collect_heads(heads_shared, member, row)], 0)
    unit_one, inverse_one, middle_low = first_norm(heads, out_w, x, vec)
    active, slope = project_hidden(middle_low, ff_in_w, ff_in_b)
    out_mine, out_leave, back_two, d_two, sums_two = second_norm(active, ff_out_w, unit_one, incoming, vec)

    ff_out_keep, ff_out_leave = grad_down(active, d_two)
    d_two, out_leave, ff_out_leave = lax.optimization_barrier((d_two, out_leave, ff_out_leave))
    ff_out_grad = reduce_grid(ff_out_keep, ff_out_leave)
    ff_out_grad = sum_dp(ff_out_grad, n_dp)
    d_hidden, ff_in_bias_part = hidden_back(d_two, ff_out_w, slope)
    ff_in_keep, ff_in_leave = grad_up(middle_low, d_hidden)
    d_hidden, ff_in_leave = lax.optimization_barrier((d_hidden, ff_in_leave))
    ff_in_grad = reduce_grid(ff_in_keep, ff_in_leave)
    layer_out = give_back(out_mine, out_leave, odd, col)
    back_one, d_one, sums_one = first_back(d_hidden, ff_in_w, back_two, unit_one, inverse_one, vec)
    d_heads = heads_back(d_one, out_w)
    d_shared = spread_heads(d_heads[SEQ:], member, row)
    d_qkv_own = attend_back(qkv, probs_own, d_heads)
    d_qkv_shared = attend_back(qkv_shared, probs_shared, d_shared)
    d_qkv = jnp.concatenate([d_qkv_own, collect_heads(d_qkv_shared, member, row)], 0)
    qkv_keep, qkv_leave = grad_up(x, d_qkv)
    d_qkv, d_one, qkv_leave = lax.optimization_barrier((d_qkv, d_one, qkv_leave))
    qkv_grad = reduce_grid(qkv_keep, qkv_leave)
    out_keep, out_leave = grad_down(heads, d_one)
    d_qkv, out_leave = lax.optimization_barrier((d_qkv, out_leave))
    out_w_grad = reduce_grid(out_keep, out_leave)
    in_mine, in_leave, column_sums = input_back(d_qkv, qkv_w, back_one)
    input_grad = give_back(in_mine, in_leave, odd, col)

    ff_in_grad = sum_dp(after(ff_in_grad, ff_out_grad), n_dp)
    qkv_grad = sum_dp(after(qkv_grad, ff_in_grad), n_dp)
    out_w_grad = sum_dp(after(out_w_grad, qkv_grad), n_dp)

    def across_grid(value):
        return sum_devices(sum_devices(value, "row", 4), "col", 2)

    def ordered(value):
        blocks = value.reshape(4, -1)
        return jnp.stack([lax.dynamic_index_in_dim(blocks, row ^ place, 0, False) for place in range(4)])

    place = row * 2 + col
    halves = jnp.concatenate([sums_one, sums_two], 0)
    halves = jnp.concatenate(in_order(halves[:, : D // 2], halves[:, D // 2 :]), 1)
    early = across_grid(jnp.concatenate([halves.reshape(-1), ordered(ff_in_bias_part).reshape(-1)]))
    halves = lax.dynamic_slice_in_dim(early[: 6 * D].reshape(6, 2, D // 2), col, 1, 1)[:, 0]
    early = jnp.concatenate([halves.reshape(-1), lax.dynamic_slice_in_dim(early, 6 * D + place * 512, 512)])
    early = sum_devices(early, "dp", n_dp)
    column_sums = ordered(column_sums).reshape(-1, 3, HD)
    late = across_grid(jnp.concatenate([column_sums[:, 0], column_sums[:, 2]], 1).reshape(-1))
    late = sum_devices(lax.dynamic_slice_in_dim(late, place * 256, 256), "dp", n_dp)
    halves = early[: 6 * 512].reshape(6, 512)
    return (
        layer_out,
        input_grad,
        qkv_grad.astype(F32),
        late.reshape(2, 2 * HD),
        out_w_grad.astype(F32),
        halves[0],
        halves[1],
        halves[2],
        ff_in_grad.astype(F32),
        early[6 * 512 :],
        ff_out_grad.astype(F32),
        halves[3],
        halves[4],
        halves[5],
    )


def solution(mesh):
    in_specs = (
        P(("dp", "row"), "col"),
        P("dp"),
        P("col", "row"),
        P(("row", "col"), None),
        P("row", "col"),
        P("col"),
        P("col"),
        P("col"),
        P("col", "row"),
        P(("row", "col")),
        P("row", "col"),
        P("col"),
        P("col"),
        P("col"),
        P(("dp", "row"), "col"),
    )
    out_specs = (
        P(("dp", "row"), "col"),
        P(("dp", "row"), "col"),
        P("col", "row"),
        P(("row", "col"), None),
        P("row", "col"),
        P("col"),
        P("col"),
        P("col"),
        P("col", "row"),
        P(("row", "col")),
        P("row", "col"),
        P("col"),
        P("col"),
        P("col"),
    )
    step = functools.partial(local, mesh.shape["dp"])
    return jax.shard_map(step, mesh=mesh, in_specs=in_specs, out_specs=out_specs, check_vma=False)
```

```python
import functools
import math

import jax
import jax.numpy as jnp
from jax import lax
from jax.experimental import pallas as pl
from jax.experimental.pallas import tpu as pltpu
from jax.sharding import PartitionSpec as P

D = 1024
HD = 64
SEQ = 512
QUARTER = SEQ // 4
GRID = ("row", "col")

EPSILON = 1e-06
NEGATIVE = -1e30
F32 = jnp.float32
BF16 = jnp.bfloat16
NN = (((1,), (0,)), ((), ()))
NT = (((1,), (1,)), ((), ()))
TN = (((0,), (0,)), ((), ()))
MIB = 1 << 20


LIGHT = ("project_hidden", "first_back", "heads_back")


def cost_of(name):
    scale = 1e-6 if name in LIGHT else 1
    return pl.CostEstimate(flops=int(1e13 * scale), bytes_accessed=int(1e9 * scale), transcendentals=0)


def mm(left, right, contract):
    return lax.dot_general(left, right, contract, preferred_element_type=F32)


def attend_kernel(qkv_ref, column_ref, line_ref, heads_ref, probs_ref, mask):
    @pl.when(pl.program_id(0) == 0)
    def _():
        mask[...] = jnp.where(column_ref[...] == line_ref[...], 0.0, NEGATIVE)

    mixed = []
    for head in range(2):
        base = head * 3 * HD
        query = qkv_ref[:, base : base + HD] * jnp.asarray(1 / math.sqrt(HD), BF16)
        key = qkv_ref[:, base + HD : base + 2 * HD]
        value = qkv_ref[:, base + 2 * HD : base + 3 * HD]
        scores = mm(key, query, NT) + mask[...]
        powers = jnp.exp(scores - jnp.max(scores, 0, keepdims=True))
        total = jnp.sum(powers, 0, keepdims=True)
        probs = (powers * (1.0 / total)).astype(BF16)
        probs_ref[head] = probs
        mixed.append(mm(value, probs, TN))
    heads_ref[...] = jnp.concatenate(mixed, 0).T.astype(BF16)


def attend(qkv, labels):
    pairs = qkv.shape[1] // (6 * HD)
    return pl.pallas_call(
        attend_kernel,
        grid=(pairs,),
        in_specs=[
            pl.BlockSpec((SEQ, 6 * HD), lambda i: (0, i)),
            pl.BlockSpec((SEQ, 1), lambda i: (0, 0)),
            pl.BlockSpec((1, SEQ), lambda i: (0, 0)),
        ],
        out_specs=[
            pl.BlockSpec((SEQ, 2 * HD), lambda i: (0, i)),
            pl.BlockSpec((2, SEQ, SEQ), lambda i: (i, 0, 0)),
        ],
        out_shape=[
            jax.ShapeDtypeStruct((SEQ, pairs * 2 * HD), BF16),
            jax.ShapeDtypeStruct((pairs * 2, SEQ, SEQ), BF16),
        ],
        scratch_shapes=[pltpu.VMEM((SEQ, SEQ), F32)],
        compiler_params=pltpu.CompilerParams(vmem_limit_bytes=32 * MIB),
        cost_estimate=cost_of("attend"),
        name="attend",
    )(qkv, labels[:, None], labels[None, :])


def attend_back_kernel(qkv_ref, probs_ref, grad_ref, out_ref):
    for head in range(2):
        base = head * 3 * HD
        scale = jnp.asarray(1 / math.sqrt(HD), BF16)
        query = qkv_ref[:, base : base + HD] * scale
        key = qkv_ref[:, base + HD : base + 2 * HD] * scale
        value = qkv_ref[:, base + 2 * HD : base + 3 * HD]
        grad = grad_ref[:, head * HD : (head + 1) * HD]
        probs = probs_ref[head]
        d_value = mm(probs, grad, NN)
        d_probs = mm(value, grad, NT)
        wide = probs.astype(F32)
        delta = jnp.sum(wide * d_probs, 0, keepdims=True)
        d_scores = (wide * (d_probs - delta)).astype(BF16)
        d_key = mm(d_scores, query, NN)
        d_query = mm(key, d_scores, TN).T
        out_ref[:, base : base + HD] = d_query.astype(BF16)
        out_ref[:, base + HD : base + 2 * HD] = d_key.astype(BF16)
        out_ref[:, base + 2 * HD : base + 3 * HD] = d_value.astype(BF16)


def attend_back(qkv, probs, grad):
    pairs = qkv.shape[1] // (6 * HD)
    return pl.pallas_call(
        attend_back_kernel,
        grid=(pairs,),
        in_specs=[
            pl.BlockSpec((SEQ, 6 * HD), lambda i: (0, i)),
            pl.BlockSpec((2, SEQ, SEQ), lambda i: (i, 0, 0)),
            pl.BlockSpec((SEQ, 2 * HD), lambda i: (0, i)),
        ],
        out_specs=pl.BlockSpec((SEQ, 6 * HD), lambda i: (0, i)),
        out_shape=jax.ShapeDtypeStruct((SEQ, qkv.shape[1]), BF16),
        compiler_params=pltpu.CompilerParams(vmem_limit_bytes=32 * MIB),
        cost_estimate=cost_of("attend_back"),
        name="attend_back",
    )(qkv, probs, grad)


def swap_core(value):
    return lax.ppermute(value, "row", [(i, i ^ 1) for i in range(4)])


def swap_row(value):
    return lax.ppermute(value, "row", [(i, i ^ 2) for i in range(4)])


def swap_col(value):
    return lax.ppermute(value, "col", [(0, 1), (1, 0)])


def after(value, *others):
    return lax.optimization_barrier((value, *others))[0]


def after_all(values, *others):
    return lax.optimization_barrier((*values, *others))[: len(values)]


def add(*values):
    total = values[0].astype(F32)
    for value in values[1:]:
        total = total + value.astype(F32)
    return total.astype(BF16)


def own_rows(value, odd, col):
    rolled = jnp.where(odd, jnp.roll(value, -2 * QUARTER, 0), value)
    first = jnp.concatenate([rolled[:SEQ], rolled[2 * SEQ : 2 * SEQ + QUARTER]], 0)
    second = jnp.concatenate([rolled[SEQ : 2 * SEQ], rolled[2 * SEQ + QUARTER :]], 0)
    mine = jnp.where(col == 0, first, second)
    return jnp.concatenate([mine, swap_col(jnp.where(col == 0, second, first))], 1)


def give_back(mine, leaving, odd, col, *ties):
    other = after(swap_col(leaving), *ties).astype(F32)
    first = jnp.where(col == 0, mine, other)
    second = jnp.where(col == 0, other, mine)
    rolled = jnp.concatenate([first[:SEQ], second[:SEQ], first[SEQ:], second[SEQ:]], 0)
    return jnp.where(odd, jnp.roll(rolled, 2 * QUARTER, 0), rolled)


def swap(offset):
    return [(i, i ^ offset) for i in range(8)]


def spread_heads(value, member, row):
    width = value.shape[1] // 4
    pieces = []
    for offset in range(4):
        piece = lax.dynamic_slice_in_dim(value, ((member ^ offset) ^ row) * width, width, 1)
        pieces.append(piece if offset == 0 else lax.ppermute(piece, GRID, swap(offset)))
    return jnp.concatenate(pieces, 0)


def send_heads(value):
    pieces = [value[offset * QUARTER : (offset + 1) * QUARTER] for offset in range(4)]
    return [piece if offset == 0 else lax.ppermute(piece, GRID, swap(offset)) for offset, piece in enumerate(pieces)]


def join_heads(pieces, member, row):
    width = pieces[0].shape[1]
    whole = jnp.zeros((QUARTER, 4 * width), pieces[0].dtype)
    for offset, piece in enumerate(pieces):
        whole = lax.dynamic_update_slice_in_dim(whole, piece, ((member ^ offset) ^ row) * width, 1)
    return whole


class Shards:
    def __init__(self, depth, shard, beside, across, *corners):
        self.depth, self.width = depth, shard.shape[1]
        near = [(0, 0, shard), (1, 0, beside), (4, 0, across)]
        near += [(5, index * depth // 2, corner) for index, corner in enumerate(corners)]
        far = [(place + 2, start, swap_core(part)) for place, start, part in near]
        self.parts = near + far

    def riders(self):
        found = {}
        for place, start, part in self.parts:
            if start + part.shape[0] > self.depth:
                found[place] = part[self.depth - start :]
        return jnp.stack([found[place] for place in range(8)])


def dense(kernel, in_specs, out_specs, out_shape, scratch, flops, name, shards=None):
    if shards is None:
        body, extra_specs, extra_scratch = kernel, [], []
    else:
        places = [(place, start, min(part.shape[0], shards.depth - start)) for place, start, part in shards.parts]
        count = len(places)
        extra_specs = [pl.BlockSpec(memory_space=pl.ANY)] * count
        extra_scratch = [
            pltpu.VMEM((8, shards.depth, shards.width), BF16),
            pltpu.SemaphoreType.DMA((count,)),
        ]

        def body(*refs):
            step = pl.program_id(0)
            held, done = refs[-2:]
            copies = [
                pltpu.make_async_copy(
                    refs[k].at[pl.ds(0, rows)], held.at[place, pl.ds(start, rows)], done.at[k]
                )
                for k, (place, start, rows) in enumerate(places)
            ]
            for block in range(4):

                @pl.when(step == 0)
                def _():
                    for copy, (place, _, _) in zip(copies, places):
                        if place // 2 == block:
                            copy.start()

            for block in range(4):

                @pl.when(step == block)
                def _():
                    for copy, (place, _, _) in zip(copies, places):
                        if place // 2 == block:
                            copy.wait()

            kernel(held.at[pl.ds(2 * step, 2)], *refs[count:-2])

    return pl.pallas_call(
        body,
        grid=(4,),
        in_specs=extra_specs + in_specs,
        out_specs=out_specs,
        out_shape=out_shape,
        scratch_shapes=scratch + extra_scratch,
        compiler_params=pltpu.CompilerParams(vmem_limit_bytes=48 * MIB),
        cost_estimate=cost_of(name),
        name=name,
    )


def whole(value):
    return pl.BlockSpec(value.shape, lambda i: (0,) * value.ndim)


def columns_of(value, parts=4):
    return pl.BlockSpec((value.shape[0], value.shape[1] // parts), lambda i: (0, i))


def shaped(shape, kind):
    return jax.ShapeDtypeStruct(shape, kind)


def halves_times(left_ref, weight_ref, start, width):
    half = left_ref.shape[1] // 2
    stop = start + width
    return mm(left_ref[:, :half], weight_ref[0, :, start:stop], NN) + mm(
        left_ref[:, half:], weight_ref[1, :, start:stop], NN
    )


def qkv_kernel(weight_ref, x_ref, bias_ref, out_ref):
    for start in range(0, out_ref.shape[1], 256):
        part = halves_times(x_ref, weight_ref, start, 256)
        out_ref[:, start : start + 256] = (part + bias_ref[:, start : start + 256]).astype(BF16)


def project_qkv(x, shards, bias):
    width = 4 * shards.width
    return dense(
        qkv_kernel,
        [whole(x), columns_of(bias)],
        pl.BlockSpec((x.shape[0], width // 4), lambda i: (0, i)),
        shaped((x.shape[0], width), BF16),
        [],
        2 * x.shape[0] * D * width,
        "project_qkv",
        shards,
    )(*[part for _, _, part in shards.parts], x, bias)


def hidden_kernel(weight_ref, x_ref, bias_ref, active_ref, slope_ref):
    for start in range(0, active_ref.shape[1], 256):
        stop = start + 256
        hidden = halves_times(x_ref, weight_ref, start, 256) + bias_ref[:, start:stop]
        share = 0.5 * (1.0 + lax.erf(hidden * math.sqrt(0.5)))
        bell = jnp.exp(hidden * hidden * -0.5) * (1 / math.sqrt(2 * math.pi))
        active_ref[:, start:stop] = (hidden * share).astype(BF16)
        slope_ref[:, start:stop] = (share + hidden * bell).astype(BF16)


def project_hidden(x, shards, bias):
    width = 4 * shards.width
    block = pl.BlockSpec((x.shape[0], width // 4), lambda i: (0, i))
    return dense(
        hidden_kernel,
        [whole(x), columns_of(bias)],
        [block, block],
        [shaped((x.shape[0], width), BF16)] * 2,
        [],
        4 * x.shape[0] * D * width,
        "project_hidden",
        shards,
    )(*[part for _, _, part in shards.parts], x, bias)


def add_product(left_ref, weight_ref, total, contract):
    step = pl.program_id(0)
    half = D // 2
    for col in range(2):
        part = mm(left_ref[...], weight_ref[col], contract)
        span = slice(col * half, (col + 1) * half)

        @pl.when(step == 0)
        def _():
            total[:, span] = part

        @pl.when(step > 0)
        def _():
            total[:, span] += part


ROWS = 16


def each_rows(count, body):
    @pl.loop(0, count // (2 * ROWS))
    def _(step):
        for part in range(2):
            body(pl.ds(pl.multiple_of((2 * step + part) * ROWS, ROWS), ROWS))


def add_rows(partial, place, value):
    partial[place] += value[:8] + value[8:]


def norm_parts(value):
    center = jnp.sum(value, 1, keepdims=True) * (1 / D)
    squares = jnp.sum(value * value, 1, keepdims=True) * (1 / D)
    inverse = lax.rsqrt(squares - center * center + EPSILON)
    return ((value - center) * inverse, inverse)


def norm_back(grad, unit, inverse, gain):
    scaled = grad * gain
    mean = jnp.sum(scaled, 1, keepdims=True) * (1 / D)
    paired = jnp.sum(scaled * unit, 1, keepdims=True) * (1 / D)
    return inverse * (scaled - mean - unit * paired)


def total_of(value):
    return jnp.sum(value, 0, keepdims=True)


def first_norm_kernel(weight_ref, heads_ref, x_ref, vec_ref, unit_ref, inverse_ref, low_ref, total):
    add_product(heads_ref, weight_ref, total, NN)

    @pl.when(pl.program_id(0) == 3)
    def _():
        def body(rows):
            value = x_ref[rows, :].astype(F32) + (total[rows, :] + vec_ref[0:1, :])
            unit, inverse = norm_parts(value)
            unit_ref[rows, :] = unit
            inverse_ref[rows, :] = inverse
            low_ref[rows, :] = (unit * vec_ref[1:2, :] + vec_ref[2:3, :]).astype(BF16)

        each_rows(x_ref.shape[0], body)


def first_norm(heads, shards, x, vec):
    rows = x.shape[0]
    outs = [shaped((rows, D), F32), shaped((rows, 1), F32), shaped((rows, D), BF16)]
    return dense(
        first_norm_kernel,
        [columns_of(heads), whole(x), whole(vec)],
        [whole(out) for out in outs],
        outs,
        [pltpu.VMEM((rows, D), F32)],
        2 * rows * D * D,
        "first_norm",
        shards,
    )(*[part for _, _, part in shards.parts], heads, x, vec)


def second_norm_kernel(
    weight_ref, active_ref, unit_ref, incoming_ref, vec_ref, out_ref, leave_ref, back_ref, low_ref, sums_ref, total, partial
):
    add_product(active_ref, weight_ref, total, NN)

    @pl.when(pl.program_id(0) == 3)
    def _():
        partial[...] = jnp.zeros_like(partial)
        half = D // 2

        def body(rows):
            middle = unit_ref[rows, :] * vec_ref[1:2, :] + vec_ref[2:3, :]
            unit, inverse = norm_parts(middle + (total[rows, :] + vec_ref[3:4, :]))
            out = unit * vec_ref[4:5, :] + vec_ref[5:6, :]
            out_ref[rows, :] = out[:, :half]
            leave_ref[rows, :] = out[:, half:].astype(BF16)
            grad = incoming_ref[rows, :].astype(F32)
            add_rows(partial, 1, grad * unit)
            add_rows(partial, 2, grad)
            back = norm_back(grad, unit, inverse, vec_ref[4:5, :])
            low = back.astype(BF16)
            back_ref[rows, :] = back
            low_ref[rows, :] = low
            add_rows(partial, 0, low.astype(F32))

        each_rows(unit_ref.shape[0], body)
        for place in range(3):
            sums_ref[place : place + 1, :] = total_of(partial[place])


def second_norm(active, shards, unit, incoming, vec):
    rows = unit.shape[0]
    outs = [
        shaped((rows, D // 2), F32),
        shaped((rows, D // 2), BF16),
        shaped((rows, D), F32),
        shaped((rows, D), BF16),
        shaped((3, D), F32),
    ]
    return dense(
        second_norm_kernel,
        [columns_of(active), whole(unit), whole(incoming), whole(vec)],
        [whole(out) for out in outs],
        outs,
        [pltpu.VMEM((rows, D), F32), pltpu.VMEM((3, 8, D), F32)],
        2 * rows * D * active.shape[1],
        "second_norm",
        shards,
    )(*[part for _, _, part in shards.parts], active, unit, incoming, vec)


def first_back_kernel(
    weight_ref, d_hidden_ref, back_ref, unit_ref, inverse_ref, vec_ref, out_ref, low_ref, sums_ref, total, partial
):
    add_product(d_hidden_ref, weight_ref, total, NT)

    @pl.when(pl.program_id(0) == 3)
    def _():
        partial[...] = jnp.zeros_like(partial)

        def body(rows):
            grad = back_ref[rows, :] + total[rows, :]
            unit = unit_ref[rows, :]
            add_rows(partial, 1, grad * unit)
            add_rows(partial, 2, grad)
            back = norm_back(grad, unit, inverse_ref[rows, :], vec_ref[1:2, :])
            low = back.astype(BF16)
            out_ref[rows, :] = back
            low_ref[rows, :] = low
            add_rows(partial, 0, low.astype(F32))

        each_rows(unit_ref.shape[0], body)
        for place in range(3):
            sums_ref[place : place + 1, :] = total_of(partial[place])


def first_back(d_hidden, shards, back, unit, inverse, vec):
    rows = unit.shape[0]
    outs = [shaped((rows, D), F32), shaped((rows, D), BF16), shaped((3, D), F32)]
    return dense(
        first_back_kernel,
        [columns_of(d_hidden), whole(back), whole(unit), whole(inverse), whole(vec)],
        [whole(out) for out in outs],
        outs,
        [pltpu.VMEM((rows, D), F32), pltpu.VMEM((3, 8, D), F32)],
        2 * rows * D * d_hidden.shape[1],
        "first_back",
        shards,
    )(*[part for _, _, part in shards.parts], d_hidden, back, unit, inverse, vec)


def input_back_kernel(weight_ref, d_qkv_ref, back_ref, out_ref, leave_ref, sums_ref, total):
    add_product(d_qkv_ref, weight_ref, total, NT)
    sums_ref[...] = total_of(d_qkv_ref[...].astype(F32))

    @pl.when(pl.program_id(0) == 3)
    def _():
        half = D // 2
        out_ref[...] = back_ref[:, :half] + total[:, :half]
        leave_ref[...] = (back_ref[:, half:] + total[:, half:]).astype(BF16)


def input_back(d_qkv, shards, back):
    rows, width = d_qkv.shape
    outs = [shaped((rows, D // 2), F32), shaped((rows, D // 2), BF16), shaped((1, width), F32)]
    return dense(
        input_back_kernel,
        [columns_of(d_qkv), whole(back)],
        [whole(outs[0]), whole(outs[1]), columns_of(outs[2])],
        outs,
        [pltpu.VMEM((rows, D), F32)],
        2 * rows * D * width,
        "input_back",
        shards,
    )(*[part for _, _, part in shards.parts], d_qkv, back)


def columns_back(grad_ref, weight_ref, start, stop):
    half = D // 2
    return mm(grad_ref[:, :half], weight_ref[0, start:stop, :], NT) + mm(
        grad_ref[:, half:], weight_ref[1, start:stop, :], NT
    )


def hidden_back_kernel(weight_ref, grad_ref, slope_ref, out_ref, sums_ref):
    for start in range(0, out_ref.shape[1], 256):
        span = slice(start, start + 256)
        part = columns_back(grad_ref, weight_ref, start, start + 256)
        low = (part * slope_ref[:, span].astype(F32)).astype(BF16)
        out_ref[:, span] = low
        sums_ref[:, span] = total_of(low.astype(F32))


def hidden_back(grad, shards, slope):
    outs = [shaped(slope.shape, BF16), shaped((1, slope.shape[1]), F32)]
    return dense(
        hidden_back_kernel,
        [whole(grad), columns_of(slope)],
        [columns_of(out) for out in outs],
        outs,
        [],
        2 * grad.shape[0] * D * slope.shape[1],
        "hidden_back",
        shards,
    )(*[part for _, _, part in shards.parts], grad, slope)


def heads_back_kernel(weight_ref, grad_ref, out_ref):
    out_ref[...] = columns_back(grad_ref, weight_ref, 0, weight_ref.shape[1]).astype(BF16)


def heads_back(grad, shards):
    return dense(
        heads_back_kernel,
        [whole(grad)],
        columns_of(grad),
        shaped(grad.shape, BF16),
        [],
        2 * grad.shape[0] * D * D,
        "heads_back",
        shards,
    )(*[part for _, _, part in shards.parts], grad)


def grad_up_kernel(left_ref, right_ref, keep_ref, leave_ref, turned):
    step = pl.program_id(0)
    half = D // 2

    @pl.when(step == 0)
    def _():
        turned[...] = left_ref[...].T

    for parity, out_ref in enumerate((keep_ref, leave_ref)):

        @pl.when(step % 2 == parity)
        def _():
            for col in range(2):
                out_ref[col] = mm(turned[col * half : (col + 1) * half, :], right_ref[...], NN).astype(BF16)


def two_blocks(out):
    return pl.BlockSpec((2, *out.shape[1:]), lambda i: (i // 2, 0, 0))


def grad_up(left, right):
    out = shaped((4, D // 2, right.shape[1] // 4), BF16)
    return dense(
        grad_up_kernel,
        [whole(left), columns_of(right)],
        [two_blocks(out)] * 2,
        [out] * 2,
        [pltpu.VMEM((D, left.shape[0]), BF16)],
        2 * left.shape[0] * D * right.shape[1],
        "grad_up",
    )(left, right)


def grad_down_kernel(left_ref, right_ref, keep_ref, leave_ref):
    step = pl.program_id(0)
    half = D // 2
    for parity, out_ref in enumerate((keep_ref, leave_ref)):

        @pl.when(step % 2 == parity)
        def _():
            turned = left_ref[...].T
            for col in range(2):
                out_ref[col] = mm(turned, right_ref[:, col * half : (col + 1) * half], NN).astype(BF16)


def grad_down(left, right):
    out = shaped((4, left.shape[1] // 4, D // 2), BF16)
    return dense(
        grad_down_kernel,
        [columns_of(left), whole(right)],
        [two_blocks(out)] * 2,
        [out] * 2,
        [],
        2 * left.shape[0] * D * left.shape[1],
        "grad_down",
    )(left, right)


def sum_devices(value, axis, size):
    if size & (size - 1):
        return lax.psum(value, axis)
    step = 1
    while step < size:
        value = value + lax.ppermute(value, axis, [(i, i ^ step) for i in range(size)])
        step *= 2
    return value


class PairSum:
    def __init__(self, value, size):
        self.whole = None
        if size & (size - 1):
            self.whole = lax.psum(value, "dp")
        self.value, self.other = value, None
        place = lax.axis_index("dp")
        levels = [1 << k for k in range(size.bit_length() - 1)]
        pairs = [([(i, i ^ step) for i in range(size)], (place // step) % 2 == 1) for step in levels]
        self.plan = [(True, *pair) for pair in pairs] + [(False, *pair) for pair in reversed(pairs)]
        self.upper = self.down = None
        if self.whole is not None:
            self.plan = []

    def step(self, last):
        self.take(last)
        if not self.plan:
            return self.value
        self.down, pairs, self.upper = self.plan.pop(0)
        if self.down:
            half = self.value.shape[0] // 2
            top, bottom = self.value[:half], self.value[half:]
            self.value = jnp.where(self.upper, bottom, top)
            leaving = jnp.where(self.upper, top, bottom)
        else:
            leaving = self.value
        leaving = after(leaving, last)
        self.other = lax.ppermute(leaving, "dp", pairs)
        return leaving

    def take(self, last):
        if self.other is None:
            return
        other = after(self.other, last)
        if self.down:
            self.value = add(self.value, other)
        else:
            parts = jnp.where(self.upper, other, self.value), jnp.where(self.upper, self.value, other)
            self.value = jnp.concatenate(parts, 0)
        self.other = None

    def result(self):
        return self.value if self.whole is None else self.whole


class GridSum:
    def __init__(self, keep, leaving):
        self.keep, self.other = keep, swap_core(leaving)
        self.half = keep.shape[1] // 2
        self.kernel = leaving

    def upper(self, place, *more):
        return add(self.keep[place, : self.half], self.other[place, : self.half], *more)

    def lower(self, place, *more):
        return add(self.keep[place, self.half :], self.other[place, self.half :], *more)

    def send(self, *ties):
        if ties:
            self.other = after(self.other, *ties)
        col = jnp.concatenate([self.upper(3), self.upper(1)], 0)
        row = jnp.concatenate([self.lower(3), self.lower(2)], 0)
        self.sent = lax.optimization_barrier((col, row))
        self.from_col, self.from_row = swap_col(self.sent[0]), swap_row(self.sent[1])
        return self.sent

    def send_last(self, *ties):
        if ties:
            self.from_row, self.from_col = lax.optimization_barrier((self.from_row, self.from_col, *ties))[:2]
        col = self.lower(1, self.from_row[: self.half])
        row = self.upper(2, self.from_col[: self.half])
        self.last = lax.optimization_barrier((col, row))
        self.last_col, self.last_row = swap_col(self.last[0]), swap_row(self.last[1])
        return self.last

    def result(self, *ties):
        from_col, last_row = self.from_col, self.last_row
        if ties:
            from_col, last_row = lax.optimization_barrier((from_col, last_row, *ties))[:2]
        upper = self.upper(0, from_col[self.half :], last_row)
        return jnp.concatenate([upper, self.lower(0, self.from_row[self.half :], self.last_col)], 0)


def in_three(value):
    high = lax.reduce_precision(value, 8, 7)
    rest = value - high
    mid = lax.reduce_precision(rest, 8, 7)
    return jnp.stack([high, mid, rest - mid]).astype(BF16)


def local(
    n_dp,
    tokens,
    segments,
    qkv_weight,
    qv_bias,
    out_weight,
    out_bias,
    ln1_gain,
    ln1_bias,
    ff_in_weight,
    ff_in_bias,
    ff_out_weight,
    ff_out_bias,
    ln2_gain,
    ln2_bias,
    out_grad,
):
    row, col = lax.axis_index("row"), lax.axis_index("col")
    odd = row % 2 == 1
    member = (row % 2) * 2 + col

    def in_order(mine, other):
        return jnp.where(col == 0, mine, other), jnp.where(col == 0, other, mine)

    packed = jnp.concatenate(
        [out_bias, ln1_gain, ln1_bias, ff_out_bias, ln2_gain, ln2_bias, ff_in_bias, qv_bias.reshape(-1)]
    )
    riders = in_three(packed).reshape(15, 768)
    riders = jnp.concatenate([qkv_weight, riders, jnp.zeros((1, 768), BF16)], 0)
    qkv_beside, qkv_across = swap_col(riders), swap_row(riders)
    x = own_rows(after(tokens, qkv_beside), odd, col)
    qkv_corner = swap_row(qkv_beside)
    qkv_w = Shards(D // 2, riders, qkv_beside, qkv_across, qkv_corner)
    out_beside = swap_col(after(out_weight, x))
    out_across = swap_row(after(out_weight, qkv_corner))
    incoming = own_rows(after(out_grad, out_beside), odd, col)
    ff_in_across = swap_row(after(ff_in_weight, out_across))

    packed = qkv_w.riders()[:, :15].astype(F32).reshape(8, 3, packed.shape[0])
    packed = (packed[:, 0] + packed[:, 1]) + packed[:, 2]
    vec = packed[:2, : 6 * 512].reshape(2, 6, 512).transpose(1, 0, 2).reshape(6, D)
    pairs = packed[:, 6 * 512 :].reshape(4, 2, 768)
    first, second = in_order(pairs[:, 0], pairs[:, 1])
    ff_in_b = jnp.concatenate([first[:, :512], second[:, :512]], 1).reshape(1, -1)
    qv_b = jnp.concatenate([first[:, 512:], second[:, 512:]], 1).reshape(-1, 2 * HD)
    hollow = jnp.zeros((qv_b.shape[0], HD), F32)
    qkv_b = jnp.concatenate([qv_b[:, :HD], hollow, qv_b[:, HD:]], 1).reshape(1, -1)

    group = (row // 2) * 5
    labels = lax.dynamic_slice_in_dim(segments, (group + (row % 2) * 3 + col) * SEQ, SEQ)
    shared = lax.dynamic_slice_in_dim(segments, (group + 2) * SEQ, SEQ)
    shared = jnp.concatenate(
        [lax.dynamic_slice_in_dim(shared, (member ^ offset) * QUARTER, QUARTER) for offset in range(4)]
    )

    qkv = project_qkv(x, qkv_w, qkv_b)
    qkv_shared = spread_heads(qkv[SEQ:], member, row)
    heads_shared, probs_shared = attend(after(qkv_shared, incoming), shared)
    pieces = send_heads(heads_shared)
    ff_in_beside = swap_col(after(ff_in_weight, heads_shared))
    half = out_weight.shape[0] // 2
    out_corners = swap_col(out_across[:half]), swap_row(out_beside[half:])
    out_w = Shards(D // 4, out_weight, out_beside, out_across, *out_corners)
    heads_own, probs_own = attend(after(qkv, heads_shared, *[part for _, _, part in out_w.parts]), labels)
    pieces = after_all(pieces, heads_own)
    heads = jnp.concatenate([heads_own, join_heads(pieces, member, row)], 0)
    ff_in_beside, ff_in_across, ff_out_weight = after_all((ff_in_beside, ff_in_across, ff_out_weight), heads)
    half = ff_in_weight.shape[0] // 2
    ff_in_corners = swap_col(ff_in_across[:half]), swap_row(ff_in_beside[half:])
    ff_in_w = Shards(D // 2, ff_in_weight, ff_in_beside, ff_in_across, *ff_in_corners)
    ff_out_beside, ff_out_across = swap_col(ff_out_weight), swap_row(ff_out_weight)
    unit_one, inverse_one, middle_low = first_norm(after(heads, ff_in_beside, ff_in_across), out_w, x, vec)
    active, slope = project_hidden(middle_low, ff_in_w, ff_in_b)
    ff_out_beside, ff_out_across = after_all((ff_out_beside, ff_out_across), active)
    half = ff_out_weight.shape[0] // 2
    ff_out_corners = swap_col(ff_out_across[:half]), swap_row(ff_out_beside[half:])
    ff_out_w = Shards(D, ff_out_weight, ff_out_beside, ff_out_across, *ff_out_corners)
    out_mine, out_leave, back_two, d_two, sums_two = second_norm(active, ff_out_w, unit_one, incoming, vec)

    ff_out = GridSum(*grad_down(active, d_two))
    d_hidden, ff_in_bias_part = hidden_back(after(d_two, ff_out.kernel), ff_out_w, slope)
    layer_out = give_back(out_mine, out_leave, odd, col, d_hidden)
    ff_out.send(d_hidden, layer_out)
    ff_in = GridSum(*grad_up(after(middle_low, *ff_out.sent), d_hidden))
    back_one, d_one, sums_one = first_back(
        after(d_hidden, ff_in.kernel), ff_in_w, back_two, unit_one, inverse_one, vec
    )
    d_heads = heads_back(d_one, out_w)
    d_shared = spread_heads(d_heads[SEQ:], member, row)
    ff_out.send_last(d_heads)
    d_qkv_shared = attend_back(qkv_shared, probs_shared, after(d_shared, *ff_out.last))
    pieces = send_heads(d_qkv_shared)
    ff_in.send(d_qkv_shared)
    d_qkv_own = attend_back(qkv, probs_own, after(d_heads, *ff_in.sent))
    d_qkv = jnp.concatenate([d_qkv_own, join_heads(after_all(pieces, d_qkv_own), member, row)], 0)
    qkv_sum = GridSum(*grad_up(x, d_qkv))
    ff_out_pairs = PairSum(ff_out.result(qkv_sum.kernel), n_dp)
    event = ff_out_pairs.step(qkv_sum.kernel)
    ff_in.send_last(event)
    out_sum = GridSum(*grad_down(heads, after(d_one, *ff_in.last)))
    event = ff_out_pairs.step(out_sum.kernel)
    qkv_sum.send(event)
    in_mine, in_leave, column_sums = input_back(after(d_qkv, *qkv_sum.sent), qkv_w, back_one)
    ff_in_pairs = PairSum(ff_in.result(in_leave), n_dp)
    event = ff_in_pairs.step(in_leave)
    event = ff_out_pairs.step(event)
    out_sum.send(event)
    qkv_sum.send_last(*out_sum.sent)
    event = ff_in_pairs.step(qkv_sum.last[0])
    event = ff_out_pairs.step(event)
    out_sum.send_last(event)
    input_grad = give_back(*after_all((in_mine, in_leave), *out_sum.last), odd, col)
    event = ff_in_pairs.step(out_sum.last[0])
    event = ff_out_pairs.step(event)
    qkv_pairs = PairSum(qkv_sum.result(event), n_dp)
    event = qkv_pairs.step(event)
    out_pairs = PairSum(out_sum.result(event), n_dp)
    sums_start = event = out_pairs.step(event)
    every = [ff_out_pairs, ff_in_pairs, qkv_pairs, out_pairs]
    while any(pairs.plan for pairs in every):
        for pairs in every:
            event = pairs.step(event)
    for pairs in every:
        pairs.take(event)
    ff_out_grad, ff_in_grad, qkv_grad, out_w_grad = [pairs.result() for pairs in every]

    def across_grid(value):
        return sum_devices(sum_devices(value, "row", 4), "col", 2)

    def ordered(value):
        blocks = value.reshape(4, -1)
        return jnp.stack([lax.dynamic_index_in_dim(blocks, row ^ place, 0, False) for place in range(4)])

    place = row * 2 + col
    halves = jnp.concatenate([sums_one, sums_two], 0)
    halves = jnp.concatenate(in_order(halves[:, : D // 2], halves[:, D // 2 :]), 1)
    column_sums = ordered(column_sums).reshape(-1, 3, HD)
    early = jnp.concatenate(
        [
            halves.reshape(-1),
            ordered(ff_in_bias_part).reshape(-1),
            jnp.concatenate([column_sums[:, 0], column_sums[:, 2]], 1).reshape(-1),
        ]
    )
    early = across_grid(after(early, sums_start))
    halves = lax.dynamic_slice_in_dim(early[: 6 * D].reshape(6, 2, D // 2), col, 1, 1)[:, 0]
    early = jnp.concatenate(
        [
            halves.reshape(-1),
            lax.dynamic_slice_in_dim(early, 6 * D + place * 512, 512),
            lax.dynamic_slice_in_dim(early, 10 * D + place * 256, 256),
        ]
    )
    early = sum_devices(early, "dp", n_dp)
    halves = early[: 6 * 512].reshape(6, 512)
    return (
        layer_out,
        input_grad,
        qkv_grad.astype(F32),
        early[7 * 512 :].reshape(2, 2 * HD),
        out_w_grad.astype(F32),
        halves[0],
        halves[1],
        halves[2],
        ff_in_grad.astype(F32),
        early[6 * 512 : 7 * 512],
        ff_out_grad.astype(F32),
        halves[3],
        halves[4],
        halves[5],
    )


def solution(mesh):
    in_specs = (
        P(("dp", "row"), "col"),
        P("dp"),
        P("col", "row"),
        P(("row", "col"), None),
        P("row", "col"),
        P("col"),
        P("col"),
        P("col"),
        P("col", "row"),
        P(("row", "col")),
        P("row", "col"),
        P("col"),
        P("col"),
        P("col"),
        P(("dp", "row"), "col"),
    )
    out_specs = (
        P(("dp", "row"), "col"),
        P(("dp", "row"), "col"),
        P("col", "row"),
        P(("row", "col"), None),
        P("row", "col"),
        P("col"),
        P("col"),
        P("col"),
        P("col", "row"),
        P(("row", "col")),
        P("row", "col"),
        P("col"),
        P("col"),
        P("col"),
    )
    step = functools.partial(local, mesh.shape["dp"])
    return jax.shard_map(step, mesh=mesh, in_specs=in_specs, out_specs=out_specs, check_vma=False)
```

```python
import functools
import math

import jax
import jax.numpy as jnp
from jax import lax
from jax.experimental import pallas as pl
from jax.experimental.pallas import tpu as pltpu
from jax.sharding import PartitionSpec as P

D = 1024
HD = 64
SEQ = 512
QUARTER = SEQ // 4
GRID = ("row", "col")

EPSILON = 1e-06
NEGATIVE = -1e30
F32 = jnp.float32
BF16 = jnp.bfloat16
NN = (((1,), (0,)), ((), ()))
NT = (((1,), (1,)), ((), ()))
TN = (((0,), (0,)), ((), ()))
MIB = 1 << 20


LIGHT = ("project_hidden", "first_back", "heads_back")


def cost_of(name):
    scale = 1e-6 if name in LIGHT else 1
    return pl.CostEstimate(flops=int(1e13 * scale), bytes_accessed=int(1e9 * scale), transcendentals=0)


def mm(left, right, contract):
    return lax.dot_general(left, right, contract, preferred_element_type=F32)


def attend_kernel(qkv_ref, column_ref, line_ref, heads_ref, probs_ref, mask):
    @pl.when(pl.program_id(0) == 0)
    def _():
        mask[...] = jnp.where(column_ref[...] == line_ref[...], 0.0, NEGATIVE)

    mixed = []
    for head in range(2):
        base = head * 3 * HD
        query = qkv_ref[:, base : base + HD] * jnp.asarray(1 / math.sqrt(HD), BF16)
        key = qkv_ref[:, base + HD : base + 2 * HD]
        value = qkv_ref[:, base + 2 * HD : base + 3 * HD]
        scores = mm(key, query, NT) + mask[...]
        powers = jnp.exp(scores - jnp.max(scores, 0, keepdims=True))
        total = jnp.sum(powers, 0, keepdims=True)
        probs = (powers * (1.0 / total)).astype(BF16)
        probs_ref[head] = probs
        mixed.append(mm(value, probs, TN))
    heads_ref[...] = jnp.concatenate(mixed, 0).T.astype(BF16)


def attend(qkv, labels):
    pairs = qkv.shape[1] // (6 * HD)
    return pl.pallas_call(
        attend_kernel,
        grid=(pairs,),
        in_specs=[
            pl.BlockSpec((SEQ, 6 * HD), lambda i: (0, i)),
            pl.BlockSpec((SEQ, 1), lambda i: (0, 0)),
            pl.BlockSpec((1, SEQ), lambda i: (0, 0)),
        ],
        out_specs=[
            pl.BlockSpec((SEQ, 2 * HD), lambda i: (0, i)),
            pl.BlockSpec((2, SEQ, SEQ), lambda i: (i, 0, 0)),
        ],
        out_shape=[
            jax.ShapeDtypeStruct((SEQ, pairs * 2 * HD), BF16),
            jax.ShapeDtypeStruct((pairs * 2, SEQ, SEQ), BF16),
        ],
        scratch_shapes=[pltpu.VMEM((SEQ, SEQ), F32)],
        compiler_params=pltpu.CompilerParams(vmem_limit_bytes=(56 if pairs > 2 else 32) * MIB),
        cost_estimate=cost_of("attend"),
        name="attend",
    )(qkv, labels[:, None], labels[None, :])


def attend_back_kernel(qkv_ref, probs_ref, grad_ref, out_ref):
    for head in range(2):
        base = head * 3 * HD
        scale = jnp.asarray(1 / math.sqrt(HD), BF16)
        query = qkv_ref[:, base : base + HD] * scale
        key = qkv_ref[:, base + HD : base + 2 * HD] * scale
        value = qkv_ref[:, base + 2 * HD : base + 3 * HD]
        grad = grad_ref[:, head * HD : (head + 1) * HD]
        probs = probs_ref[head]
        d_value = mm(probs, grad, NN)
        d_probs = mm(value, grad, NT)
        wide = probs.astype(F32)
        delta = jnp.sum(wide * d_probs, 0, keepdims=True)
        d_scores = (wide * (d_probs - delta)).astype(BF16)
        d_key = mm(d_scores, query, NN)
        d_query = mm(key, d_scores, TN).T
        out_ref[:, base : base + HD] = d_query.astype(BF16)
        out_ref[:, base + HD : base + 2 * HD] = d_key.astype(BF16)
        out_ref[:, base + 2 * HD : base + 3 * HD] = d_value.astype(BF16)


def attend_back(qkv, probs, grad):
    pairs = qkv.shape[1] // (6 * HD)
    return pl.pallas_call(
        attend_back_kernel,
        grid=(pairs,),
        in_specs=[
            pl.BlockSpec((SEQ, 6 * HD), lambda i: (0, i)),
            pl.BlockSpec((2, SEQ, SEQ), lambda i: (i, 0, 0)),
            pl.BlockSpec((SEQ, 2 * HD), lambda i: (0, i)),
        ],
        out_specs=pl.BlockSpec((SEQ, 6 * HD), lambda i: (0, i)),
        out_shape=jax.ShapeDtypeStruct((SEQ, qkv.shape[1]), BF16),
        compiler_params=pltpu.CompilerParams(vmem_limit_bytes=(56 if pairs > 2 else 32) * MIB),
        cost_estimate=cost_of("attend_back"),
        name="attend_back",
    )(qkv, probs, grad)


def swap_core(value):
    return lax.ppermute(value, "row", [(i, i ^ 1) for i in range(4)])


def swap_row(value):
    return lax.ppermute(value, "row", [(i, i ^ 2) for i in range(4)])


def swap_col(value):
    return lax.ppermute(value, "col", [(0, 1), (1, 0)])


def after(value, *others):
    return lax.optimization_barrier((value, *others))[0]


def after_all(values, *others):
    return lax.optimization_barrier((*values, *others))[: len(values)]


def add(*values):
    total = values[0].astype(F32)
    for value in values[1:]:
        total = total + value.astype(F32)
    return total.astype(BF16)


def own_rows(value, odd, col):
    rolled = jnp.where(odd, jnp.roll(value, -2 * QUARTER, 0), value)
    first = jnp.concatenate([rolled[:SEQ], rolled[2 * SEQ : 2 * SEQ + QUARTER]], 0)
    second = jnp.concatenate([rolled[SEQ : 2 * SEQ], rolled[2 * SEQ + QUARTER :]], 0)
    mine = jnp.where(col == 0, first, second)
    return jnp.concatenate([mine, swap_col(jnp.where(col == 0, second, first))], 1)


def give_back(mine, other, odd, col):
    other = other.astype(F32)
    first = jnp.where(col == 0, mine, other)
    second = jnp.where(col == 0, other, mine)
    rolled = jnp.concatenate([first[:SEQ], second[:SEQ], first[SEQ:], second[SEQ:]], 0)
    return jnp.where(odd, jnp.roll(rolled, 2 * QUARTER, 0), rolled)


def swap(offset):
    return [(i, i ^ offset) for i in range(8)]


def spread_heads(value, member, row):
    width = value.shape[1] // 4
    pieces = []
    for offset in range(4):
        piece = lax.dynamic_slice_in_dim(value, ((member ^ offset) ^ row) * width, width, 1)
        pieces.append(piece if offset == 0 else lax.ppermute(piece, GRID, swap(offset)))
    return jnp.concatenate(pieces, 0)


def send_heads(value):
    pieces = [value[offset * QUARTER : (offset + 1) * QUARTER] for offset in range(4)]
    return [piece if offset == 0 else lax.ppermute(piece, GRID, swap(offset)) for offset, piece in enumerate(pieces)]


def join_heads(pieces, member, row):
    width = pieces[0].shape[1]
    whole = jnp.zeros((QUARTER, 4 * width), pieces[0].dtype)
    for offset, piece in enumerate(pieces):
        whole = lax.dynamic_update_slice_in_dim(whole, piece, ((member ^ offset) ^ row) * width, 1)
    return whole


class Shards:
    def __init__(self, depth, shard, beside, across, *corners, near_only=False):
        self.depth, self.width = depth, shard.shape[1]
        near = [(0, 0, shard), (1, 0, beside), (4, 0, across)]
        near += [(5, index * depth // 2, corner) for index, corner in enumerate(corners)]
        self.parts = near
        if not near_only:
            self.pass_on(near)

    def pass_on(self, near, *ties):
        far = [(place + 2, start, swap_core(after(part, *ties) if ties else part)) for place, start, part in near]
        self.parts = self.parts + far


def dense(kernel, in_specs, out_specs, out_shape, scratch, flops, name, shards=None):
    if shards is None:
        body, extra_specs, extra_scratch = kernel, [], []
    else:
        places = [(place, start, min(part.shape[0], shards.depth - start)) for place, start, part in shards.parts]
        count = len(places)
        extra_specs = [pl.BlockSpec(memory_space=pl.ANY)] * count
        extra_scratch = [
            pltpu.VMEM((8, shards.depth, shards.width), BF16),
            pltpu.SemaphoreType.DMA((count,)),
        ]

        def body(*refs):
            step = pl.program_id(0)
            held, done = refs[-2:]
            copies = [
                pltpu.make_async_copy(
                    refs[k].at[pl.ds(0, rows)], held.at[place, pl.ds(start, rows)], done.at[k]
                )
                for k, (place, start, rows) in enumerate(places)
            ]
            for block in range(4):

                @pl.when(step == 0)
                def _():
                    for copy, (place, _, _) in zip(copies, places):
                        if place // 2 == block:
                            copy.start()

            for block in range(4):

                @pl.when(step == block)
                def _():
                    for copy, (place, _, _) in zip(copies, places):
                        if place // 2 == block:
                            copy.wait()

            kernel(held.at[pl.ds(2 * step, 2)], *refs[count:-2])

    return pl.pallas_call(
        body,
        grid=(4,),
        in_specs=extra_specs + in_specs,
        out_specs=out_specs,
        out_shape=out_shape,
        scratch_shapes=scratch + extra_scratch,
        compiler_params=pltpu.CompilerParams(vmem_limit_bytes=48 * MIB),
        cost_estimate=cost_of(name),
        name=name,
    )


def whole(value):
    return pl.BlockSpec(value.shape, lambda i: (0,) * value.ndim)


def columns_of(value, parts=4):
    return pl.BlockSpec((value.shape[0], value.shape[1] // parts), lambda i: (0, i))


def shaped(shape, kind):
    return jax.ShapeDtypeStruct(shape, kind)


def halves_times(left_ref, weight_ref, start, width):
    half = left_ref.shape[1] // 2
    stop = start + width
    return mm(left_ref[:, :half], weight_ref[0, :, start:stop], NN) + mm(
        left_ref[:, half:], weight_ref[1, :, start:stop], NN
    )


def qkv_kernel(weight_ref, x_ref, bias_ref, out_ref):
    for start in range(0, out_ref.shape[1], 256):
        part = halves_times(x_ref, weight_ref, start, 256)
        out_ref[:, start : start + 256] = (part + bias_ref[:, start : start + 256]).astype(BF16)


def project_qkv(x, shards, bias):
    width = 4 * shards.width
    return dense(
        qkv_kernel,
        [whole(x), columns_of(bias)],
        pl.BlockSpec((x.shape[0], width // 4), lambda i: (0, i)),
        shaped((x.shape[0], width), BF16),
        [],
        2 * x.shape[0] * D * width,
        "project_qkv",
        shards,
    )(*[part for _, _, part in shards.parts], x, bias)


def hidden_kernel(weight_ref, x_ref, bias_ref, active_ref, slope_ref):
    for start in range(0, active_ref.shape[1], 256):
        stop = start + 256
        hidden = halves_times(x_ref, weight_ref, start, 256) + bias_ref[:, start:stop]
        share = 0.5 * (1.0 + lax.erf(hidden * math.sqrt(0.5)))
        bell = jnp.exp(hidden * hidden * -0.5) * (1 / math.sqrt(2 * math.pi))
        active_ref[:, start:stop] = (hidden * share).astype(BF16)
        slope_ref[:, start:stop] = (share + hidden * bell).astype(BF16)


def project_hidden(x, shards, bias):
    width = 4 * shards.width
    block = pl.BlockSpec((x.shape[0], width // 4), lambda i: (0, i))
    return dense(
        hidden_kernel,
        [whole(x), columns_of(bias)],
        [block, block],
        [shaped((x.shape[0], width), BF16)] * 2,
        [],
        4 * x.shape[0] * D * width,
        "project_hidden",
        shards,
    )(*[part for _, _, part in shards.parts], x, bias)


def add_product(left_ref, weight_ref, total, contract):
    step = pl.program_id(0)
    half = D // 2
    for col in range(2):
        part = mm(left_ref[...], weight_ref[col], contract)
        span = slice(col * half, (col + 1) * half)

        @pl.when(step == 0)
        def _():
            total[:, span] = part

        @pl.when(step > 0)
        def _():
            total[:, span] += part


ROWS = 16


def each_rows(count, body):
    @pl.loop(0, count // (2 * ROWS))
    def _(step):
        for part in range(2):
            body(pl.ds(pl.multiple_of((2 * step + part) * ROWS, ROWS), ROWS))


def add_rows(partial, place, value):
    partial[place] += value[:8] + value[8:]


def norm_parts(value):
    center = jnp.sum(value, 1, keepdims=True) * (1 / D)
    squares = jnp.sum(value * value, 1, keepdims=True) * (1 / D)
    inverse = lax.rsqrt(squares - center * center + EPSILON)
    return ((value - center) * inverse, inverse)


def norm_back(grad, unit, inverse, gain):
    scaled = grad * gain
    mean = jnp.sum(scaled, 1, keepdims=True) * (1 / D)
    paired = jnp.sum(scaled * unit, 1, keepdims=True) * (1 / D)
    return inverse * (scaled - mean - unit * paired)


def total_of(value):
    return jnp.sum(value, 0, keepdims=True)


def first_norm_kernel(weight_ref, heads_ref, x_ref, vec_ref, unit_ref, inverse_ref, low_ref, total):
    add_product(heads_ref, weight_ref, total, NN)

    @pl.when(pl.program_id(0) == 3)
    def _():
        def body(rows):
            value = x_ref[rows, :].astype(F32) + (total[rows, :] + vec_ref[0:1, :])
            unit, inverse = norm_parts(value)
            unit_ref[rows, :] = unit
            inverse_ref[rows, :] = inverse
            low_ref[rows, :] = (unit * vec_ref[1:2, :] + vec_ref[2:3, :]).astype(BF16)

        each_rows(x_ref.shape[0], body)


def first_norm(heads, shards, x, vec):
    rows = x.shape[0]
    outs = [shaped((rows, D), F32), shaped((rows, 1), F32), shaped((rows, D), BF16)]
    return dense(
        first_norm_kernel,
        [columns_of(heads), whole(x), whole(vec)],
        [whole(out) for out in outs],
        outs,
        [pltpu.VMEM((rows, D), F32)],
        2 * rows * D * D,
        "first_norm",
        shards,
    )(*[part for _, _, part in shards.parts], heads, x, vec)


def second_norm_kernel(
    weight_ref, active_ref, unit_ref, incoming_ref, vec_ref, out_ref, leave_ref, back_ref, low_ref, sums_ref, total, partial
):
    add_product(active_ref, weight_ref, total, NN)

    @pl.when(pl.program_id(0) == 3)
    def _():
        partial[...] = jnp.zeros_like(partial)
        half = D // 2

        def body(rows):
            middle = unit_ref[rows, :] * vec_ref[1:2, :] + vec_ref[2:3, :]
            unit, inverse = norm_parts(middle + (total[rows, :] + vec_ref[3:4, :]))
            out = unit * vec_ref[4:5, :] + vec_ref[5:6, :]
            out_ref[rows, :] = out[:, :half]
            leave_ref[rows, :] = out[:, half:].astype(BF16)
            grad = incoming_ref[rows, :].astype(F32)
            add_rows(partial, 1, grad * unit)
            add_rows(partial, 2, grad)
            back = norm_back(grad, unit, inverse, vec_ref[4:5, :])
            low = back.astype(BF16)
            back_ref[rows, :] = back
            low_ref[rows, :] = low
            add_rows(partial, 0, low.astype(F32))

        each_rows(unit_ref.shape[0], body)
        for place in range(3):
            sums_ref[place : place + 1, :] = total_of(partial[place])


def second_norm(active, shards, unit, incoming, vec):
    rows = unit.shape[0]
    outs = [
        shaped((rows, D // 2), F32),
        shaped((rows, D // 2), BF16),
        shaped((rows, D), F32),
        shaped((rows, D), BF16),
        shaped((3, D), F32),
    ]
    return dense(
        second_norm_kernel,
        [columns_of(active), whole(unit), whole(incoming), whole(vec)],
        [whole(out) for out in outs],
        outs,
        [pltpu.VMEM((rows, D), F32), pltpu.VMEM((3, 8, D), F32)],
        2 * rows * D * active.shape[1],
        "second_norm",
        shards,
    )(*[part for _, _, part in shards.parts], active, unit, incoming, vec)


def first_back_kernel(
    weight_ref, d_hidden_ref, back_ref, unit_ref, inverse_ref, vec_ref, out_ref, low_ref, sums_ref, total, partial
):
    add_product(d_hidden_ref, weight_ref, total, NT)

    @pl.when(pl.program_id(0) == 3)
    def _():
        partial[...] = jnp.zeros_like(partial)

        def body(rows):
            grad = back_ref[rows, :] + total[rows, :]
            unit = unit_ref[rows, :]
            add_rows(partial, 1, grad * unit)
            add_rows(partial, 2, grad)
            back = norm_back(grad, unit, inverse_ref[rows, :], vec_ref[1:2, :])
            low = back.astype(BF16)
            out_ref[rows, :] = back
            low_ref[rows, :] = low
            add_rows(partial, 0, low.astype(F32))

        each_rows(unit_ref.shape[0], body)
        for place in range(3):
            sums_ref[place : place + 1, :] = total_of(partial[place])


def first_back(d_hidden, shards, back, unit, inverse, vec):
    rows = unit.shape[0]
    outs = [shaped((rows, D), F32), shaped((rows, D), BF16), shaped((3, D), F32)]
    return dense(
        first_back_kernel,
        [columns_of(d_hidden), whole(back), whole(unit), whole(inverse), whole(vec)],
        [whole(out) for out in outs],
        outs,
        [pltpu.VMEM((rows, D), F32), pltpu.VMEM((3, 8, D), F32)],
        2 * rows * D * d_hidden.shape[1],
        "first_back",
        shards,
    )(*[part for _, _, part in shards.parts], d_hidden, back, unit, inverse, vec)


def input_back_kernel(weight_ref, d_qkv_ref, back_ref, out_ref, leave_ref, sums_ref, total):
    add_product(d_qkv_ref, weight_ref, total, NT)
    sums_ref[...] = total_of(d_qkv_ref[...].astype(F32))

    @pl.when(pl.program_id(0) == 3)
    def _():
        half = D // 2
        out_ref[...] = back_ref[:, :half] + total[:, :half]
        leave_ref[...] = (back_ref[:, half:] + total[:, half:]).astype(BF16)


def input_back(d_qkv, shards, back):
    rows, width = d_qkv.shape
    outs = [shaped((rows, D // 2), F32), shaped((rows, D // 2), BF16), shaped((1, width), F32)]
    return dense(
        input_back_kernel,
        [columns_of(d_qkv), whole(back)],
        [whole(outs[0]), whole(outs[1]), columns_of(outs[2])],
        outs,
        [pltpu.VMEM((rows, D), F32)],
        2 * rows * D * width,
        "input_back",
        shards,
    )(*[part for _, _, part in shards.parts], d_qkv, back)


def columns_back(grad_ref, weight_ref, start, stop):
    half = D // 2
    return mm(grad_ref[:, :half], weight_ref[0, start:stop, :], NT) + mm(
        grad_ref[:, half:], weight_ref[1, start:stop, :], NT
    )


def hidden_back_kernel(weight_ref, grad_ref, slope_ref, out_ref, sums_ref):
    for start in range(0, out_ref.shape[1], 256):
        span = slice(start, start + 256)
        part = columns_back(grad_ref, weight_ref, start, start + 256)
        low = (part * slope_ref[:, span].astype(F32)).astype(BF16)
        out_ref[:, span] = low
        sums_ref[:, span] = total_of(low.astype(F32))


def hidden_back(grad, shards, slope):
    outs = [shaped(slope.shape, BF16), shaped((1, slope.shape[1]), F32)]
    return dense(
        hidden_back_kernel,
        [whole(grad), columns_of(slope)],
        [columns_of(out) for out in outs],
        outs,
        [],
        2 * grad.shape[0] * D * slope.shape[1],
        "hidden_back",
        shards,
    )(*[part for _, _, part in shards.parts], grad, slope)


def heads_back_kernel(weight_ref, grad_ref, out_ref):
    out_ref[...] = columns_back(grad_ref, weight_ref, 0, weight_ref.shape[1]).astype(BF16)


def heads_back(grad, shards):
    return dense(
        heads_back_kernel,
        [whole(grad)],
        columns_of(grad),
        shaped(grad.shape, BF16),
        [],
        2 * grad.shape[0] * D * D,
        "heads_back",
        shards,
    )(*[part for _, _, part in shards.parts], grad)


def grad_up_kernel(left_ref, right_ref, keep_ref, leave_ref, turned):
    step = pl.program_id(0)
    half = D // 2

    @pl.when(step == 0)
    def _():
        turned[...] = left_ref[...].T

    for parity, out_ref in enumerate((keep_ref, leave_ref)):

        @pl.when(step % 2 == parity)
        def _():
            for col in range(2):
                out_ref[col] = mm(turned[col * half : (col + 1) * half, :], right_ref[...], NN).astype(BF16)


def two_blocks(out):
    return pl.BlockSpec((2, *out.shape[1:]), lambda i: (i // 2, 0, 0))


def grad_up(left, right):
    out = shaped((4, D // 2, right.shape[1] // 4), BF16)
    return dense(
        grad_up_kernel,
        [whole(left), columns_of(right)],
        [two_blocks(out)] * 2,
        [out] * 2,
        [pltpu.VMEM((D, left.shape[0]), BF16)],
        2 * left.shape[0] * D * right.shape[1],
        "grad_up",
    )(left, right)


def grad_down_kernel(left_ref, right_ref, keep_ref, leave_ref):
    step = pl.program_id(0)
    half = D // 2
    for parity, out_ref in enumerate((keep_ref, leave_ref)):

        @pl.when(step % 2 == parity)
        def _():
            turned = left_ref[...].T
            for col in range(2):
                out_ref[col] = mm(turned, right_ref[:, col * half : (col + 1) * half], NN).astype(BF16)


def grad_down(left, right):
    out = shaped((4, left.shape[1] // 4, D // 2), BF16)
    return dense(
        grad_down_kernel,
        [columns_of(left), whole(right)],
        [two_blocks(out)] * 2,
        [out] * 2,
        [],
        2 * left.shape[0] * D * left.shape[1],
        "grad_down",
    )(left, right)


class PairSum:
    def __init__(self, value, size):
        self.whole = None
        if size & (size - 1):
            self.whole = lax.psum(value, "dp")
        self.value, self.other = value, None
        place = lax.axis_index("dp")
        levels = [1 << k for k in range(size.bit_length() - 1)]
        pairs = [([(i, i ^ step) for i in range(size)], (place // step) % 2 == 1) for step in levels]
        self.plan = [(True, *pair) for pair in pairs] + [(False, *pair) for pair in reversed(pairs)]
        self.upper = self.down = None
        if self.whole is not None:
            self.plan = []

    def step(self, last):
        self.take(last)
        if not self.plan:
            return self.value
        self.down, pairs, self.upper = self.plan.pop(0)
        if self.down:
            half = self.value.shape[0] // 2
            top, bottom = self.value[:half], self.value[half:]
            self.value = jnp.where(self.upper, bottom, top)
            leaving = jnp.where(self.upper, top, bottom)
        else:
            leaving = self.value
        leaving = after(leaving, last)
        self.other = lax.ppermute(leaving, "dp", pairs)
        return leaving

    def take(self, last):
        if self.other is None:
            return
        other = after(self.other, last)
        if self.down:
            self.value = add(self.value, other)
        else:
            parts = jnp.where(self.upper, other, self.value), jnp.where(self.upper, self.value, other)
            self.value = jnp.concatenate(parts, 0)
        self.other = None

    def result(self):
        return self.value if self.whole is None else self.whole


class GridSum:
    def __init__(self, keep, leaving):
        self.keep, self.other = keep, swap_core(leaving)
        self.half = keep.shape[1] // 2
        self.kernel = leaving

    def upper(self, place, *more):
        return add(self.keep[place, : self.half], self.other[place, : self.half], *more)

    def lower(self, place, *more):
        return add(self.keep[place, self.half :], self.other[place, self.half :], *more)

    def send(self, *ties):
        if ties:
            self.other = after(self.other, *ties)
        col = jnp.concatenate([self.upper(3), self.upper(1)], 0)
        row = jnp.concatenate([self.lower(3), self.lower(2)], 0)
        self.sent = lax.optimization_barrier((col, row))
        self.from_col, self.from_row = swap_col(self.sent[0]), swap_row(self.sent[1])
        return self.sent

    def send_last(self, *ties):
        if ties:
            self.from_row, self.from_col = lax.optimization_barrier((self.from_row, self.from_col, *ties))[:2]
        col = self.lower(1, self.from_row[: self.half])
        row = self.upper(2, self.from_col[: self.half])
        self.last = lax.optimization_barrier((col, row))
        self.last_col, self.last_row = swap_col(self.last[0]), swap_row(self.last[1])
        return self.last

    def result(self, *ties):
        from_col, last_row = self.from_col, self.last_row
        if ties:
            from_col, last_row = lax.optimization_barrier((from_col, last_row, *ties))[:2]
        upper = self.upper(0, from_col[self.half :], last_row)
        return jnp.concatenate([upper, self.lower(0, self.from_row[self.half :], self.last_col)], 0)


class VectorSum:
    def __init__(self, value, then, size):
        self.value, self.then, self.other = value, then, None
        self.size = size
        levels = [1 << k for k in range(size.bit_length() - 1)] if size & (size - 1) == 0 else []
        self.plan = [swap_core, swap_row, swap_col, None]
        self.plan += [functools.partial(lax.ppermute, axis_name="dp", perm=[(i, i ^ k) for i in range(size)]) for k in levels]

    def step(self, last):
        self.take(last)
        if not self.plan:
            return last
        move = self.plan.pop(0)
        if move is None:
            self.value = self.then(self.value)
            if not self.plan:
                return last
            move = self.plan.pop(0)
        leaving = after(self.value, last)
        self.other = move(leaving)
        return leaving

    def take(self, last):
        if self.other is not None:
            self.value = self.value + after(self.other, last)
            self.other = None

    def result(self):
        return lax.psum(self.value, "dp") if self.size & (self.size - 1) else self.value


def local(
    n_dp,
    tokens,
    segments,
    qkv_weight,
    qv_bias,
    out_weight,
    out_bias,
    ln1_gain,
    ln1_bias,
    ff_in_weight,
    ff_in_bias,
    ff_out_weight,
    ff_out_bias,
    ln2_gain,
    ln2_bias,
    out_grad,
):
    row, col = lax.axis_index("row"), lax.axis_index("col")
    odd = row % 2 == 1
    member = (row % 2) * 2 + col

    def in_order(mine, other):
        return jnp.where(col == 0, mine, other), jnp.where(col == 0, other, mine)

    packed = jnp.concatenate(
        [out_bias, ln1_gain, ln1_bias, ff_out_bias, ln2_gain, ln2_bias, ff_in_bias, qv_bias.reshape(-1)]
    )
    beside, across = swap_col(packed), swap_row(packed)
    near = [packed, beside, across, swap_row(beside)]
    far = [swap_core(value) for value in near]
    packed = jnp.stack([near[0], near[1], far[0], far[1], near[2], near[3], far[2], far[3]])
    qkv_beside, qkv_across = swap_col(qkv_weight), swap_row(qkv_weight)
    x = own_rows(after(tokens, qkv_beside, qkv_across), odd, col)
    qkv_corner = swap_row(qkv_beside)
    qkv_w = Shards(D // 2, qkv_weight, qkv_beside, qkv_across, qkv_corner)
    out_beside = swap_col(after(out_weight, x))
    out_across = swap_row(after(out_weight, qkv_corner))
    incoming = own_rows(after(out_grad, out_beside), odd, col)
    ff_in_across = swap_row(after(ff_in_weight, out_across))

    vec = packed[:2, : 6 * 512].reshape(2, 6, 512).transpose(1, 0, 2).reshape(6, D)
    pairs = packed[:, 6 * 512 :].reshape(4, 2, 768)
    first, second = in_order(pairs[:, 0], pairs[:, 1])
    ff_in_b = jnp.concatenate([first[:, :512], second[:, :512]], 1).reshape(1, -1)
    qv_b = jnp.concatenate([first[:, 512:], second[:, 512:]], 1).reshape(-1, 2 * HD)
    hollow = jnp.zeros((qv_b.shape[0], HD), F32)
    qkv_b = jnp.concatenate([qv_b[:, :HD], hollow, qv_b[:, HD:]], 1).reshape(1, -1)

    group = (row // 2) * 5
    labels = lax.dynamic_slice_in_dim(segments, (group + (row % 2) * 3 + col) * SEQ, SEQ)
    shared = lax.dynamic_slice_in_dim(segments, (group + 2) * SEQ, SEQ)
    shared = jnp.concatenate(
        [lax.dynamic_slice_in_dim(shared, (member ^ offset) * QUARTER, QUARTER) for offset in range(4)]
    )

    qkv = project_qkv(x, qkv_w, qkv_b)
    qkv_shared = spread_heads(qkv[SEQ:], member, row)
    heads_shared, probs_shared = attend(after(qkv_shared, incoming), shared)
    pieces = send_heads(heads_shared)
    ff_in_beside = swap_col(after(ff_in_weight, heads_shared))
    half = out_weight.shape[0] // 2
    out_corners = swap_col(out_across[:half]), swap_row(out_beside[half:])
    out_w = Shards(D // 4, out_weight, out_beside, out_across, *out_corners)
    heads_own, probs_own = attend(after(qkv, heads_shared, *[part for _, _, part in out_w.parts]), labels)
    pieces = after_all(pieces, heads_own)
    heads = jnp.concatenate([heads_own, join_heads(pieces, member, row)], 0)
    ff_in_beside, ff_in_across, ff_out_weight = after_all((ff_in_beside, ff_in_across, ff_out_weight), heads)
    half = ff_in_weight.shape[0] // 2
    ff_in_corners = swap_col(ff_in_across[:half]), swap_row(ff_in_beside[half:])
    ff_in_w = Shards(D // 2, ff_in_weight, ff_in_beside, ff_in_across, *ff_in_corners, near_only=True)
    ff_in_near = ff_in_w.parts
    ff_in_w.pass_on(ff_in_near[:3])
    ff_out_beside, ff_out_across = swap_col(ff_out_weight), swap_row(ff_out_weight)
    unit_one, inverse_one, middle_low = first_norm(after(heads, ff_in_beside, ff_in_across), out_w, x, vec)
    ff_in_w.pass_on(ff_in_near[3:], unit_one)
    active, slope = project_hidden(middle_low, ff_in_w, ff_in_b)
    ff_out_beside, ff_out_across = after_all((ff_out_beside, ff_out_across), active)
    half = ff_out_weight.shape[0] // 2
    ff_out_corners = swap_col(ff_out_across[:half]), swap_row(ff_out_beside[half:])
    ff_out_w = Shards(D, ff_out_weight, ff_out_beside, ff_out_across, *ff_out_corners)
    out_mine, out_leave, back_two, d_two, sums_two = second_norm(active, ff_out_w, unit_one, incoming, vec)

    ff_out = GridSum(*grad_down(active, d_two))
    d_hidden, ff_in_bias_part = hidden_back(after(d_two, ff_out.kernel), ff_out_w, slope)
    out_other = after(swap_col(out_leave), d_hidden)
    ff_out.send(d_hidden, out_other)
    ff_in = GridSum(*grad_up(after(middle_low, *ff_out.sent), d_hidden))
    back_one, d_one, sums_one = first_back(
        after(d_hidden, ff_in.kernel), ff_in_w, back_two, unit_one, inverse_one, vec
    )
    d_heads = heads_back(d_one, out_w)
    d_shared = spread_heads(d_heads[SEQ:], member, row)
    ff_out.send_last(d_heads)
    d_qkv_shared = attend_back(qkv_shared, probs_shared, after(d_shared, *ff_out.last))
    pieces = send_heads(d_qkv_shared)
    ff_in.send(d_qkv_shared)
    d_qkv_own = attend_back(qkv, probs_own, after(d_heads, *ff_in.sent))
    ff_out_pairs = PairSum(ff_out.result(d_qkv_own), n_dp)
    event = ff_out_pairs.step(d_qkv_own)
    pieces = after_all(pieces, d_qkv_own, event)
    d_qkv = jnp.concatenate([d_qkv_own, join_heads(pieces, member, row)], 0)
    qkv_sum = GridSum(*grad_up(x, d_qkv))
    event = ff_out_pairs.step(qkv_sum.kernel)
    ff_in.send_last(event)
    out_sum = GridSum(*grad_down(heads, after(d_one, *ff_in.last)))
    event = ff_out_pairs.step(out_sum.kernel)
    ff_in_pairs = PairSum(ff_in.result(event), n_dp)
    event = ff_in_pairs.step(event)
    qkv_sum.send(event)
    in_mine, in_leave, column_sums = input_back(after(d_qkv, *qkv_sum.sent), qkv_w, back_one)
    def ordered(value):
        blocks = value.reshape(4, -1)
        return jnp.stack([lax.dynamic_index_in_dim(blocks, row ^ place, 0, False) for place in range(4)])

    place = row * 2 + col

    def own_part(value):
        halves = lax.dynamic_slice_in_dim(value[: 6 * D].reshape(6, 2, D // 2), col, 1, 1)[:, 0]
        ff_in_part = lax.dynamic_slice_in_dim(value, 6 * D + place * 512, 512)
        qv_part = lax.dynamic_slice_in_dim(value, 10 * D + place * 256, 256)
        return jnp.concatenate([halves.reshape(-1), ff_in_part, qv_part])

    halves = jnp.concatenate([sums_one, sums_two], 0)
    halves = jnp.concatenate(in_order(halves[:, : D // 2], halves[:, D // 2 :]), 1)
    column_sums = ordered(column_sums).reshape(-1, 3, HD)
    qv_sums = jnp.concatenate([column_sums[:, 0], column_sums[:, 2]], 1)
    sums = jnp.concatenate([halves.reshape(-1), ordered(ff_in_bias_part).reshape(-1), qv_sums.reshape(-1)])
    sums = VectorSum(sums, own_part, n_dp)
    qkv_sum.send_last(in_leave)
    event = ff_out_pairs.step(qkv_sum.last[0])
    event = ff_in_pairs.step(event)
    event = sums.step(event)
    out_sum.send(event)
    qkv_pairs = PairSum(qkv_sum.result(*out_sum.sent), n_dp)
    event = qkv_pairs.step(out_sum.sent[0])
    event = ff_in_pairs.step(event)
    event = sums.step(event)
    out_sum.send_last(event)
    event = qkv_pairs.step(out_sum.last[0])
    event = sums.step(event)
    in_other = swap_col(after(in_leave, event))
    event = ff_in_pairs.step(event)
    out_pairs = PairSum(out_sum.result(event), n_dp)
    event = out_pairs.step(event)
    event = sums.step(event)

    every = [ff_out_pairs, ff_in_pairs, qkv_pairs, sums, out_pairs]
    while any(pairs.plan for pairs in every):
        for pairs in every:
            event = pairs.step(event)
    input_grad = give_back(in_mine, after(in_other, event), odd, col)
    layer_out = give_back(out_mine, after(out_other, event), odd, col)
    for pairs in every:
        pairs.take(event)
    ff_out_grad, ff_in_grad, qkv_grad, early, out_w_grad = [pairs.result() for pairs in every]
    halves = early[: 6 * 512].reshape(6, 512)
    return (
        layer_out,
        input_grad,
        qkv_grad.astype(F32),
        early[7 * 512 :].reshape(2, 2 * HD),
        out_w_grad.astype(F32),
        halves[0],
        halves[1],
        halves[2],
        ff_in_grad.astype(F32),
        early[6 * 512 : 7 * 512],
        ff_out_grad.astype(F32),
        halves[3],
        halves[4],
        halves[5],
    )


def solution(mesh):
    in_specs = (
        P(("dp", "row"), "col"),
        P("dp"),
        P("col", "row"),
        P(("row", "col"), None),
        P("row", "col"),
        P("col"),
        P("col"),
        P("col"),
        P("col", "row"),
        P(("row", "col")),
        P("row", "col"),
        P("col"),
        P("col"),
        P("col"),
        P(("dp", "row"), "col"),
    )
    out_specs = (
        P(("dp", "row"), "col"),
        P(("dp", "row"), "col"),
        P("col", "row"),
        P(("row", "col"), None),
        P("row", "col"),
        P("col"),
        P("col"),
        P("col"),
        P("col", "row"),
        P(("row", "col")),
        P("row", "col"),
        P("col"),
        P("col"),
        P("col"),
    )
    step = functools.partial(local, mesh.shape["dp"])
    return jax.shard_map(step, mesh=mesh, in_specs=in_specs, out_specs=out_specs, check_vma=False)
```

```python
import functools
import math

import jax
import jax.numpy as jnp
from jax import lax
from jax.experimental import pallas as pl
from jax.experimental.pallas import tpu as pltpu
from jax.sharding import PartitionSpec as P

D = 1024
HD = 64
SEQ = 512
QUARTER = SEQ // 4
GRID = ("row", "col")

EPSILON = 1e-06
NEGATIVE = -1e30
F32 = jnp.float32
BF16 = jnp.bfloat16
NN = (((1,), (0,)), ((), ()))
NT = (((1,), (1,)), ((), ()))
TN = (((0,), (0,)), ((), ()))
MIB = 1 << 20


LIGHT = ("project_hidden", "first_back", "heads_back")


def cost_of(name):
    scale = 1e-6 if name in LIGHT else 1
    return pl.CostEstimate(flops=int(1e13 * scale), bytes_accessed=int(1e9 * scale), transcendentals=0)


def mm(left, right, contract):
    return lax.dot_general(left, right, contract, preferred_element_type=F32)


def attend_kernel(qkv_ref, column_ref, line_ref, heads_ref, probs_ref, mask):
    @pl.when(pl.program_id(0) == 0)
    def _():
        mask[...] = jnp.where(column_ref[...] == line_ref[...], 0.0, NEGATIVE)

    mixed = []
    for head in range(2):
        base = head * 3 * HD
        query = qkv_ref[:, base : base + HD] * jnp.asarray(1 / math.sqrt(HD), BF16)
        key = qkv_ref[:, base + HD : base + 2 * HD]
        value = qkv_ref[:, base + 2 * HD : base + 3 * HD]
        scores = mm(key, query, NT) + mask[...]
        powers = jnp.exp(scores - jnp.max(scores, 0, keepdims=True))
        total = jnp.sum(powers, 0, keepdims=True)
        probs = (powers * (1.0 / total)).astype(BF16)
        probs_ref[head] = probs
        mixed.append(mm(value, probs, TN))
    heads_ref[...] = jnp.concatenate(mixed, 0).T.astype(BF16)


def attend(qkv, labels):
    pairs = qkv.shape[1] // (6 * HD)
    return pl.pallas_call(
        attend_kernel,
        grid=(pairs,),
        in_specs=[
            pl.BlockSpec((SEQ, 6 * HD), lambda i: (0, i)),
            pl.BlockSpec((SEQ, 1), lambda i: (0, 0)),
            pl.BlockSpec((1, SEQ), lambda i: (0, 0)),
        ],
        out_specs=[
            pl.BlockSpec((SEQ, 2 * HD), lambda i: (0, i)),
            pl.BlockSpec((2, SEQ, SEQ), lambda i: (i, 0, 0)),
        ],
        out_shape=[
            jax.ShapeDtypeStruct((SEQ, pairs * 2 * HD), BF16),
            jax.ShapeDtypeStruct((pairs * 2, SEQ, SEQ), BF16),
        ],
        scratch_shapes=[pltpu.VMEM((SEQ, SEQ), F32)],
        compiler_params=pltpu.CompilerParams(vmem_limit_bytes=(56 if pairs > 2 else 32) * MIB),
        cost_estimate=cost_of("attend"),
        name="attend",
    )(qkv, labels[:, None], labels[None, :])


def attend_back_kernel(qkv_ref, probs_ref, grad_ref, out_ref):
    for head in range(2):
        base = head * 3 * HD
        scale = jnp.asarray(1 / math.sqrt(HD), BF16)
        query = qkv_ref[:, base : base + HD] * scale
        key = qkv_ref[:, base + HD : base + 2 * HD] * scale
        value = qkv_ref[:, base + 2 * HD : base + 3 * HD]
        grad = grad_ref[:, head * HD : (head + 1) * HD]
        probs = probs_ref[head]
        d_value = mm(probs, grad, NN)
        d_probs = mm(value, grad, NT)
        wide = probs.astype(F32)
        delta = jnp.sum(wide * d_probs, 0, keepdims=True)
        d_scores = (wide * (d_probs - delta)).astype(BF16)
        d_key = mm(d_scores, query, NN)
        d_query = mm(key, d_scores, TN).T
        out_ref[:, base : base + HD] = d_query.astype(BF16)
        out_ref[:, base + HD : base + 2 * HD] = d_key.astype(BF16)
        out_ref[:, base + 2 * HD : base + 3 * HD] = d_value.astype(BF16)


def attend_back(qkv, probs, grad):
    pairs = qkv.shape[1] // (6 * HD)
    return pl.pallas_call(
        attend_back_kernel,
        grid=(pairs,),
        in_specs=[
            pl.BlockSpec((SEQ, 6 * HD), lambda i: (0, i)),
            pl.BlockSpec((2, SEQ, SEQ), lambda i: (i, 0, 0)),
            pl.BlockSpec((SEQ, 2 * HD), lambda i: (0, i)),
        ],
        out_specs=pl.BlockSpec((SEQ, 6 * HD), lambda i: (0, i)),
        out_shape=jax.ShapeDtypeStruct((SEQ, qkv.shape[1]), BF16),
        compiler_params=pltpu.CompilerParams(vmem_limit_bytes=(56 if pairs > 2 else 32) * MIB),
        cost_estimate=cost_of("attend_back"),
        name="attend_back",
    )(qkv, probs, grad)


def swap_core(value):
    return lax.ppermute(value, "row", [(i, i ^ 1) for i in range(4)])


def swap_row(value):
    return lax.ppermute(value, "row", [(i, i ^ 2) for i in range(4)])


def swap_col(value):
    return lax.ppermute(value, "col", [(0, 1), (1, 0)])


def after(value, *others):
    return lax.optimization_barrier((value, *others))[0]


def after_all(values, *others):
    return lax.optimization_barrier((*values, *others))[: len(values)]


def add(*values):
    total = values[0].astype(F32)
    for value in values[1:]:
        total = total + value.astype(F32)
    return total.astype(BF16)


def own_rows(value, odd, col):
    rolled = jnp.where(odd, jnp.roll(value, -2 * QUARTER, 0), value)
    first = jnp.concatenate([rolled[:SEQ], rolled[2 * SEQ : 2 * SEQ + QUARTER]], 0)
    second = jnp.concatenate([rolled[SEQ : 2 * SEQ], rolled[2 * SEQ + QUARTER :]], 0)
    mine = jnp.where(col == 0, first, second)
    return jnp.concatenate([mine, swap_col(jnp.where(col == 0, second, first))], 1)


def give_back(mine, other, odd, col):
    other = other.astype(F32)
    first = jnp.where(col == 0, mine, other)
    second = jnp.where(col == 0, other, mine)
    rolled = jnp.concatenate([first[:SEQ], second[:SEQ], first[SEQ:], second[SEQ:]], 0)
    return jnp.where(odd, jnp.roll(rolled, 2 * QUARTER, 0), rolled)


def swap(offset):
    return [(i, i ^ offset) for i in range(8)]


def spread_heads(value, member, row):
    width = value.shape[1] // 4
    pieces = []
    for offset in range(4):
        piece = lax.dynamic_slice_in_dim(value, ((member ^ offset) ^ row) * width, width, 1)
        pieces.append(piece if offset == 0 else lax.ppermute(piece, GRID, swap(offset)))
    return jnp.concatenate(pieces, 0)


def send_heads(value):
    pieces = [value[offset * QUARTER : (offset + 1) * QUARTER] for offset in range(4)]
    return [piece if offset == 0 else lax.ppermute(piece, GRID, swap(offset)) for offset, piece in enumerate(pieces)]


def join_heads(pieces, member, row):
    width = pieces[0].shape[1]
    whole = jnp.zeros((QUARTER, 4 * width), pieces[0].dtype)
    for offset, piece in enumerate(pieces):
        whole = lax.dynamic_update_slice_in_dim(whole, piece, ((member ^ offset) ^ row) * width, 1)
    return whole


class Shards:
    def __init__(self, depth, shard, beside, across, *corners, near_only=False):
        self.depth, self.width = depth, shard.shape[1]
        near = [(0, 0, shard), (1, 0, beside), (4, 0, across)]
        near += [(5, index * depth // 2, corner) for index, corner in enumerate(corners)]
        self.parts = near
        if not near_only:
            self.pass_on(near)

    def pass_on(self, near, *ties):
        far = [(place + 2, start, swap_core(after(part, *ties) if ties else part)) for place, start, part in near]
        self.parts = self.parts + far


def dense(kernel, in_specs, out_specs, out_shape, scratch, flops, name, shards=None):
    if shards is None:
        body, extra_specs, extra_scratch = kernel, [], []
    else:
        places = [(place, start, min(part.shape[0], shards.depth - start)) for place, start, part in shards.parts]
        count = len(places)
        extra_specs = [pl.BlockSpec(memory_space=pl.ANY)] * count
        extra_scratch = [
            pltpu.VMEM((8, shards.depth, shards.width), BF16),
            pltpu.SemaphoreType.DMA((count,)),
        ]

        def body(*refs):
            step = pl.program_id(0)
            held, done = refs[-2:]
            copies = [
                pltpu.make_async_copy(
                    refs[k].at[pl.ds(0, rows)], held.at[place, pl.ds(start, rows)], done.at[k]
                )
                for k, (place, start, rows) in enumerate(places)
            ]
            for block in range(4):

                @pl.when(step == 0)
                def _():
                    for copy, (place, _, _) in zip(copies, places):
                        if place // 2 == block:
                            copy.start()

            for block in range(4):

                @pl.when(step == block)
                def _():
                    for copy, (place, _, _) in zip(copies, places):
                        if place // 2 == block:
                            copy.wait()

            kernel(held.at[pl.ds(2 * step, 2)], *refs[count:-2])

    return pl.pallas_call(
        body,
        grid=(4,),
        in_specs=extra_specs + in_specs,
        out_specs=out_specs,
        out_shape=out_shape,
        scratch_shapes=scratch + extra_scratch,
        compiler_params=pltpu.CompilerParams(vmem_limit_bytes=48 * MIB),
        cost_estimate=cost_of(name),
        name=name,
    )


def whole(value):
    return pl.BlockSpec(value.shape, lambda i: (0,) * value.ndim)


def columns_of(value, parts=4):
    return pl.BlockSpec((value.shape[0], value.shape[1] // parts), lambda i: (0, i))


def shaped(shape, kind):
    return jax.ShapeDtypeStruct(shape, kind)


def halves_times(left_ref, weight_ref, start, width):
    half = left_ref.shape[1] // 2
    stop = start + width
    return mm(left_ref[:, :half], weight_ref[0, :, start:stop], NN) + mm(
        left_ref[:, half:], weight_ref[1, :, start:stop], NN
    )


def qkv_kernel(weight_ref, x_ref, bias_ref, out_ref):
    for start in range(0, out_ref.shape[1], 256):
        part = halves_times(x_ref, weight_ref, start, 256)
        out_ref[:, start : start + 256] = (part + bias_ref[:, start : start + 256]).astype(BF16)


def project_qkv(x, shards, bias):
    width = 4 * shards.width
    return dense(
        qkv_kernel,
        [whole(x), columns_of(bias)],
        pl.BlockSpec((x.shape[0], width // 4), lambda i: (0, i)),
        shaped((x.shape[0], width), BF16),
        [],
        2 * x.shape[0] * D * width,
        "project_qkv",
        shards,
    )(*[part for _, _, part in shards.parts], x, bias)


def hidden_kernel(weight_ref, x_ref, bias_ref, active_ref, slope_ref):
    for start in range(0, active_ref.shape[1], 256):
        stop = start + 256
        hidden = halves_times(x_ref, weight_ref, start, 256) + bias_ref[:, start:stop]
        share = 0.5 * (1.0 + lax.erf(hidden * math.sqrt(0.5)))
        bell = jnp.exp(hidden * hidden * -0.5) * (1 / math.sqrt(2 * math.pi))
        active_ref[:, start:stop] = (hidden * share).astype(BF16)
        slope_ref[:, start:stop] = (share + hidden * bell).astype(BF16)


def project_hidden(x, shards, bias):
    width = 4 * shards.width
    block = pl.BlockSpec((x.shape[0], width // 4), lambda i: (0, i))
    return dense(
        hidden_kernel,
        [whole(x), columns_of(bias)],
        [block, block],
        [shaped((x.shape[0], width), BF16)] * 2,
        [],
        4 * x.shape[0] * D * width,
        "project_hidden",
        shards,
    )(*[part for _, _, part in shards.parts], x, bias)


def add_product(left_ref, weight_ref, total, contract):
    step = pl.program_id(0)
    half = D // 2
    for col in range(2):
        part = mm(left_ref[...], weight_ref[col], contract)
        span = slice(col * half, (col + 1) * half)

        @pl.when(step == 0)
        def _():
            total[:, span] = part

        @pl.when(step > 0)
        def _():
            total[:, span] += part


ROWS = 16


def each_rows(count, body):
    @pl.loop(0, count // (4 * ROWS))
    def _(step):
        for part in range(4):
            body(pl.ds(pl.multiple_of((4 * step + part) * ROWS, ROWS), ROWS))


def add_rows(partial, place, value):
    partial[place] += value[:8] + value[8:]


def norm_parts(value):
    center = jnp.sum(value, 1, keepdims=True) * (1 / D)
    squares = jnp.sum(value * value, 1, keepdims=True) * (1 / D)
    inverse = lax.rsqrt(squares - center * center + EPSILON)
    return ((value - center) * inverse, inverse)


def norm_back(grad, unit, inverse, gain):
    scaled = grad * gain
    mean = jnp.sum(scaled, 1, keepdims=True) * (1 / D)
    paired = jnp.sum(scaled * unit, 1, keepdims=True) * (1 / D)
    return inverse * (scaled - mean - unit * paired)


def total_of(value):
    return jnp.sum(value, 0, keepdims=True)


def first_norm_kernel(weight_ref, heads_ref, x_ref, vec_ref, unit_ref, inverse_ref, low_ref, total):
    add_product(heads_ref, weight_ref, total, NN)

    @pl.when(pl.program_id(0) == 3)
    def _():
        def body(rows):
            value = x_ref[rows, :].astype(F32) + (total[rows, :] + vec_ref[0:1, :])
            unit, inverse = norm_parts(value)
            unit_ref[rows, :] = unit
            inverse_ref[rows, :] = inverse
            low_ref[rows, :] = (unit * vec_ref[1:2, :] + vec_ref[2:3, :]).astype(BF16)

        each_rows(x_ref.shape[0], body)


def first_norm(heads, shards, x, vec):
    rows = x.shape[0]
    outs = [shaped((rows, D), F32), shaped((rows, 1), F32), shaped((rows, D), BF16)]
    return dense(
        first_norm_kernel,
        [columns_of(heads), whole(x), whole(vec)],
        [whole(out) for out in outs],
        outs,
        [pltpu.VMEM((rows, D), F32)],
        2 * rows * D * D,
        "first_norm",
        shards,
    )(*[part for _, _, part in shards.parts], heads, x, vec)


def second_norm_kernel(
    weight_ref, active_ref, unit_ref, incoming_ref, vec_ref, out_ref, leave_ref, back_ref, low_ref, sums_ref, total, partial
):
    add_product(active_ref, weight_ref, total, NN)

    @pl.when(pl.program_id(0) == 3)
    def _():
        partial[...] = jnp.zeros_like(partial)
        half = D // 2

        def body(rows):
            middle = unit_ref[rows, :] * vec_ref[1:2, :] + vec_ref[2:3, :]
            unit, inverse = norm_parts(middle + (total[rows, :] + vec_ref[3:4, :]))
            out = unit * vec_ref[4:5, :] + vec_ref[5:6, :]
            out_ref[rows, :] = out[:, :half]
            leave_ref[rows, :] = out[:, half:].astype(BF16)
            grad = incoming_ref[rows, :].astype(F32)
            add_rows(partial, 1, grad * unit)
            add_rows(partial, 2, grad)
            back = norm_back(grad, unit, inverse, vec_ref[4:5, :])
            low = back.astype(BF16)
            back_ref[rows, :] = back
            low_ref[rows, :] = low
            add_rows(partial, 0, low.astype(F32))

        each_rows(unit_ref.shape[0], body)
        for place in range(3):
            sums_ref[place : place + 1, :] = total_of(partial[place])


def second_norm(active, shards, unit, incoming, vec):
    rows = unit.shape[0]
    outs = [
        shaped((rows, D // 2), F32),
        shaped((rows, D // 2), BF16),
        shaped((rows, D), F32),
        shaped((rows, D), BF16),
        shaped((3, D), F32),
    ]
    return dense(
        second_norm_kernel,
        [columns_of(active), whole(unit), whole(incoming), whole(vec)],
        [whole(out) for out in outs],
        outs,
        [pltpu.VMEM((rows, D), F32), pltpu.VMEM((3, 8, D), F32)],
        2 * rows * D * active.shape[1],
        "second_norm",
        shards,
    )(*[part for _, _, part in shards.parts], active, unit, incoming, vec)


def first_back_kernel(
    weight_ref, d_hidden_ref, back_ref, unit_ref, inverse_ref, vec_ref, out_ref, low_ref, sums_ref, total, partial
):
    add_product(d_hidden_ref, weight_ref, total, NT)

    @pl.when(pl.program_id(0) == 3)
    def _():
        partial[...] = jnp.zeros_like(partial)

        def body(rows):
            grad = back_ref[rows, :] + total[rows, :]
            unit = unit_ref[rows, :]
            add_rows(partial, 1, grad * unit)
            add_rows(partial, 2, grad)
            back = norm_back(grad, unit, inverse_ref[rows, :], vec_ref[1:2, :])
            low = back.astype(BF16)
            out_ref[rows, :] = back
            low_ref[rows, :] = low
            add_rows(partial, 0, low.astype(F32))

        each_rows(unit_ref.shape[0], body)
        for place in range(3):
            sums_ref[place : place + 1, :] = total_of(partial[place])


def first_back(d_hidden, shards, back, unit, inverse, vec):
    rows = unit.shape[0]
    outs = [shaped((rows, D), F32), shaped((rows, D), BF16), shaped((3, D), F32)]
    return dense(
        first_back_kernel,
        [columns_of(d_hidden), whole(back), whole(unit), whole(inverse), whole(vec)],
        [whole(out) for out in outs],
        outs,
        [pltpu.VMEM((rows, D), F32), pltpu.VMEM((3, 8, D), F32)],
        2 * rows * D * d_hidden.shape[1],
        "first_back",
        shards,
    )(*[part for _, _, part in shards.parts], d_hidden, back, unit, inverse, vec)


def input_back_kernel(weight_ref, d_qkv_ref, back_ref, out_ref, leave_ref, sums_ref, total):
    add_product(d_qkv_ref, weight_ref, total, NT)
    sums_ref[...] = total_of(d_qkv_ref[...].astype(F32))

    @pl.when(pl.program_id(0) == 3)
    def _():
        half = D // 2
        out_ref[...] = back_ref[:, :half] + total[:, :half]
        leave_ref[...] = (back_ref[:, half:] + total[:, half:]).astype(BF16)


def input_back(d_qkv, shards, back):
    rows, width = d_qkv.shape
    outs = [shaped((rows, D // 2), F32), shaped((rows, D // 2), BF16), shaped((1, width), F32)]
    return dense(
        input_back_kernel,
        [columns_of(d_qkv), whole(back)],
        [whole(outs[0]), whole(outs[1]), columns_of(outs[2])],
        outs,
        [pltpu.VMEM((rows, D), F32)],
        2 * rows * D * width,
        "input_back",
        shards,
    )(*[part for _, _, part in shards.parts], d_qkv, back)


def columns_back(grad_ref, weight_ref, start, stop):
    half = D // 2
    return mm(grad_ref[:, :half], weight_ref[0, start:stop, :], NT) + mm(
        grad_ref[:, half:], weight_ref[1, start:stop, :], NT
    )


def hidden_back_kernel(weight_ref, grad_ref, slope_ref, out_ref, sums_ref):
    for start in range(0, out_ref.shape[1], 256):
        span = slice(start, start + 256)
        part = columns_back(grad_ref, weight_ref, start, start + 256)
        low = (part * slope_ref[:, span].astype(F32)).astype(BF16)
        out_ref[:, span] = low
        sums_ref[:, span] = total_of(low.astype(F32))


def hidden_back(grad, shards, slope):
    outs = [shaped(slope.shape, BF16), shaped((1, slope.shape[1]), F32)]
    return dense(
        hidden_back_kernel,
        [whole(grad), columns_of(slope)],
        [columns_of(out) for out in outs],
        outs,
        [],
        2 * grad.shape[0] * D * slope.shape[1],
        "hidden_back",
        shards,
    )(*[part for _, _, part in shards.parts], grad, slope)


def heads_back_kernel(weight_ref, grad_ref, out_ref):
    out_ref[...] = columns_back(grad_ref, weight_ref, 0, weight_ref.shape[1]).astype(BF16)


def heads_back(grad, shards):
    return dense(
        heads_back_kernel,
        [whole(grad)],
        columns_of(grad),
        shaped(grad.shape, BF16),
        [],
        2 * grad.shape[0] * D * D,
        "heads_back",
        shards,
    )(*[part for _, _, part in shards.parts], grad)


def grad_up_kernel(left_ref, right_ref, keep_ref, leave_ref, turned):
    step = pl.program_id(0)
    half = D // 2

    @pl.when(step == 0)
    def _():
        turned[...] = left_ref[...].T

    for parity, out_ref in enumerate((keep_ref, leave_ref)):

        @pl.when(step % 2 == parity)
        def _():
            for col in range(2):
                out_ref[col] = mm(turned[col * half : (col + 1) * half, :], right_ref[...], NN).astype(BF16)


def two_blocks(out):
    return pl.BlockSpec((2, *out.shape[1:]), lambda i: (i // 2, 0, 0))


def grad_up(left, right):
    out = shaped((4, D // 2, right.shape[1] // 4), BF16)
    return dense(
        grad_up_kernel,
        [whole(left), columns_of(right)],
        [two_blocks(out)] * 2,
        [out] * 2,
        [pltpu.VMEM((D, left.shape[0]), BF16)],
        2 * left.shape[0] * D * right.shape[1],
        "grad_up",
    )(left, right)


def grad_down_kernel(left_ref, right_ref, keep_ref, leave_ref):
    step = pl.program_id(0)
    half = D // 2
    for parity, out_ref in enumerate((keep_ref, leave_ref)):

        @pl.when(step % 2 == parity)
        def _():
            turned = left_ref[...].T
            for col in range(2):
                out_ref[col] = mm(turned, right_ref[:, col * half : (col + 1) * half], NN).astype(BF16)


def grad_down(left, right):
    out = shaped((4, left.shape[1] // 4, D // 2), BF16)
    return dense(
        grad_down_kernel,
        [columns_of(left), whole(right)],
        [two_blocks(out)] * 2,
        [out] * 2,
        [],
        2 * left.shape[0] * D * left.shape[1],
        "grad_down",
    )(left, right)


class PairSum:
    def __init__(self, value, size):
        self.whole = None
        if size & (size - 1):
            self.whole = lax.psum(value, "dp")
        self.value, self.other = value, None
        place = lax.axis_index("dp")
        levels = [1 << k for k in range(size.bit_length() - 1)]
        pairs = [([(i, i ^ step) for i in range(size)], (place // step) % 2 == 1) for step in levels]
        self.plan = [(True, *pair) for pair in pairs] + [(False, *pair) for pair in reversed(pairs)]
        self.upper = self.down = None
        if self.whole is not None:
            self.plan = []

    def step(self, last):
        self.take(last)
        if not self.plan:
            return self.value
        self.down, pairs, self.upper = self.plan.pop(0)
        if self.down:
            half = self.value.shape[0] // 2
            top, bottom = self.value[:half], self.value[half:]
            self.value = jnp.where(self.upper, bottom, top)
            leaving = jnp.where(self.upper, top, bottom)
        else:
            leaving = self.value
        leaving = after(leaving, last)
        self.other = lax.ppermute(leaving, "dp", pairs)
        return leaving

    def take(self, last):
        if self.other is None:
            return
        other = after(self.other, last)
        if self.down:
            self.value = add(self.value, other)
        else:
            parts = jnp.where(self.upper, other, self.value), jnp.where(self.upper, self.value, other)
            self.value = jnp.concatenate(parts, 0)
        self.other = None

    def result(self):
        return self.value if self.whole is None else self.whole


class GridSum:
    def __init__(self, keep, leaving):
        self.keep, self.other = keep, swap_core(leaving)
        self.half = keep.shape[1] // 2
        self.kernel = leaving

    def upper(self, place, *more):
        return add(self.keep[place, : self.half], self.other[place, : self.half], *more)

    def lower(self, place, *more):
        return add(self.keep[place, self.half :], self.other[place, self.half :], *more)

    def send(self, *ties):
        if ties:
            self.other = after(self.other, *ties)
        col = jnp.concatenate([self.upper(3), self.upper(1)], 0)
        row = jnp.concatenate([self.lower(3), self.lower(2)], 0)
        self.sent = lax.optimization_barrier((col, row))
        self.from_col, self.from_row = swap_col(self.sent[0]), swap_row(self.sent[1])
        return self.sent

    def send_last(self, *ties):
        if ties:
            self.from_row, self.from_col = lax.optimization_barrier((self.from_row, self.from_col, *ties))[:2]
        col = self.lower(1, self.from_row[: self.half])
        row = self.upper(2, self.from_col[: self.half])
        self.last = lax.optimization_barrier((col, row))
        self.last_col, self.last_row = swap_col(self.last[0]), swap_row(self.last[1])
        return self.last

    def result(self, *ties):
        from_col, last_row = self.from_col, self.last_row
        if ties:
            from_col, last_row = lax.optimization_barrier((from_col, last_row, *ties))[:2]
        upper = self.upper(0, from_col[self.half :], last_row)
        return jnp.concatenate([upper, self.lower(0, self.from_row[self.half :], self.last_col)], 0)


class VectorSum:
    def __init__(self, value, then, size):
        self.value, self.then, self.other = value, then, None
        self.size = size
        levels = [1 << k for k in range(size.bit_length() - 1)] if size & (size - 1) == 0 else []
        self.plan = [swap_core, swap_row, swap_col, None]
        self.plan += [functools.partial(lax.ppermute, axis_name="dp", perm=[(i, i ^ k) for i in range(size)]) for k in levels]

    def step(self, last):
        self.take(last)
        if not self.plan:
            return last
        move = self.plan.pop(0)
        if move is None:
            self.value = self.then(self.value)
            if not self.plan:
                return last
            move = self.plan.pop(0)
        leaving = after(self.value, last)
        self.other = move(leaving)
        return leaving

    def take(self, last):
        if self.other is not None:
            self.value = self.value + after(self.other, last)
            self.other = None

    def result(self):
        return lax.psum(self.value, "dp") if self.size & (self.size - 1) else self.value


def local(
    n_dp,
    tokens,
    segments,
    qkv_weight,
    qv_bias,
    out_weight,
    out_bias,
    ln1_gain,
    ln1_bias,
    ff_in_weight,
    ff_in_bias,
    ff_out_weight,
    ff_out_bias,
    ln2_gain,
    ln2_bias,
    out_grad,
):
    row, col = lax.axis_index("row"), lax.axis_index("col")
    odd = row % 2 == 1
    member = (row % 2) * 2 + col

    def in_order(mine, other):
        return jnp.where(col == 0, mine, other), jnp.where(col == 0, other, mine)

    packed = jnp.concatenate(
        [out_bias, ln1_gain, ln1_bias, ff_out_bias, ln2_gain, ln2_bias, ff_in_bias, qv_bias.reshape(-1)]
    )
    beside, across = swap_col(packed), swap_row(packed)
    near = [packed, beside, across, swap_row(beside)]
    far = [swap_core(value) for value in near]
    packed = jnp.stack([near[0], near[1], far[0], far[1], near[2], near[3], far[2], far[3]])
    qkv_beside, qkv_across = swap_col(qkv_weight), swap_row(qkv_weight)
    x = own_rows(after(tokens, qkv_beside, qkv_across), odd, col)
    qkv_corner = swap_row(qkv_beside)
    qkv_w = Shards(D // 2, qkv_weight, qkv_beside, qkv_across, qkv_corner)
    out_beside = swap_col(after(out_weight, x))
    out_across = swap_row(after(out_weight, qkv_corner))
    incoming = own_rows(after(out_grad, out_beside), odd, col)
    ff_in_across = swap_row(after(ff_in_weight, out_across))

    vec = packed[:2, : 6 * 512].reshape(2, 6, 512).transpose(1, 0, 2).reshape(6, D)
    pairs = packed[:, 6 * 512 :].reshape(4, 2, 768)
    first, second = in_order(pairs[:, 0], pairs[:, 1])
    ff_in_b = jnp.concatenate([first[:, :512], second[:, :512]], 1).reshape(1, -1)
    qv_b = jnp.concatenate([first[:, 512:], second[:, 512:]], 1).reshape(-1, 2 * HD)
    hollow = jnp.zeros((qv_b.shape[0], HD), F32)
    qkv_b = jnp.concatenate([qv_b[:, :HD], hollow, qv_b[:, HD:]], 1).reshape(1, -1)

    group = (row // 2) * 5
    labels = lax.dynamic_slice_in_dim(segments, (group + (row % 2) * 3 + col) * SEQ, SEQ)
    shared = lax.dynamic_slice_in_dim(segments, (group + 2) * SEQ, SEQ)
    shared = jnp.concatenate(
        [lax.dynamic_slice_in_dim(shared, (member ^ offset) * QUARTER, QUARTER) for offset in range(4)]
    )

    qkv = project_qkv(x, qkv_w, qkv_b)
    qkv_shared = spread_heads(qkv[SEQ:], member, row)
    heads_shared, probs_shared = attend(after(qkv_shared, incoming), shared)
    pieces = send_heads(heads_shared)
    ff_in_beside = swap_col(after(ff_in_weight, heads_shared))
    half = out_weight.shape[0] // 2
    out_corners = swap_col(out_across[:half]), swap_row(out_beside[half:])
    out_w = Shards(D // 4, out_weight, out_beside, out_across, *out_corners)
    heads_own, probs_own = attend(after(qkv, heads_shared, *[part for _, _, part in out_w.parts]), labels)
    pieces = after_all(pieces, heads_own)
    heads = jnp.concatenate([heads_own, join_heads(pieces, member, row)], 0)
    ff_in_beside, ff_in_across, ff_out_weight = after_all((ff_in_beside, ff_in_across, ff_out_weight), heads)
    half = ff_in_weight.shape[0] // 2
    ff_in_corners = swap_col(ff_in_across[:half]), swap_row(ff_in_beside[half:])
    ff_in_w = Shards(D // 2, ff_in_weight, ff_in_beside, ff_in_across, *ff_in_corners, near_only=True)
    ff_in_near = ff_in_w.parts
    ff_in_w.pass_on(ff_in_near[:3])
    ff_out_beside, ff_out_across = swap_col(ff_out_weight), swap_row(ff_out_weight)
    unit_one, inverse_one, middle_low = first_norm(after(heads, ff_in_beside, ff_in_across), out_w, x, vec)
    ff_in_w.pass_on(ff_in_near[3:], unit_one)
    active, slope = project_hidden(middle_low, ff_in_w, ff_in_b)
    ff_out_beside, ff_out_across = after_all((ff_out_beside, ff_out_across), active)
    half = ff_out_weight.shape[0] // 2
    ff_out_corners = swap_col(ff_out_across[:half]), swap_row(ff_out_beside[half:])
    ff_out_w = Shards(D, ff_out_weight, ff_out_beside, ff_out_across, *ff_out_corners)
    out_mine, out_leave, back_two, d_two, sums_two = second_norm(active, ff_out_w, unit_one, incoming, vec)

    ff_out = GridSum(*grad_down(active, d_two))
    d_hidden, ff_in_bias_part = hidden_back(after(d_two, ff_out.kernel), ff_out_w, slope)
    out_other = after(swap_col(out_leave), d_hidden)
    ff_out.send(d_hidden, out_other)
    ff_in = GridSum(*grad_up(after(middle_low, *ff_out.sent), d_hidden))
    back_one, d_one, sums_one = first_back(
        after(d_hidden, ff_in.kernel), ff_in_w, back_two, unit_one, inverse_one, vec
    )
    d_heads = heads_back(d_one, out_w)
    d_shared = spread_heads(d_heads[SEQ:], member, row)
    ff_out.send_last(d_heads)
    d_qkv_shared = attend_back(qkv_shared, probs_shared, after(d_shared, *ff_out.last))
    pieces = send_heads(d_qkv_shared)
    ff_in.send(d_qkv_shared)
    d_qkv_own = attend_back(qkv, probs_own, after(d_heads, *ff_in.sent))
    ff_out_pairs = PairSum(ff_out.result(d_qkv_own), n_dp)
    event = ff_out_pairs.step(d_qkv_own)
    pieces = after_all(pieces, d_qkv_own, event)
    d_qkv = jnp.concatenate([d_qkv_own, join_heads(pieces, member, row)], 0)
    qkv_sum = GridSum(*grad_up(x, d_qkv))
    event = ff_out_pairs.step(qkv_sum.kernel)
    ff_in.send_last(event)
    out_sum = GridSum(*grad_down(heads, after(d_one, *ff_in.last)))
    event = ff_out_pairs.step(out_sum.kernel)
    ff_in_pairs = PairSum(ff_in.result(event), n_dp)
    event = ff_in_pairs.step(event)
    qkv_sum.send(event)
    in_mine, in_leave, column_sums = input_back(after(d_qkv, *qkv_sum.sent), qkv_w, back_one)
    def ordered(value):
        blocks = value.reshape(4, -1)
        return jnp.stack([lax.dynamic_index_in_dim(blocks, row ^ place, 0, False) for place in range(4)])

    place = row * 2 + col

    def own_part(value):
        halves = lax.dynamic_slice_in_dim(value[: 6 * D].reshape(6, 2, D // 2), col, 1, 1)[:, 0]
        ff_in_part = lax.dynamic_slice_in_dim(value, 6 * D + place * 512, 512)
        qv_part = lax.dynamic_slice_in_dim(value, 10 * D + place * 256, 256)
        return jnp.concatenate([halves.reshape(-1), ff_in_part, qv_part])

    halves = jnp.concatenate([sums_one, sums_two], 0)
    halves = jnp.concatenate(in_order(halves[:, : D // 2], halves[:, D // 2 :]), 1)
    column_sums = ordered(column_sums).reshape(-1, 3, HD)
    qv_sums = jnp.concatenate([column_sums[:, 0], column_sums[:, 2]], 1)
    sums = jnp.concatenate([halves.reshape(-1), ordered(ff_in_bias_part).reshape(-1), qv_sums.reshape(-1)])
    sums = VectorSum(sums, own_part, n_dp)
    event = ff_out_pairs.step(in_leave)
    event = ff_in_pairs.step(event)
    qkv_sum.send_last(event)
    event = sums.step(qkv_sum.last[0])
    out_sum.send(event)
    event = ff_in_pairs.step(out_sum.sent[0])
    event = ff_out_pairs.step(event)
    event = sums.step(event)
    qkv_pairs = PairSum(qkv_sum.result(event), n_dp)
    event = qkv_pairs.step(event)
    out_sum.send_last(event)
    event = ff_in_pairs.step(out_sum.last[0])
    event = sums.step(event)
    event = qkv_pairs.step(event)
    out_pairs = PairSum(out_sum.result(event), n_dp)
    event = out_pairs.step(event)
    event = sums.step(event)
    in_other = swap_col(after(in_leave, event))
    every = [ff_out_pairs, qkv_pairs, ff_in_pairs, out_pairs, sums]
    while any(pairs.plan for pairs in every):
        for pairs in every:
            event = pairs.step(event)
    input_grad = give_back(in_mine, after(in_other, event), odd, col)
    layer_out = give_back(out_mine, after(out_other, event), odd, col)
    for pairs in every:
        pairs.take(event)
    ff_out_grad, qkv_grad, ff_in_grad, out_w_grad, early = [pairs.result() for pairs in every]
    halves = early[: 6 * 512].reshape(6, 512)
    return (
        layer_out,
        input_grad,
        qkv_grad.astype(F32),
        early[7 * 512 :].reshape(2, 2 * HD),
        out_w_grad.astype(F32),
        halves[0],
        halves[1],
        halves[2],
        ff_in_grad.astype(F32),
        early[6 * 512 : 7 * 512],
        ff_out_grad.astype(F32),
        halves[3],
        halves[4],
        halves[5],
    )


def solution(mesh):
    in_specs = (
        P(("dp", "row"), "col"),
        P("dp"),
        P("col", "row"),
        P(("row", "col"), None),
        P("row", "col"),
        P("col"),
        P("col"),
        P("col"),
        P("col", "row"),
        P(("row", "col")),
        P("row", "col"),
        P("col"),
        P("col"),
        P("col"),
        P(("dp", "row"), "col"),
    )
    out_specs = (
        P(("dp", "row"), "col"),
        P(("dp", "row"), "col"),
        P("col", "row"),
        P(("row", "col"), None),
        P("row", "col"),
        P("col"),
        P("col"),
        P("col"),
        P("col", "row"),
        P(("row", "col")),
        P("row", "col"),
        P("col"),
        P("col"),
        P("col"),
    )
    step = functools.partial(local, mesh.shape["dp"])
    return jax.shard_map(step, mesh=mesh, in_specs=in_specs, out_specs=out_specs, check_vma=False)
```

```python
import functools
import math

import jax
import jax.numpy as jnp
from jax import lax
from jax.experimental import pallas as pl
from jax.experimental.pallas import tpu as pltpu
from jax.sharding import PartitionSpec as P

D = 1024
HD = 64
SEQ = 512
QUARTER = SEQ // 4
GRID = ("row", "col")

EPSILON = 1e-06
NEGATIVE = -1e30
F32 = jnp.float32
BF16 = jnp.bfloat16
NN = (((1,), (0,)), ((), ()))
NT = (((1,), (1,)), ((), ()))
TN = (((0,), (0,)), ((), ()))
MIB = 1 << 20


LIGHT = ("project_hidden", "first_back", "heads_back")


def cost_of(name):
    scale = 1e-6 if name in LIGHT else 1
    return pl.CostEstimate(flops=int(1e13 * scale), bytes_accessed=int(1e9 * scale), transcendentals=0)


def mm(left, right, contract):
    return lax.dot_general(left, right, contract, preferred_element_type=F32)


def attend_kernel(qkv_ref, column_ref, line_ref, heads_ref, probs_ref, mask):
    @pl.when(pl.program_id(0) == 0)
    def _():
        mask[...] = jnp.where(column_ref[...] == line_ref[...], 0.0, NEGATIVE)

    mixed = []
    for head in range(2):
        base = head * 3 * HD
        query = qkv_ref[:, base : base + HD] * jnp.asarray(1 / math.sqrt(HD), BF16)
        key = qkv_ref[:, base + HD : base + 2 * HD]
        value = qkv_ref[:, base + 2 * HD : base + 3 * HD]
        scores = mm(key, query, NT) + mask[...]
        powers = jnp.exp(scores - jnp.max(scores, 0, keepdims=True))
        total = jnp.sum(powers, 0, keepdims=True)
        probs = (powers * (1.0 / total)).astype(BF16)
        probs_ref[head] = probs
        mixed.append(mm(value, probs, TN))
    heads_ref[...] = jnp.concatenate(mixed, 0).T.astype(BF16)


def attend(qkv, labels):
    pairs = qkv.shape[1] // (6 * HD)
    return pl.pallas_call(
        attend_kernel,
        grid=(pairs,),
        in_specs=[
            pl.BlockSpec((SEQ, 6 * HD), lambda i: (0, i)),
            pl.BlockSpec((SEQ, 1), lambda i: (0, 0)),
            pl.BlockSpec((1, SEQ), lambda i: (0, 0)),
        ],
        out_specs=[
            pl.BlockSpec((SEQ, 2 * HD), lambda i: (0, i)),
            pl.BlockSpec((2, SEQ, SEQ), lambda i: (i, 0, 0)),
        ],
        out_shape=[
            jax.ShapeDtypeStruct((SEQ, pairs * 2 * HD), BF16),
            jax.ShapeDtypeStruct((pairs * 2, SEQ, SEQ), BF16),
        ],
        scratch_shapes=[pltpu.VMEM((SEQ, SEQ), F32)],
        compiler_params=pltpu.CompilerParams(vmem_limit_bytes=(56 if pairs > 2 else 32) * MIB),
        cost_estimate=cost_of("attend"),
        name="attend",
    )(qkv, labels[:, None], labels[None, :])


def attend_back_kernel(qkv_ref, probs_ref, grad_ref, out_ref):
    for head in range(2):
        base = head * 3 * HD
        scale = jnp.asarray(1 / math.sqrt(HD), BF16)
        query = qkv_ref[:, base : base + HD] * scale
        key = qkv_ref[:, base + HD : base + 2 * HD] * scale
        value = qkv_ref[:, base + 2 * HD : base + 3 * HD]
        grad = grad_ref[:, head * HD : (head + 1) * HD]
        probs = probs_ref[head]
        d_value = mm(probs, grad, NN)
        d_probs = mm(value, grad, NT)
        wide = probs.astype(F32)
        delta = jnp.sum(wide * d_probs, 0, keepdims=True)
        d_scores = (wide * (d_probs - delta)).astype(BF16)
        d_key = mm(d_scores, query, NN)
        d_query = mm(key, d_scores, TN).T
        out_ref[:, base : base + HD] = d_query.astype(BF16)
        out_ref[:, base + HD : base + 2 * HD] = d_key.astype(BF16)
        out_ref[:, base + 2 * HD : base + 3 * HD] = d_value.astype(BF16)


def attend_back(qkv, probs, grad):
    pairs = qkv.shape[1] // (6 * HD)
    return pl.pallas_call(
        attend_back_kernel,
        grid=(pairs,),
        in_specs=[
            pl.BlockSpec((SEQ, 6 * HD), lambda i: (0, i)),
            pl.BlockSpec((2, SEQ, SEQ), lambda i: (i, 0, 0)),
            pl.BlockSpec((SEQ, 2 * HD), lambda i: (0, i)),
        ],
        out_specs=pl.BlockSpec((SEQ, 6 * HD), lambda i: (0, i)),
        out_shape=jax.ShapeDtypeStruct((SEQ, qkv.shape[1]), BF16),
        compiler_params=pltpu.CompilerParams(vmem_limit_bytes=(56 if pairs > 2 else 32) * MIB),
        cost_estimate=cost_of("attend_back"),
        name="attend_back",
    )(qkv, probs, grad)


def swap_core(value):
    return lax.ppermute(value, "row", [(i, i ^ 1) for i in range(4)])


def swap_row(value):
    return lax.ppermute(value, "row", [(i, i ^ 2) for i in range(4)])


def swap_col(value):
    return lax.ppermute(value, "col", [(0, 1), (1, 0)])


def after(value, *others):
    return lax.optimization_barrier((value, *others))[0]


def after_all(values, *others):
    return lax.optimization_barrier((*values, *others))[: len(values)]


def add(*values):
    total = values[0].astype(F32)
    for value in values[1:]:
        total = total + value.astype(F32)
    return total.astype(BF16)


def own_rows(value, odd, col):
    rolled = jnp.where(odd, jnp.roll(value, -2 * QUARTER, 0), value)
    first = jnp.concatenate([rolled[:SEQ], rolled[2 * SEQ : 2 * SEQ + QUARTER]], 0)
    second = jnp.concatenate([rolled[SEQ : 2 * SEQ], rolled[2 * SEQ + QUARTER :]], 0)
    mine = jnp.where(col == 0, first, second)
    return jnp.concatenate([mine, swap_col(jnp.where(col == 0, second, first))], 1)


def give_back(mine, other, odd, col):
    other = other.astype(F32)
    first = jnp.where(col == 0, mine, other)
    second = jnp.where(col == 0, other, mine)
    rolled = jnp.concatenate([first[:SEQ], second[:SEQ], first[SEQ:], second[SEQ:]], 0)
    return jnp.where(odd, jnp.roll(rolled, 2 * QUARTER, 0), rolled)


def swap(offset):
    return [(i, i ^ offset) for i in range(8)]


def spread_heads(value, member, row):
    width = value.shape[1] // 4
    pieces = []
    for offset in range(4):
        piece = lax.dynamic_slice_in_dim(value, ((member ^ offset) ^ row) * width, width, 1)
        pieces.append(piece if offset == 0 else lax.ppermute(piece, GRID, swap(offset)))
    return jnp.concatenate(pieces, 0)


def send_heads(value):
    pieces = [value[offset * QUARTER : (offset + 1) * QUARTER] for offset in range(4)]
    return [piece if offset == 0 else lax.ppermute(piece, GRID, swap(offset)) for offset, piece in enumerate(pieces)]


def join_heads(pieces, member, row):
    width = pieces[0].shape[1]
    whole = jnp.zeros((QUARTER, 4 * width), pieces[0].dtype)
    for offset, piece in enumerate(pieces):
        whole = lax.dynamic_update_slice_in_dim(whole, piece, ((member ^ offset) ^ row) * width, 1)
    return whole


class Shards:
    def __init__(self, depth, shard, beside, across, *corners, near_only=False):
        self.depth, self.width = depth, shard.shape[1]
        near = [(0, 0, shard), (1, 0, beside), (4, 0, across)]
        near += [(5, index * depth // 2, corner) for index, corner in enumerate(corners)]
        self.parts = near
        if not near_only:
            self.pass_on(near)

    def pass_on(self, near, *ties):
        far = [(place + 2, start, swap_core(after(part, *ties) if ties else part)) for place, start, part in near]
        self.parts = self.parts + far


def dense(kernel, in_specs, out_specs, out_shape, scratch, flops, name, shards=None):
    if shards is None:
        body, extra_specs, extra_scratch = kernel, [], []
    else:
        places = [(place, start, min(part.shape[0], shards.depth - start)) for place, start, part in shards.parts]
        count = len(places)
        extra_specs = [pl.BlockSpec(memory_space=pl.ANY)] * count
        extra_scratch = [
            pltpu.VMEM((8, shards.depth, shards.width), BF16),
            pltpu.SemaphoreType.DMA((count,)),
        ]

        def body(*refs):
            step = pl.program_id(0)
            held, done = refs[-2:]
            copies = [
                pltpu.make_async_copy(
                    refs[k].at[pl.ds(0, rows)], held.at[place, pl.ds(start, rows)], done.at[k]
                )
                for k, (place, start, rows) in enumerate(places)
            ]
            for block in range(4):

                @pl.when(step == 0)
                def _():
                    for copy, (place, _, _) in zip(copies, places):
                        if place // 2 == block:
                            copy.start()

            for block in range(4):

                @pl.when(step == block)
                def _():
                    for copy, (place, _, _) in zip(copies, places):
                        if place // 2 == block:
                            copy.wait()

            kernel(held.at[pl.ds(2 * step, 2)], *refs[count:-2])

    return pl.pallas_call(
        body,
        grid=(4,),
        in_specs=extra_specs + in_specs,
        out_specs=out_specs,
        out_shape=out_shape,
        scratch_shapes=scratch + extra_scratch,
        compiler_params=pltpu.CompilerParams(vmem_limit_bytes=48 * MIB),
        cost_estimate=cost_of(name),
        name=name,
    )


def whole(value):
    return pl.BlockSpec(value.shape, lambda i: (0,) * value.ndim)


def columns_of(value, parts=4):
    return pl.BlockSpec((value.shape[0], value.shape[1] // parts), lambda i: (0, i))


def shaped(shape, kind):
    return jax.ShapeDtypeStruct(shape, kind)


def halves_times(left_ref, weight_ref, start, width):
    half = left_ref.shape[1] // 2
    stop = start + width
    return mm(left_ref[:, :half], weight_ref[0, :, start:stop], NN) + mm(
        left_ref[:, half:], weight_ref[1, :, start:stop], NN
    )


def qkv_kernel(weight_ref, x_ref, bias_ref, out_ref):
    for start in range(0, out_ref.shape[1], 256):
        part = halves_times(x_ref, weight_ref, start, 256)
        out_ref[:, start : start + 256] = (part + bias_ref[:, start : start + 256]).astype(BF16)


def project_qkv(x, shards, bias):
    width = 4 * shards.width
    return dense(
        qkv_kernel,
        [whole(x), columns_of(bias)],
        pl.BlockSpec((x.shape[0], width // 4), lambda i: (0, i)),
        shaped((x.shape[0], width), BF16),
        [],
        2 * x.shape[0] * D * width,
        "project_qkv",
        shards,
    )(*[part for _, _, part in shards.parts], x, bias)


def hidden_kernel(weight_ref, x_ref, bias_ref, active_ref, slope_ref):
    for start in range(0, active_ref.shape[1], 256):
        stop = start + 256
        hidden = halves_times(x_ref, weight_ref, start, 256) + bias_ref[:, start:stop]
        share = 0.5 * (1.0 + lax.erf(hidden * math.sqrt(0.5)))
        bell = jnp.exp(hidden * hidden * -0.5) * (1 / math.sqrt(2 * math.pi))
        active_ref[:, start:stop] = (hidden * share).astype(BF16)
        slope_ref[:, start:stop] = (share + hidden * bell).astype(BF16)


def project_hidden(x, shards, bias):
    width = 4 * shards.width
    block = pl.BlockSpec((x.shape[0], width // 4), lambda i: (0, i))
    return dense(
        hidden_kernel,
        [whole(x), columns_of(bias)],
        [block, block],
        [shaped((x.shape[0], width), BF16)] * 2,
        [],
        4 * x.shape[0] * D * width,
        "project_hidden",
        shards,
    )(*[part for _, _, part in shards.parts], x, bias)


def add_product(left_ref, weight_ref, total, contract):
    step = pl.program_id(0)
    half = D // 2
    for col in range(2):
        part = mm(left_ref[...], weight_ref[col], contract)
        span = slice(col * half, (col + 1) * half)

        @pl.when(step == 0)
        def _():
            total[:, span] = part

        @pl.when(step > 0)
        def _():
            total[:, span] += part


ROWS = 16


def each_rows(count, body):
    @pl.loop(0, count // (4 * ROWS))
    def _(step):
        for part in range(4):
            body(pl.ds(pl.multiple_of((4 * step + part) * ROWS, ROWS), ROWS))


def add_rows(partial, place, value):
    partial[place] += value[:8] + value[8:]


def norm_parts(value):
    center = jnp.sum(value, 1, keepdims=True) * (1 / D)
    squares = jnp.sum(value * value, 1, keepdims=True) * (1 / D)
    inverse = lax.rsqrt(squares - center * center + EPSILON)
    return ((value - center) * inverse, inverse)


def norm_back(grad, unit, inverse, gain):
    scaled = grad * gain
    mean = jnp.sum(scaled, 1, keepdims=True) * (1 / D)
    paired = jnp.sum(scaled * unit, 1, keepdims=True) * (1 / D)
    return inverse * (scaled - mean - unit * paired)


def total_of(value):
    return jnp.sum(value, 0, keepdims=True)


def first_norm_kernel(weight_ref, heads_ref, x_ref, vec_ref, unit_ref, inverse_ref, low_ref, total):
    add_product(heads_ref, weight_ref, total, NN)

    @pl.when(pl.program_id(0) == 3)
    def _():
        def body(rows):
            value = x_ref[rows, :].astype(F32) + (total[rows, :] + vec_ref[0:1, :])
            unit, inverse = norm_parts(value)
            unit_ref[rows, :] = unit
            inverse_ref[rows, :] = inverse
            low_ref[rows, :] = (unit * vec_ref[1:2, :] + vec_ref[2:3, :]).astype(BF16)

        each_rows(x_ref.shape[0], body)


def first_norm(heads, shards, x, vec):
    rows = x.shape[0]
    outs = [shaped((rows, D), F32), shaped((rows, 1), F32), shaped((rows, D), BF16)]
    return dense(
        first_norm_kernel,
        [columns_of(heads), whole(x), whole(vec)],
        [whole(out) for out in outs],
        outs,
        [pltpu.VMEM((rows, D), F32)],
        2 * rows * D * D,
        "first_norm",
        shards,
    )(*[part for _, _, part in shards.parts], heads, x, vec)


def second_norm_kernel(
    weight_ref, active_ref, unit_ref, incoming_ref, vec_ref, out_ref, leave_ref, back_ref, low_ref, sums_ref, total, partial
):
    add_product(active_ref, weight_ref, total, NN)

    @pl.when(pl.program_id(0) == 3)
    def _():
        partial[...] = jnp.zeros_like(partial)
        half = D // 2

        def body(rows):
            middle = unit_ref[rows, :] * vec_ref[1:2, :] + vec_ref[2:3, :]
            unit, inverse = norm_parts(middle + (total[rows, :] + vec_ref[3:4, :]))
            out = unit * vec_ref[4:5, :] + vec_ref[5:6, :]
            out_ref[rows, :] = out[:, :half]
            leave_ref[rows, :] = out[:, half:].astype(BF16)
            grad = incoming_ref[rows, :].astype(F32)
            add_rows(partial, 1, grad * unit)
            add_rows(partial, 2, grad)
            back = norm_back(grad, unit, inverse, vec_ref[4:5, :])
            low = back.astype(BF16)
            back_ref[rows, :] = back
            low_ref[rows, :] = low
            add_rows(partial, 0, low.astype(F32))

        each_rows(unit_ref.shape[0], body)
        for place in range(3):
            sums_ref[place : place + 1, :] = total_of(partial[place])


def second_norm(active, shards, unit, incoming, vec):
    rows = unit.shape[0]
    outs = [
        shaped((rows, D // 2), F32),
        shaped((rows, D // 2), BF16),
        shaped((rows, D), F32),
        shaped((rows, D), BF16),
        shaped((3, D), F32),
    ]
    return dense(
        second_norm_kernel,
        [columns_of(active), whole(unit), whole(incoming), whole(vec)],
        [whole(out) for out in outs],
        outs,
        [pltpu.VMEM((rows, D), F32), pltpu.VMEM((3, 8, D), F32)],
        2 * rows * D * active.shape[1],
        "second_norm",
        shards,
    )(*[part for _, _, part in shards.parts], active, unit, incoming, vec)


def first_back_kernel(
    weight_ref, d_hidden_ref, back_ref, unit_ref, inverse_ref, vec_ref, out_ref, low_ref, sums_ref, total, partial
):
    add_product(d_hidden_ref, weight_ref, total, NT)

    @pl.when(pl.program_id(0) == 3)
    def _():
        partial[...] = jnp.zeros_like(partial)

        def body(rows):
            grad = back_ref[rows, :] + total[rows, :]
            unit = unit_ref[rows, :]
            add_rows(partial, 1, grad * unit)
            add_rows(partial, 2, grad)
            back = norm_back(grad, unit, inverse_ref[rows, :], vec_ref[1:2, :])
            low = back.astype(BF16)
            out_ref[rows, :] = back
            low_ref[rows, :] = low
            add_rows(partial, 0, low.astype(F32))

        each_rows(unit_ref.shape[0], body)
        for place in range(3):
            sums_ref[place : place + 1, :] = total_of(partial[place])


def first_back(d_hidden, shards, back, unit, inverse, vec):
    rows = unit.shape[0]
    outs = [shaped((rows, D), F32), shaped((rows, D), BF16), shaped((3, D), F32)]
    return dense(
        first_back_kernel,
        [columns_of(d_hidden), whole(back), whole(unit), whole(inverse), whole(vec)],
        [whole(out) for out in outs],
        outs,
        [pltpu.VMEM((rows, D), F32), pltpu.VMEM((3, 8, D), F32)],
        2 * rows * D * d_hidden.shape[1],
        "first_back",
        shards,
    )(*[part for _, _, part in shards.parts], d_hidden, back, unit, inverse, vec)


def input_back_kernel(weight_ref, d_qkv_ref, back_ref, out_ref, leave_ref, sums_ref, total):
    add_product(d_qkv_ref, weight_ref, total, NT)
    sums_ref[...] = total_of(d_qkv_ref[...].astype(F32))

    @pl.when(pl.program_id(0) == 3)
    def _():
        half = D // 2
        out_ref[...] = back_ref[:, :half] + total[:, :half]
        leave_ref[...] = (back_ref[:, half:] + total[:, half:]).astype(BF16)


def input_back(d_qkv, shards, back):
    rows, width = d_qkv.shape
    outs = [shaped((rows, D // 2), F32), shaped((rows, D // 2), BF16), shaped((1, width), F32)]
    return dense(
        input_back_kernel,
        [columns_of(d_qkv), whole(back)],
        [whole(outs[0]), whole(outs[1]), columns_of(outs[2])],
        outs,
        [pltpu.VMEM((rows, D), F32)],
        2 * rows * D * width,
        "input_back",
        shards,
    )(*[part for _, _, part in shards.parts], d_qkv, back)


def columns_back(grad_ref, weight_ref, start, stop):
    half = D // 2
    return mm(grad_ref[:, :half], weight_ref[0, start:stop, :], NT) + mm(
        grad_ref[:, half:], weight_ref[1, start:stop, :], NT
    )


def hidden_back_kernel(weight_ref, grad_ref, slope_ref, out_ref, sums_ref):
    for start in range(0, out_ref.shape[1], 256):
        span = slice(start, start + 256)
        part = columns_back(grad_ref, weight_ref, start, start + 256)
        low = (part * slope_ref[:, span].astype(F32)).astype(BF16)
        out_ref[:, span] = low
        sums_ref[:, span] = total_of(low.astype(F32))


def hidden_back(grad, shards, slope):
    outs = [shaped(slope.shape, BF16), shaped((1, slope.shape[1]), F32)]
    return dense(
        hidden_back_kernel,
        [whole(grad), columns_of(slope)],
        [columns_of(out) for out in outs],
        outs,
        [],
        2 * grad.shape[0] * D * slope.shape[1],
        "hidden_back",
        shards,
    )(*[part for _, _, part in shards.parts], grad, slope)


def heads_back_kernel(weight_ref, grad_ref, out_ref):
    out_ref[...] = columns_back(grad_ref, weight_ref, 0, weight_ref.shape[1]).astype(BF16)


def heads_back(grad, shards):
    return dense(
        heads_back_kernel,
        [whole(grad)],
        columns_of(grad),
        shaped(grad.shape, BF16),
        [],
        2 * grad.shape[0] * D * D,
        "heads_back",
        shards,
    )(*[part for _, _, part in shards.parts], grad)


def grad_up_kernel(left_ref, right_ref, keep_ref, leave_ref, turned):
    step = pl.program_id(0)
    half = D // 2

    @pl.when(step == 0)
    def _():
        turned[...] = left_ref[...].T

    for parity, out_ref in enumerate((keep_ref, leave_ref)):

        @pl.when(step % 2 == parity)
        def _():
            for col in range(2):
                out_ref[col] = mm(turned[col * half : (col + 1) * half, :], right_ref[...], NN).astype(BF16)


def two_blocks(out):
    return pl.BlockSpec((2, *out.shape[1:]), lambda i: (i // 2, 0, 0))


def grad_up(left, right):
    out = shaped((4, D // 2, right.shape[1] // 4), BF16)
    return dense(
        grad_up_kernel,
        [whole(left), columns_of(right)],
        [two_blocks(out)] * 2,
        [out] * 2,
        [pltpu.VMEM((D, left.shape[0]), BF16)],
        2 * left.shape[0] * D * right.shape[1],
        "grad_up",
    )(left, right)


def grad_down_kernel(left_ref, right_ref, keep_ref, leave_ref):
    step = pl.program_id(0)
    half = D // 2
    for parity, out_ref in enumerate((keep_ref, leave_ref)):

        @pl.when(step % 2 == parity)
        def _():
            turned = left_ref[...].T
            for col in range(2):
                out_ref[col] = mm(turned, right_ref[:, col * half : (col + 1) * half], NN).astype(BF16)


def grad_down(left, right):
    out = shaped((4, left.shape[1] // 4, D // 2), BF16)
    return dense(
        grad_down_kernel,
        [columns_of(left), whole(right)],
        [two_blocks(out)] * 2,
        [out] * 2,
        [],
        2 * left.shape[0] * D * left.shape[1],
        "grad_down",
    )(left, right)


class PairSum:
    def __init__(self, value, size):
        self.whole = None
        if size & (size - 1):
            self.whole = lax.psum(value, "dp")
        self.value, self.other = value, None
        place = lax.axis_index("dp")
        levels = [1 << k for k in range(size.bit_length() - 1)]
        pairs = [([(i, i ^ step) for i in range(size)], (place // step) % 2 == 1) for step in levels]
        self.plan = [(True, *pair) for pair in pairs] + [(False, *pair) for pair in reversed(pairs)]
        self.upper = self.down = None
        if self.whole is not None:
            self.plan = []

    def step(self, last):
        self.take(last)
        if not self.plan:
            return self.value
        self.down, pairs, self.upper = self.plan.pop(0)
        if self.down:
            half = self.value.shape[0] // 2
            top, bottom = self.value[:half], self.value[half:]
            self.value = jnp.where(self.upper, bottom, top)
            leaving = jnp.where(self.upper, top, bottom)
        else:
            leaving = self.value
        leaving = after(leaving, last)
        self.other = lax.ppermute(leaving, "dp", pairs)
        return leaving

    def take(self, last):
        if self.other is None:
            return
        other = after(self.other, last)
        if self.down:
            self.value = add(self.value, other)
        else:
            parts = jnp.where(self.upper, other, self.value), jnp.where(self.upper, self.value, other)
            self.value = jnp.concatenate(parts, 0)
        self.other = None

    def result(self):
        return self.value if self.whole is None else self.whole


class GridSum:
    def __init__(self, keep, leaving):
        self.keep, self.other = keep, swap_core(leaving)
        self.half = keep.shape[1] // 2
        self.kernel = leaving

    def upper(self, place, *more):
        return add(self.keep[place, : self.half], self.other[place, : self.half], *more)

    def lower(self, place, *more):
        return add(self.keep[place, self.half :], self.other[place, self.half :], *more)

    def send(self, *ties):
        if ties:
            self.other = after(self.other, *ties)
        col = jnp.concatenate([self.upper(3), self.upper(1)], 0)
        row = jnp.concatenate([self.lower(3), self.lower(2)], 0)
        self.sent = lax.optimization_barrier((col, row))
        self.from_col, self.from_row = swap_col(self.sent[0]), swap_row(self.sent[1])
        return self.sent

    def send_last(self, *ties):
        if ties:
            self.from_row, self.from_col = lax.optimization_barrier((self.from_row, self.from_col, *ties))[:2]
        col = self.lower(1, self.from_row[: self.half])
        row = self.upper(2, self.from_col[: self.half])
        self.last = lax.optimization_barrier((col, row))
        self.last_col, self.last_row = swap_col(self.last[0]), swap_row(self.last[1])
        return self.last

    def result(self, *ties):
        from_col, last_row = self.from_col, self.last_row
        if ties:
            from_col, last_row = lax.optimization_barrier((from_col, last_row, *ties))[:2]
        upper = self.upper(0, from_col[self.half :], last_row)
        return jnp.concatenate([upper, self.lower(0, self.from_row[self.half :], self.last_col)], 0)


class VectorSum:
    def __init__(self, value, then, size):
        self.value, self.then, self.other = value, then, None
        self.size = size
        levels = [1 << k for k in range(size.bit_length() - 1)] if size & (size - 1) == 0 else []
        self.plan = [swap_core, swap_row, swap_col, None]
        self.plan += [functools.partial(lax.ppermute, axis_name="dp", perm=[(i, i ^ k) for i in range(size)]) for k in levels]

    def step(self, last):
        self.take(last)
        if not self.plan:
            return last
        move = self.plan.pop(0)
        if move is None:
            self.value = self.then(self.value)
            if not self.plan:
                return last
            move = self.plan.pop(0)
        leaving = after(self.value, last)
        self.other = move(leaving)
        return leaving

    def take(self, last):
        if self.other is not None:
            self.value = self.value + after(self.other, last)
            self.other = None

    def result(self):
        return lax.psum(self.value, "dp") if self.size & (self.size - 1) else self.value


def local(
    n_dp,
    tokens,
    segments,
    qkv_weight,
    qv_bias,
    out_weight,
    out_bias,
    ln1_gain,
    ln1_bias,
    ff_in_weight,
    ff_in_bias,
    ff_out_weight,
    ff_out_bias,
    ln2_gain,
    ln2_bias,
    out_grad,
):
    row, col = lax.axis_index("row"), lax.axis_index("col")
    odd = row % 2 == 1
    member = (row % 2) * 2 + col

    def in_order(mine, other):
        return jnp.where(col == 0, mine, other), jnp.where(col == 0, other, mine)

    packed = jnp.concatenate(
        [out_bias, ln1_gain, ln1_bias, ff_out_bias, ln2_gain, ln2_bias, ff_in_bias, qv_bias.reshape(-1)]
    )
    beside, across = swap_col(packed), swap_row(packed)
    near = [packed, beside, across, swap_row(beside)]
    far = [swap_core(value) for value in near]
    packed = jnp.stack([near[0], near[1], far[0], far[1], near[2], near[3], far[2], far[3]])
    qkv_beside, qkv_across = swap_col(qkv_weight), swap_row(qkv_weight)
    x = own_rows(after(tokens, qkv_beside, qkv_across), odd, col)
    qkv_corner = swap_row(qkv_beside)
    qkv_w = Shards(D // 2, qkv_weight, qkv_beside, qkv_across, qkv_corner)
    out_beside = swap_col(after(out_weight, x))
    out_across = swap_row(after(out_weight, qkv_corner))
    incoming = own_rows(after(out_grad, x), odd, col)
    ff_in_across = swap_row(after(ff_in_weight, out_across))

    vec = packed[:2, : 6 * 512].reshape(2, 6, 512).transpose(1, 0, 2).reshape(6, D)
    pairs = packed[:, 6 * 512 :].reshape(4, 2, 768)
    first, second = in_order(pairs[:, 0], pairs[:, 1])
    ff_in_b = jnp.concatenate([first[:, :512], second[:, :512]], 1).reshape(1, -1)
    qv_b = jnp.concatenate([first[:, 512:], second[:, 512:]], 1).reshape(-1, 2 * HD)
    hollow = jnp.zeros((qv_b.shape[0], HD), F32)
    qkv_b = jnp.concatenate([qv_b[:, :HD], hollow, qv_b[:, HD:]], 1).reshape(1, -1)

    group = (row // 2) * 5
    labels = lax.dynamic_slice_in_dim(segments, (group + (row % 2) * 3 + col) * SEQ, SEQ)
    shared = lax.dynamic_slice_in_dim(segments, (group + 2) * SEQ, SEQ)
    shared = jnp.concatenate(
        [lax.dynamic_slice_in_dim(shared, (member ^ offset) * QUARTER, QUARTER) for offset in range(4)]
    )

    qkv = project_qkv(x, qkv_w, qkv_b)
    qkv_shared = spread_heads(qkv[SEQ:], member, row)
    heads_shared, probs_shared = attend(after(qkv_shared, incoming), shared)
    pieces = send_heads(heads_shared)
    ff_in_beside = swap_col(after(ff_in_weight, heads_shared))
    half = out_weight.shape[0] // 2
    out_corners = swap_col(out_across[:half]), swap_row(out_beside[half:])
    out_w = Shards(D // 4, out_weight, out_beside, out_across, *out_corners)
    heads_own, probs_own = attend(after(qkv, heads_shared, *[part for _, _, part in out_w.parts]), labels)
    pieces = after_all(pieces, heads_own)
    heads = jnp.concatenate([heads_own, join_heads(pieces, member, row)], 0)
    ff_in_beside, ff_in_across, ff_out_weight = after_all((ff_in_beside, ff_in_across, ff_out_weight), heads)
    half = ff_in_weight.shape[0] // 2
    ff_in_corners = swap_col(ff_in_across[:half]), swap_row(ff_in_beside[half:])
    ff_in_w = Shards(D // 2, ff_in_weight, ff_in_beside, ff_in_across, *ff_in_corners, near_only=True)
    ff_in_near = ff_in_w.parts
    ff_in_w.pass_on(ff_in_near[:3])
    ff_out_beside, ff_out_across = swap_col(ff_out_weight), swap_row(ff_out_weight)
    unit_one, inverse_one, middle_low = first_norm(after(heads, ff_in_beside, ff_in_across), out_w, x, vec)
    ff_in_w.pass_on(ff_in_near[3:], unit_one)
    active, slope = project_hidden(middle_low, ff_in_w, ff_in_b)
    ff_out_beside, ff_out_across = after_all((ff_out_beside, ff_out_across), active)
    half = ff_out_weight.shape[0] // 2
    ff_out_corners = swap_col(ff_out_across[:half]), swap_row(ff_out_beside[half:])
    ff_out_w = Shards(D, ff_out_weight, ff_out_beside, ff_out_across, *ff_out_corners)
    out_mine, out_leave, back_two, d_two, sums_two = second_norm(active, ff_out_w, unit_one, incoming, vec)

    ff_out = GridSum(*grad_down(active, d_two))
    d_hidden, ff_in_bias_part = hidden_back(after(d_two, ff_out.kernel), ff_out_w, slope)
    out_other = after(swap_col(out_leave), d_hidden)
    ff_out.send(d_hidden, out_other)
    ff_in = GridSum(*grad_up(after(middle_low, *ff_out.sent), d_hidden))
    back_one, d_one, sums_one = first_back(
        after(d_hidden, ff_in.kernel), ff_in_w, back_two, unit_one, inverse_one, vec
    )
    d_heads = heads_back(d_one, out_w)
    d_shared = spread_heads(d_heads[SEQ:], member, row)
    ff_out.send_last(d_heads)
    d_qkv_shared = attend_back(qkv_shared, probs_shared, after(d_shared, *ff_out.last))
    pieces = send_heads(d_qkv_shared)
    ff_in.send(d_qkv_shared)
    d_qkv_own = attend_back(qkv, probs_own, after(d_heads, *ff_in.sent))
    ff_out_pairs = PairSum(ff_out.result(d_qkv_own), n_dp)
    event = ff_out_pairs.step(d_qkv_own)
    pieces = after_all(pieces, d_qkv_own, event)
    d_qkv = jnp.concatenate([d_qkv_own, join_heads(pieces, member, row)], 0)
    qkv_sum = GridSum(*grad_up(x, d_qkv))
    event = ff_out_pairs.step(qkv_sum.kernel)
    ff_in.send_last(event)
    out_sum = GridSum(*grad_down(heads, after(d_one, *ff_in.last)))
    event = ff_out_pairs.step(out_sum.kernel)
    ff_in_pairs = PairSum(ff_in.result(event), n_dp)
    event = ff_in_pairs.step(event)
    qkv_sum.send(event)
    in_mine, in_leave, column_sums = input_back(after(d_qkv, *qkv_sum.sent), qkv_w, back_one)
    def ordered(value):
        blocks = value.reshape(4, -1)
        return jnp.stack([lax.dynamic_index_in_dim(blocks, row ^ place, 0, False) for place in range(4)])

    place = row * 2 + col

    def own_part(value):
        halves = lax.dynamic_slice_in_dim(value[: 6 * D].reshape(6, 2, D // 2), col, 1, 1)[:, 0]
        ff_in_part = lax.dynamic_slice_in_dim(value, 6 * D + place * 512, 512)
        qv_part = lax.dynamic_slice_in_dim(value, 10 * D + place * 256, 256)
        return jnp.concatenate([halves.reshape(-1), ff_in_part, qv_part])

    halves = jnp.concatenate([sums_one, sums_two], 0)
    halves = jnp.concatenate(in_order(halves[:, : D // 2], halves[:, D // 2 :]), 1)
    column_sums = ordered(column_sums).reshape(-1, 3, HD)
    qv_sums = jnp.concatenate([column_sums[:, 0], column_sums[:, 2]], 1)
    sums = jnp.concatenate([halves.reshape(-1), ordered(ff_in_bias_part).reshape(-1), qv_sums.reshape(-1)])
    sums = VectorSum(sums, own_part, n_dp)
    event = ff_out_pairs.step(in_leave)
    event = ff_in_pairs.step(event)
    qkv_sum.send_last(event)
    event = sums.step(qkv_sum.last[0])
    out_sum.send(event)
    event = ff_in_pairs.step(out_sum.sent[0])
    event = ff_out_pairs.step(event)
    event = sums.step(event)
    qkv_pairs = PairSum(qkv_sum.result(event), n_dp)
    event = qkv_pairs.step(event)
    out_sum.send_last(event)
    event = ff_in_pairs.step(out_sum.last[0])
    event = sums.step(event)
    event = qkv_pairs.step(event)
    out_pairs = PairSum(out_sum.result(event), n_dp)
    event = out_pairs.step(event)
    event = sums.step(event)
    in_other = swap_col(after(in_leave, event))
    every = [ff_out_pairs, qkv_pairs, ff_in_pairs, out_pairs, sums]
    while any(pairs.plan for pairs in every):
        for pairs in every:
            event = pairs.step(event)
    input_grad = give_back(in_mine, after(in_other, event), odd, col)
    layer_out = give_back(out_mine, after(out_other, event), odd, col)
    for pairs in every:
        pairs.take(event)
    ff_out_grad, qkv_grad, ff_in_grad, out_w_grad, early = [pairs.result() for pairs in every]
    halves = early[: 6 * 512].reshape(6, 512)
    return (
        layer_out,
        input_grad,
        qkv_grad.astype(F32),
        early[7 * 512 :].reshape(2, 2 * HD),
        out_w_grad.astype(F32),
        halves[0],
        halves[1],
        halves[2],
        ff_in_grad.astype(F32),
        early[6 * 512 : 7 * 512],
        ff_out_grad.astype(F32),
        halves[3],
        halves[4],
        halves[5],
    )


def solution(mesh):
    in_specs = (
        P(("dp", "row"), "col"),
        P("dp"),
        P("col", "row"),
        P(("row", "col"), None),
        P("row", "col"),
        P("col"),
        P("col"),
        P("col"),
        P("col", "row"),
        P(("row", "col")),
        P("row", "col"),
        P("col"),
        P("col"),
        P("col"),
        P(("dp", "row"), "col"),
    )
    out_specs = (
        P(("dp", "row"), "col"),
        P(("dp", "row"), "col"),
        P("col", "row"),
        P(("row", "col"), None),
        P("row", "col"),
        P("col"),
        P("col"),
        P("col"),
        P("col", "row"),
        P(("row", "col")),
        P("row", "col"),
        P("col"),
        P("col"),
        P("col"),
    )
    step = functools.partial(local, mesh.shape["dp"])
    return jax.shard_map(step, mesh=mesh, in_specs=in_specs, out_specs=out_specs, check_vma=False)
```
